32 devices in a mesh: dp: 16 (over z, x, core), mesh: 2 (over y).
Axes of the slice: x: 2, y: 2, z: 4, core: 2. Of those that a mesh axis runs over, the one named last changes fastest.
Arguments:
- node_feats: bfloat16 [16, 128, 512], P('dp', 'mesh'), may hold values from -6 to 6
- edge_feats: bfloat16 [16, 128, 8, 512], P('dp', 'mesh'), may hold values from -6 to 6
- node_cot: bfloat16 [16, 128, 512], P('dp', 'mesh'), may hold values from -6 to 6
- edge_cot: bfloat16 [16, 128, 8, 512], P('dp', 'mesh'), may hold values from -6 to 6
- w_edge_in: bfloat16 [2, 1536, 512], replicated, may hold values from -0.15625 to 0.15625
- w_edge_out: bfloat16 [2, 512, 512], replicated, may hold values from -0.25 to 0.25
- w_node_in: bfloat16 [2, 1024, 512], replicated, may hold values from -0.1875 to 0.1875
- w_node_out: bfloat16 [2, 512, 512], replicated, may hold values from -0.25 to 0.25
- neighbours: int32 [128, 8], P('mesh'), may hold values from 0 to 95
- send_rows: int32 [2, 32], P('mesh'), may hold values from 0 to 63, as said below
- edge_counts: int32 [128], P('mesh'), may hold values from 1 to 8
- ocean_mask: int32 [128], P('mesh'), may hold values 0 or 1
Outputs:
- grad_nodes: float32 [16, 128, 512], P('dp', 'mesh')
- grad_edges: bfloat16 [16, 128, 8, 512], P('dp', 'mesh')
- grad_edge_in: float32 [2, 1536, 512], P(None, 'dp')
- grad_edge_out: float32 [2, 512, 512], P(None, 'dp')
- grad_node_in: float32 [2, 1024, 512], P(None, 'dp')
- grad_node_out: float32 [2, 512, 512], P(None, 'dp')
The draws below stay inside these ranges and needn't reach their ends.
Inputs may be any that keep to these rules, and one draw needn't show every extreme that they name: `send_rows`: within each partition's row the (32) entries are distinct local rows.
All inputs are finite; a program needn't handle non-finite values. No bound on the sum of `ocean_mask` on one device may be relied on, other than what follows from the above.
Results may differ from the reference program's by a relative error of at most 0.03.
Values may be sent and summed in bfloat16 or wider, within the bound.
No kernel may reach another device: no remote copies, remote signals or barrier semaphores. Data moves between devices by JAX's collectives and lax.ppermute only.
A program may use at most 128 MiB of HBM per device.

```python
import jax
import jax.numpy as jnp
from jax import lax

D = 512
K = 8
LAYERS = 2
ND = 64
HALO = 16
SAMPLES = 16
NODES = 128
N_MESH = 2


def draw_send_rows(key, part):
    scores = jax.random.randint(key, (N_MESH, ND), 0, 1 << 20, dtype=jnp.int32) * ND
    scores = scores + jnp.arange(ND, dtype=jnp.int32)[None, :]
    ranking = jnp.argsort(scores, axis=1)
    return ranking[:, :2 * HALO].astype(jnp.int32)


def plant(drawn, key, least, high):
    extent = drawn.shape
    index_at = [jax.random.randint(jax.random.fold_in(key, axis), (), 0, extent[axis]) for axis in range(len(extent))]
    drawn = drawn.at[tuple(index_at)].set(least)
    longest = extent.index(max(extent))
    index_at[longest] = (index_at[longest] + 1) % extent[longest]
    return drawn.at[tuple(index_at)].set(high)


def spiked(drawn, stream_key, source, target, parts, factor):
    def block_of(position):
        return (jnp.arange(drawn.shape[position]) // (drawn.shape[position] // parts)).reshape((-1,) + (1,) * (drawn.ndim - 1 - position))

    one_side = jax.random.permutation(stream_key, parts)[block_of(target)]
    second = (block_of(target) + parts // 2) % parts
    return jnp.where((block_of(source) == one_side) | (block_of(source) == second), factor * drawn, drawn)


def block_levels(rng, extent, cuts, least, top_value):
    gain = 1.0
    for axis_at, shards_of in cuts:
        draws = jax.random.uniform(jax.random.fold_in(jax.random.fold_in(rng, 6), axis_at), (shards_of,), jnp.float32, least / len(cuts), top_value / len(cuts))
        gain = gain * jnp.repeat(jnp.exp(draws), extent[axis_at] // shards_of).reshape((-1,) + (1,) * (len(extent) - 1 - axis_at))
    return gain


def gaussian(key, dims, scale, reach, cuts=(), held_as=jnp.bfloat16):
    array = jax.random.normal(key, dims, jnp.float32) * scale
    if len(cuts) > 0:
        array = block_levels(key, dims, cuts, -0.22, 0.18) * array
    return jnp.clip(array, min=-reach, max=reach).astype(held_as)


def noise_with(stream_key, extent, width, reach, pieces, heavy, held_as=jnp.bfloat16):
    drawn = width * jax.random.normal(stream_key, extent, jnp.float32)
    if pieces:
        drawn = drawn * block_levels(stream_key, extent, pieces, -0.22, 0.18)
    return jnp.clip(spiked(drawn, jax.random.fold_in(stream_key, 3), *heavy), -reach, reach).astype(held_as)


def setup_inputs(seed: int = 0) -> dict:
    arg_keys = jax.random.split(jax.random.key(seed), 13)
    node_feats = noise_with(arg_keys[0], (SAMPLES, NODES, D), 1.0, 6.0, ((0, 16), (1, 2)), (0, 2, 16, 2.0))
    edge_feats = noise_with(arg_keys[1], (SAMPLES, NODES, K, D), 1.0, 6.0, ((0, 16), (1, 2)), (0, 3, 16, 2.0))
    node_cot = gaussian(arg_keys[2], (SAMPLES, NODES, D), 1.0, 6.0, ((0, 16), (1, 2)))
    edge_cot = gaussian(arg_keys[3], (SAMPLES, NODES, K, D), 1.0, 6.0, ((0, 16), (1, 2)))
    w_edge_in = gaussian(arg_keys[4], (LAYERS, 3 * D, D), (3 * D) ** -0.5, 0.15625)
    w_edge_out = gaussian(arg_keys[5], (LAYERS, D, D), D ** -0.5, 0.25)
    w_node_in = gaussian(arg_keys[6], (LAYERS, 2 * D, D), (2 * D) ** -0.5, 0.1875)
    w_node_out = gaussian(arg_keys[7], (LAYERS, D, D), D ** -0.5, 0.25)
    neighbours = plant(jax.random.randint(arg_keys[8], (NODES, K), 0, ND + 2 * HALO), jax.random.fold_in(arg_keys[8], 1), 0, (ND + 2 * HALO) - 1).astype(jnp.int32)
    send_rows = draw_send_rows(jax.random.fold_in(arg_keys[12], 71), 0)
    edge_counts = plant(jax.random.randint(arg_keys[10], (NODES,), 1, K + 1), jax.random.fold_in(arg_keys[10], 1), 1, K).astype(jnp.int32)
    ocean_mask = plant((jax.random.randint(arg_keys[11], (NODES,), 0, 4) < 3).astype(jnp.int32), jax.random.fold_in(arg_keys[11], 1), 0, 1)
    return dict(node_feats=node_feats, edge_feats=edge_feats, node_cot=node_cot, edge_cot=edge_cot, w_edge_in=w_edge_in, w_edge_out=w_edge_out, w_node_in=w_node_in, w_node_out=w_node_out, neighbours=neighbours, send_rows=send_rows, edge_counts=edge_counts, ocean_mask=ocean_mask)


def normalize(values):
    center = lax.optimization_barrier(jnp.mean(values, axis=-1, keepdims=True))
    shifted = values - center
    inverse = lax.rsqrt(lax.optimization_barrier(jnp.mean(shifted * shifted, axis=-1, keepdims=True)) + 1e-05)
    return shifted * inverse

def normalize_back(values, upstream):
    center = lax.optimization_barrier(jnp.mean(values, axis=-1, keepdims=True))
    shifted = values - center
    inverse = lax.rsqrt(lax.optimization_barrier(jnp.mean(shifted * shifted, axis=-1, keepdims=True)) + 1e-05)
    normed = shifted * inverse
    return inverse * (upstream - lax.optimization_barrier(jnp.mean(upstream, axis=-1, keepdims=True)) - normed * lax.optimization_barrier(jnp.mean(upstream * normed, axis=-1, keepdims=True)))

def silu_slope(values):
    sigmoid_val = jax.nn.sigmoid(values)
    return sigmoid_val * (1.0 + values * (1.0 - sigmoid_val))

def forward(nodes, edges, sources, active_slots, wet_ocean_rows, weights):
    edge_in, edge_out, node_in, node_out = weights
    count, slot_count, features = edges.shape
    edge_input = jnp.concatenate([edges, sources, jnp.broadcast_to(nodes[:, None, :], edges.shape)], axis=-1).reshape(count * slot_count, 3 * features)
    pre_edge = jnp.dot(edge_input, edge_in, preferred_element_type=jnp.float32)
    act_edge = jax.nn.silu(pre_edge).astype(jnp.bfloat16)
    pre_edge_out = jnp.dot(act_edge, edge_out, preferred_element_type=jnp.float32)
    update = normalize(pre_edge_out).reshape(count, slot_count, features)
    new_edges = (edges.astype(jnp.float32) + active_slots[:, :, None] * update).astype(jnp.bfloat16)
    message = lax.optimization_barrier(jnp.sum(active_slots[:, :, None] * new_edges.astype(jnp.float32), axis=1)).astype(jnp.bfloat16)
    node_input = jnp.concatenate([nodes, message], axis=-1)
    pre_node = jnp.dot(node_input, node_in, preferred_element_type=jnp.float32)
    act_node = jax.nn.silu(pre_node).astype(jnp.bfloat16)
    pre_node_out = jnp.dot(act_node, node_out, preferred_element_type=jnp.float32)
    new_nodes = (nodes.astype(jnp.float32) + wet_ocean_rows[:, None] * normalize(pre_node_out)).astype(jnp.bfloat16)
    return (new_nodes, new_edges, (edge_input, pre_edge, act_edge, pre_edge_out, node_input, pre_node, act_node, pre_node_out))

def reverse_sweep(saved_activation, grad_nodes, grad_edges, active_slots, wet_ocean_rows, weights):
    edge_in, edge_out, node_in, node_out = weights
    edge_input, pre_edge, act_edge, pre_edge_out, node_input, pre_node, act_node, pre_node_out = saved_activation
    count, slot_count, features = grad_edges.shape
    grad_out = normalize_back(pre_node_out, wet_ocean_rows[:, None] * grad_nodes).astype(jnp.bfloat16)
    grad_node_out = jnp.dot(act_node.T, grad_out, preferred_element_type=jnp.float32)
    grad_act = jnp.dot(grad_out, node_out.T, preferred_element_type=jnp.float32)
    grad_pre = (grad_act * silu_slope(pre_node)).astype(jnp.bfloat16)
    grad_node_in = jnp.dot(node_input.T, grad_pre, preferred_element_type=jnp.float32)
    grad_input = jnp.dot(grad_pre, node_in.T, preferred_element_type=jnp.float32)
    grad_nodes = grad_nodes + grad_input[:, :features]
    grad_edges = grad_edges + active_slots[:, :, None] * grad_input[:, None, features:]
    upstream = (active_slots[:, :, None] * grad_edges).reshape(count * slot_count, features)
    grad_edge_pre_out = normalize_back(pre_edge_out, upstream).astype(jnp.bfloat16)
    grad_edge_out = jnp.dot(act_edge.T, grad_edge_pre_out, preferred_element_type=jnp.float32)
    grad_edge_act = jnp.dot(grad_edge_pre_out, edge_out.T, preferred_element_type=jnp.float32)
    grad_edge_pre = (grad_edge_act * silu_slope(pre_edge)).astype(jnp.bfloat16)
    grad_edge_in = jnp.dot(edge_input.T, grad_edge_pre, preferred_element_type=jnp.float32)
    grad_edge_input = jnp.dot(grad_edge_pre, edge_in.T, preferred_element_type=jnp.float32)
    grad_edge_input = grad_edge_input.reshape(count, slot_count, 3 * features)
    grad_edges = grad_edges + grad_edge_input[:, :, :features]
    source_gradient = grad_edge_input[:, :, features:2 * features]
    grad_nodes = grad_nodes + lax.optimization_barrier(jnp.sum(grad_edge_input[:, :, 2 * features:], axis=1))
    return (grad_nodes, grad_edges, source_gradient, (grad_edge_in, grad_edge_out, grad_node_in, grad_node_out))

def reference(node_feats, edge_feats, node_cot, edge_cot, w_edge_in, w_edge_out, w_node_in, w_node_out, neighbours, send_rows, edge_counts, ocean_mask):
    part_of = (jnp.arange(NODES, dtype=jnp.int32) // ND)[:, None]
    before = (part_of - 1) % N_MESH
    after = (part_of + 1) % N_MESH
    left_slot = jnp.clip(neighbours - ND, 0, HALO - 1).astype(jnp.int32)
    right_slot = jnp.clip(neighbours - ND - HALO, 0, HALO - 1).astype(jnp.int32)
    own_pick = part_of * ND + neighbours
    left_pick = before * ND + send_rows[before, HALO + left_slot]
    right_pick = after * ND + send_rows[after, right_slot]
    source = jnp.where(neighbours < ND, own_pick, jnp.where(neighbours < ND + HALO, left_pick, right_pick)).astype(jnp.int32)
    flat_source = source.reshape(-1)
    active_slots = (jnp.arange(K, dtype=jnp.int32)[None, :] < edge_counts[:, None]).astype(jnp.float32)
    wet_ocean_rows = ocean_mask.astype(jnp.float32)
    weight_per_layer = [(w_edge_in[layer_index], w_edge_out[layer_index], w_node_in[layer_index], w_node_out[layer_index]) for layer_index in range(LAYERS)]

    def one_sample(carry, inputs):
        nodes, edges, node_grad, edge_grad = inputs
        saved_activations = []
        for layer_index in range(LAYERS):
            sources = nodes[flat_source].reshape(NODES, K, D)
            nodes, edges, saved_activation = forward(nodes, edges, sources, active_slots, wet_ocean_rows, weight_per_layer[layer_index])
            saved_activations.append(saved_activation)
        node_gradient = node_grad.astype(jnp.float32)
        edge_gradient = edge_grad.astype(jnp.float32)
        totals = list(carry)
        for layer_index in reversed(range(LAYERS)):
            node_gradient, edge_gradient, source_gradient, layer_gradients = reverse_sweep(saved_activations[layer_index], node_gradient, edge_gradient, active_slots, wet_ocean_rows, weight_per_layer[layer_index])
            node_gradient = node_gradient.at[flat_source].add(source_gradient.reshape(-1, D))
            totals[layer_index] = tuple((total + term for total, term in zip(totals[layer_index], layer_gradients)))
        return (tuple(totals), (node_gradient, edge_gradient.astype(jnp.bfloat16)))
    initial = tuple(((jnp.zeros((3 * D, D), jnp.float32), jnp.zeros((D, D), jnp.float32), jnp.zeros((2 * D, D), jnp.float32), jnp.zeros((D, D), jnp.float32)) for layer_index in range(LAYERS)))
    sums, (grad_nodes, grad_edges) = lax.scan(one_sample, initial, (node_feats, edge_feats, node_cot, edge_cot))
    factor = 1.0 / (SAMPLES * NODES) ** 0.5
    stacked = [jnp.stack([sums[layer_index][kind] for layer_index in range(LAYERS)]) * factor for kind in range(4)]
    return (grad_nodes, grad_edges, stacked[0], stacked[1], stacked[2], stacked[3])
```

```python
import functools

import jax
import jax.numpy as jnp
from jax import lax
from jax.experimental import pallas as pl
from jax.experimental.pallas import tpu as pltpu
from jax.sharding import PartitionSpec as P

F32 = jnp.float32
BF16 = jnp.bfloat16
VMEM = pltpu.VMEM
EPS = 1e-05


def params():
    return pltpu.CompilerParams(vmem_limit_bytes=48 * 1024 * 1024)


def whole(shape):
    return pl.BlockSpec(shape, lambda i: (0,) * len(shape))


def layer_of(array, layer):
    return pl.BlockSpec((1,) + array.shape[1:], lambda i: (layer, 0, 0))


def call(kernel, operands, specs, outs, scratch=(), flops=0):
    shapes = tuple(jax.ShapeDtypeStruct(shape, dtype) for shape, dtype in outs)
    moved = sum(a.size * a.dtype.itemsize for a in operands)
    moved += sum(s.size * s.dtype.itemsize for s in shapes)
    return pl.pallas_call(
        kernel,
        grid=(1,),
        in_specs=[whole(a.shape) if s is None else s for a, s in zip(operands, specs)],
        out_specs=tuple(whole(s.shape) for s in shapes),
        out_shape=shapes,
        scratch_shapes=list(scratch),
        compiler_params=params(),
        cost_estimate=pl.CostEstimate(flops=flops, bytes_accessed=moved, transcendentals=0),
    )(*operands)


def dot(a, b):
    return jnp.dot(a, b, preferred_element_type=F32)


def dot_nt(a, b):
    return lax.dot_general(a, b, (((1,), (1,)), ((), ())), preferred_element_type=F32)


def dot_tn(a, b):
    return lax.dot_general(a, b, (((0,), (0,)), ((), ())), preferred_element_type=F32)


def silu_and_slope(values):
    sigmoid = 0.5 * jnp.tanh(0.5 * values) + 0.5
    act = values * sigmoid
    return act, sigmoid + act * (1.0 - sigmoid)


def norm_parts(values):
    center = jnp.mean(values, axis=-1, keepdims=True)
    shifted = values - center
    inverse = lax.rsqrt(jnp.mean(shifted * shifted, axis=-1, keepdims=True) + EPS)
    return shifted * inverse, inverse


def norm_back(normed, inverse, upstream):
    return inverse * (
        upstream
        - jnp.mean(upstream, axis=-1, keepdims=True)
        - normed * jnp.mean(upstream * normed, axis=-1, keepdims=True)
    )


def halves(values):
    high = values.astype(BF16)
    low = (values - high.astype(F32)).astype(BF16)
    return jnp.concatenate([high, low], axis=0)


def node_of_edge(rows, nodes, slots):
    edge = lax.broadcasted_iota(jnp.int32, (rows, nodes), 0)
    node = lax.broadcasted_iota(jnp.int32, (rows, nodes), 1)
    return (edge // slots) == node


def pack_kernel(send_ref, h_ref, packed_ref):
    nodes, sent = h_ref.shape[0], send_ref.shape[1]
    row = lax.broadcasted_iota(jnp.int32, (nodes, sent), 0)
    pick = (row == send_ref[...]).astype(F32).astype(BF16)
    packed_ref[...] = dot_tn(pick, h_ref[...]).astype(BF16)


def prepare_kernel(slots, table, nb_ref, count_ref, spread_ref, mask_ref, live_ref):
    nodes = nb_ref.shape[0]
    rows = nodes * slots
    owner = node_of_edge(rows, nodes, slots).astype(F32)
    owner16 = owner.astype(BF16)
    listed = dot(owner16, nb_ref[...].astype(F32).astype(BF16))
    counts = dot(owner16, count_ref[...].astype(F32).astype(BF16))
    slot_here = lax.broadcasted_iota(jnp.int32, (rows, slots), 0) % slots
    slot_at = lax.broadcasted_iota(jnp.int32, (rows, slots), 1)
    source = jnp.sum(jnp.where(slot_here == slot_at, listed, 0.0), axis=1, keepdims=True)
    live = jnp.where(slot_here[:, :1].astype(F32) < counts, 1.0, 0.0)
    at = lax.broadcasted_iota(jnp.int32, (rows, table), 1).astype(F32)
    spread_ref[:, :table] = jnp.where(at == source, 1.0, 0.0).astype(BF16)
    spread_ref[:, table:] = owner16
    mask_ref[...] = (owner * live).astype(BF16)
    live_ref[...] = live


def forward_edges(chunk, e_ref, h, table, spread_ref, live_ref, wi_ref, wo_ref, put):
    rows, width = e_ref.shape
    known = table.shape[0]
    for start in range(0, rows, chunk):
        at = pl.ds(start, chunk)
        spread = spread_ref[at, :]
        src = dot(spread[:, :known], table).astype(BF16)
        own = dot(spread[:, known:], h).astype(BF16)
        e = e_ref[at, :]
        pre = dot(e, wi_ref[0, :width, :])
        pre += dot(src, wi_ref[0, width : 2 * width, :])
        pre += dot(own, wi_ref[0, 2 * width :, :])
        act, slope = silu_and_slope(pre)
        act = act.astype(BF16)
        normed, inverse = norm_parts(dot(act, wo_ref[0]))
        new_e = (e.astype(F32) + live_ref[at, :] * normed).astype(BF16)
        put(at, act, slope, normed, inverse, new_e)


def forward_nodes(h, message, wi_ref, wo_ref):
    width = h.shape[1]
    pre = dot(h, wi_ref[0, :width, :]) + dot(message, wi_ref[0, width:, :])
    act, slope = silu_and_slope(pre)
    act = act.astype(BF16)
    normed, inverse = norm_parts(dot(act, wo_ref[0]))
    return act, slope, normed, inverse


def first_forward_kernel(
    chunk, e_ref, h_ref, halo_ref, spread_ref, mask_ref, live_ref, ocean_ref, send_ref,
    wei_ref, weo_ref, wni_ref, wno_ref,
    act_ref, slope_ref, normed_ref, inverse_ref, new_e_ref,
    new_h_ref, message_ref, act_n_ref, slope_n_ref, normed_n_ref, inverse_n_ref, packed_ref,
):
    h = h_ref[...]
    table = jnp.concatenate([h, halo_ref[...]], axis=0)

    def put(at, act, slope, normed, inverse, new_e):
        act_ref[at, :] = act
        slope_ref[at, :] = slope.astype(BF16)
        normed_ref[at, :] = normed.astype(BF16)
        inverse_ref[at, :] = inverse
        new_e_ref[at, :] = new_e

    forward_edges(chunk, e_ref, h, table, spread_ref, live_ref, wei_ref, weo_ref, put)
    message = dot_tn(mask_ref[...], new_e_ref[...]).astype(BF16)
    act, slope, normed, inverse = forward_nodes(h, message, wni_ref, wno_ref)
    new_h = (h.astype(F32) + ocean_ref[...].astype(F32) * normed).astype(BF16)
    new_h_ref[...] = new_h
    message_ref[...] = message
    act_n_ref[...] = act
    slope_n_ref[...] = slope.astype(BF16)
    normed_n_ref[...] = normed.astype(BF16)
    inverse_n_ref[...] = inverse
    pack_kernel(send_ref, new_h_ref, packed_ref)


def backward_nodes(gh, h, message, act, slope, normed, inverse, ocean_ref, wi_ref, wo_ref):
    up = ocean_ref[...].astype(F32) * gh
    gout = norm_back(normed, inverse, up).astype(BF16)
    grad_out = dot_tn(act, gout)
    gpre = (dot_nt(gout, wo_ref[0]) * slope).astype(BF16)
    grad_in = dot_tn(jnp.concatenate([h, message], axis=1), gpre)
    ginput = dot_nt(gpre, wi_ref[0])
    width = h.shape[1]
    return gh + ginput[:, :width], ginput[:, width:], grad_in, grad_out


def place(blocks, me, sources, keep_ref, send_ref):
    for slot, bits in enumerate(blocks):
        for bit, ref in ((0, keep_ref), (1, send_ref)):
            device = jnp.bitwise_xor(me, bits + bit)
            row = 0
            for source in sources:
                size = source.shape[0] // (2 * len(blocks))
                start = pl.multiple_of(device * size, 16)
                ref[slot, row : row + size, :] = source[pl.ds(start, size), :].astype(BF16)
                row += size


def middle_kernel(
    chunk, blocks, me_ref, e_ref, h_ref, halo_ref, spread_ref, mask_ref, live_ref, ocean_ref,
    gh_ref, wei_ref, weo_ref, wni_ref, wno_ref,
    act_ref, slope_ref, normed_ref, inverse_ref,
    gh_out_ref, gmsg_ref, keep_ref, sent_ref,
    new_e_ref, grad_in_ref, grad_out_ref,
):
    h = h_ref[...]
    table = jnp.concatenate([h, halo_ref[...]], axis=0)

    def put(at, act, slope, normed, inverse, new_e):
        act_ref[at, :] = act
        slope_ref[at, :] = slope.astype(BF16)
        normed_ref[at, :] = normed.astype(BF16)
        inverse_ref[at, :] = inverse
        new_e_ref[at, :] = new_e

    forward_edges(chunk, e_ref, h, table, spread_ref, live_ref, wei_ref, weo_ref, put)
    message = dot_tn(mask_ref[...], new_e_ref[...]).astype(BF16)
    act, slope, normed, inverse = forward_nodes(h, message, wni_ref, wno_ref)
    gh, gmsg, grad_in, grad_out = backward_nodes(
        gh_ref[...].astype(F32), h, message, act, slope, normed, inverse, ocean_ref, wni_ref, wno_ref
    )
    gh_out_ref[...] = gh
    gmsg_ref[...] = gmsg
    grad_in_ref[...] = grad_in
    grad_out_ref[...] = grad_out
    place(blocks, me_ref[0], (grad_in_ref, grad_out_ref), keep_ref, sent_ref)


def return_halo(gh_ref, own_ref, back_ref, send_ref, wei_ref):
    nodes, width = gh_ref.shape
    row = lax.broadcasted_iota(jnp.int32, (nodes, send_ref.shape[1]), 0)
    pick = (row == send_ref[...]).astype(F32).astype(BF16)
    total = own_ref[...] + dot(pick, back_ref[...])
    both = dot_nt(halves(total), wei_ref[0, width : 2 * width, :])
    return gh_ref[...] + both[:nodes] + both[nodes:]


def nodes_back_kernel(
    blocks, me_ref, gh_ref, own_ref, back_ref, send_ref, h_ref, message_ref, act_ref, slope_ref,
    normed_ref, inverse_ref, ocean_ref, wei_ref, wni_ref, wno_ref,
    gh_out_ref, gmsg_ref, keep_ref, sent_ref, grad_in_ref, grad_out_ref,
):
    gh = return_halo(gh_ref, own_ref, back_ref, send_ref, wei_ref)
    gh, gmsg, grad_in, grad_out = backward_nodes(
        gh, h_ref[...], message_ref[...], act_ref[...], slope_ref[...].astype(F32),
        normed_ref[...].astype(F32), inverse_ref[...], ocean_ref, wni_ref, wno_ref,
    )
    gh_out_ref[...] = gh
    gmsg_ref[...] = gmsg
    grad_in_ref[...] = grad_in
    grad_out_ref[...] = grad_out
    place(blocks, me_ref[0], (grad_in_ref, grad_out_ref), keep_ref, sent_ref)


def edges_back_kernel(
    chunk, blocks, me_ref, gh_ref, gmsg_ref, ge_ref, e_ref, h_ref, halo_ref, spread_ref, live_ref,
    act_ref, slope_ref, normed_ref, inverse_ref, wei_ref, weo_ref,
    gh_out_ref, own_ref, halo_out_ref, ge_out_ref, keep_ref, sent_ref,
    gedge_ref, gpe_ref, grad_in_ref, grad_out_ref,
):
    rows, width = e_ref.shape
    nodes = h_ref.shape[0]
    known = nodes + halo_ref.shape[0]
    gmsg = halves(gmsg_ref[...])
    for start in range(0, rows, chunk):
        at = pl.ds(start, chunk)
        live = live_ref[at, :]
        owner = spread_ref[at, known:]
        sent = dot(jnp.concatenate([owner, owner], axis=1), gmsg)
        ge = ge_ref[at, :].astype(F32) + live * sent
        gedge = norm_back(normed_ref[at, :].astype(F32), inverse_ref[at, :], live * ge)
        gedge = gedge.astype(BF16)
        gpe = (dot_nt(gedge, weo_ref[0]) * slope_ref[at, :].astype(F32)).astype(BF16)
        gedge_ref[at, :] = gedge
        gpe_ref[at, :] = gpe
        ge = ge + dot_nt(gpe, wei_ref[0, :width, :])
        ge_out_ref[at, :] = ge.astype(ge_out_ref.dtype)
    gpe = gpe_ref[...]
    gathered = dot_tn(spread_ref[...], gpe)
    source, own = gathered[:known], gathered[known:]
    own_ref[...] = source[:nodes]
    halo_out_ref[...] = source[nodes:].astype(BF16)
    both = dot_nt(halves(own), wei_ref[0, 2 * width :, :])
    gh_out_ref[...] = gh_ref[...] + both[:nodes] + both[nodes:]
    h = h_ref[...]
    table = jnp.concatenate([h, halo_ref[...]], axis=0)
    grad_in_ref[:width, :] = dot_tn(e_ref[...], gpe)
    grad_in_ref[width : 2 * width, :] = dot_tn(table, source.astype(BF16))
    grad_in_ref[2 * width :, :] = dot_tn(h, own.astype(BF16))
    grad_out_ref[...] = dot_tn(act_ref[...], gedge_ref[...])
    place(blocks, me_ref[0], (grad_in_ref, grad_out_ref), keep_ref, sent_ref)


def last_kernel(gh_ref, own_ref, back_ref, send_ref, wei_ref, out_ref):
    out_ref[...] = return_halo(gh_ref, own_ref, back_ref, send_ref, wei_ref)


def trade(rows):
    count = lax.axis_size("mesh")
    half = rows.shape[0] // 2
    if count == 2:
        other = lax.ppermute(rows, "mesh", [(0, 1), (1, 0)])
        return jnp.concatenate([other[half:], other[:half]], axis=0)
    up = [(i, (i + 1) % count) for i in range(count)]
    down = [(j, i) for i, j in up]
    return jnp.concatenate(
        [lax.ppermute(rows[half:], "mesh", up), lax.ppermute(rows[:half], "mesh", down)], axis=0
    )


def flip(values, axis, bit):
    return lax.ppermute(values, axis, [(i, i ^ bit) for i in range(lax.axis_size(axis))])


def bits_of(axis):
    size = lax.axis_size(axis)
    return [1 << i for i in range(size.bit_length() - 1)]


def slot_order(route):
    order = [0]
    for bit in reversed(route):
        order = order + [slot + bit for slot in order]
    return order


def scatter_sum(keep, sent, route):
    held = [keep, flip(sent, "dp", 1)]

    def total(start, stop):
        return sum(part[start:stop].astype(F32) for part in held)

    slots = keep.shape[0]
    for bit in route:
        slots //= 2
        held.append(flip(total(slots, 2 * slots).astype(BF16), "dp", bit))
    value = total(0, 1)[0]
    for bit in bits_of("mesh"):
        mine = value.astype(BF16)
        value = mine.astype(F32) + flip(mine, "mesh", bit).astype(F32)
    return value


def body(
    node_feats,
    edge_feats,
    node_cot,
    edge_cot,
    w_edge_in,
    w_edge_out,
    w_node_in,
    w_node_out,
    neighbours,
    send_rows,
    edge_counts,
    ocean_mask,
):
    samples, nodes, width = node_feats.shape
    slots = neighbours.shape[1]
    rows = nodes * slots
    sent = send_rows.shape[1]
    known = nodes + sent
    chunk = rows // 2
    shards = lax.axis_size("dp")
    route = bits_of("dp")[1:]
    blocks = slot_order(route)
    total_rows = samples * shards * nodes * lax.axis_size("mesh")
    factor = 1.0 / total_rows**0.5
    me = lax.axis_index("dp").astype(jnp.int32).reshape(1)
    scalar = pl.BlockSpec(memory_space=pltpu.SMEM)

    h0 = node_feats.reshape(nodes, width)
    e0 = edge_feats.reshape(rows, width)
    gh = node_cot.reshape(nodes, width)
    ge = edge_cot.reshape(rows, width)
    ocean = ocean_mask.reshape(nodes, 1)
    small, large = (nodes, width), (rows, width)

    (packed0,) = call(pack_kernel, (send_rows, h0), (None,) * 2, [((sent, width), BF16)])
    halo0 = trade(packed0)
    spread, mask, live = call(
        functools.partial(prepare_kernel, slots, known),
        (neighbours, edge_counts.reshape(nodes, 1)),
        (None,) * 2,
        [((rows, known + nodes), BF16), ((rows, nodes), BF16), ((rows, 1), F32)],
    )

    weights = (w_edge_in, w_edge_out, w_node_in, w_node_out)
    specs = [tuple(layer_of(w, layer) for w in weights) for layer in range(2)]
    square = rows * width * width
    (
        act0, slope0, normed0, inverse0, e1,
        h1, message0, act_n0, slope_n0, normed_n0, inverse_n0, packed1,
    ) = call(
        functools.partial(first_forward_kernel, chunk),
        (e0, h0, halo0, spread, mask, live, ocean, send_rows) + weights,
        (None,) * 8 + specs[0],
        [(large, BF16)] * 3 + [((rows, 1), F32), (large, BF16)]
        + [(small, BF16)] * 5 + [((nodes, 1), F32), ((sent, width), BF16)],
        flops=8 * square,
    )
    halo1 = trade(packed1)

    def split(kinds):
        size = sum(w.shape[1] // shards for w in kinds)
        return [((len(blocks), size, width), BF16)] * 2

    node_kinds, edge_kinds = (w_node_in, w_node_out), (w_edge_in, w_edge_out)
    node_scratch = [VMEM(w.shape[1:], F32) for w in node_kinds]
    edge_scratch = [VMEM(large, BF16)] * 2 + [VMEM(w.shape[1:], F32) for w in edge_kinds]

    act1, slope1, normed1, inverse1, gh, gmsg, keep_n1, sent_n1 = call(
        functools.partial(middle_kernel, chunk, blocks),
        (me, e1, h1, halo1, spread, mask, live, ocean, gh) + weights,
        (scalar,) + (None,) * 8 + specs[1],
        [(large, BF16)] * 3 + [((rows, 1), F32)] + [(small, F32)] * 2 + split(node_kinds),
        scratch=[VMEM(large, BF16)] + node_scratch,
        flops=10 * square,
    )
    sum_n1 = scatter_sum(keep_n1, sent_n1, route)

    def edges_back(layer, gh, gmsg, ge, e, h, halo, act, slope, normed, inverse, ge_type):
        return call(
            functools.partial(edges_back_kernel, chunk, blocks),
            (me, gh, gmsg, ge, e, h, halo, spread, live, act, slope, normed, inverse) + weights[:2],
            (scalar,) + (None,) * 12 + specs[layer][:2],
            [(small, F32)] * 2 + [((sent, width), BF16), (large, ge_type)] + split(edge_kinds),
            scratch=edge_scratch,
            flops=12 * square,
        )

    gh, own, halo_out, ge, keep_e1, sent_e1 = edges_back(
        1, gh, gmsg, ge, e1, h1, halo1, act1, slope1, normed1, inverse1, F32
    )
    back = trade(halo_out)
    sum_e1 = scatter_sum(keep_e1, sent_e1, route)

    gh, gmsg, keep_n0, sent_n0 = call(
        functools.partial(nodes_back_kernel, blocks),
        (me, gh, own, back, send_rows, h0, message0, act_n0, slope_n0, normed_n0, inverse_n0, ocean)
        + (w_edge_in, w_node_in, w_node_out),
        (scalar,) + (None,) * 11 + (specs[1][0],) + specs[0][2:],
        [(small, F32)] * 2 + split(node_kinds),
        scratch=node_scratch,
        flops=3 * square,
    )
    sum_n0 = scatter_sum(keep_n0, sent_n0, route)
    gh, own, halo_out, ge, keep_e0, sent_e0 = edges_back(
        0, gh, gmsg, ge, e0, h0, halo0, act0, slope0, normed0, inverse0, BF16
    )
    back = trade(halo_out)
    sum_e0 = scatter_sum(keep_e0, sent_e0, route)
    (gh,) = call(
        last_kernel,
        (gh, own, back, send_rows, w_edge_in),
        (None,) * 4 + (specs[0][0],),
        [(small, F32)],
        flops=square // 4,
    )

    def joined(first, last, start, stop):
        return jnp.stack([first[start:stop], last[start:stop]]) * factor

    cut_e, cut_n = w_edge_in.shape[1] // shards, w_node_in.shape[1] // shards
    return (
        gh.reshape(samples, nodes, width),
        ge.reshape(samples, nodes, slots, width),
        joined(sum_e0, sum_e1, 0, cut_e),
        joined(sum_e0, sum_e1, cut_e, None),
        joined(sum_n0, sum_n1, 0, cut_n),
        joined(sum_n0, sum_n1, cut_n, None),
    )


def solution(mesh):
    placed = (
        P("dp", "mesh", None),
        P("dp", "mesh", None, None),
        P("dp", "mesh", None),
        P("dp", "mesh", None, None),
        P(),
        P(),
        P(),
        P(),
        P("mesh", None),
        P("mesh", None),
        P("mesh"),
        P("mesh"),
    )
    return jax.shard_map(
        body,
        mesh=mesh,
        in_specs=placed,
        out_specs=(
            P("dp", "mesh", None),
            P("dp", "mesh", None, None),
            P(None, "dp", None),
            P(None, "dp", None),
            P(None, "dp", None),
            P(None, "dp", None),
        ),
        check_vma=False,
    )
```

```python
import functools

import jax
import jax.numpy as jnp
from jax import lax
from jax.experimental import pallas as pl
from jax.experimental.pallas import tpu as pltpu
from jax.sharding import PartitionSpec as P

F32 = jnp.float32
BF16 = jnp.bfloat16
VMEM = pltpu.VMEM
EPS = 1e-05
MIB = 1024 * 1024
LIMIT = 20 * MIB


def in_hbm(array):
    return pltpu.with_memory_space_constraint(array, pltpu.HBM)


class Part:
    def __init__(self, array, index=(), shape=None, pin=True):
        self.array, self.index = (in_hbm(array) if pin else array), index
        self.shape = tuple(array.shape if shape is None else shape)


def rows_of(weight, layer, start=0, stop=None):
    stop = weight.shape[1] if stop is None else stop
    return Part(weight, (layer, pl.ds(start, stop - start)), (stop - start, weight.shape[2]))


class Arriving:
    def __init__(self, copy, ref):
        self.copy, self.ref, self.shape, self.dtype = copy, ref, ref.shape, ref.dtype

    def __getitem__(self, index):
        if self.copy is not None:
            self.copy.wait()
            self.copy = None
        return self.ref[index]


class Leaving:
    def __init__(self, copy, ref):
        self.copy, self.ref, self.shape, self.dtype = copy, ref, ref.shape, ref.dtype
        self.started = False

    def __getitem__(self, index):
        return self.ref[index]

    def __setitem__(self, index, value):
        self.ref[index] = value

    def flush(self):
        if not self.started:
            self.copy.start()
            self.started = True


def far(shape, dtype):
    return (shape, dtype, True)


def call(kernel, operands, outs, scratch=(), smem=(), after=(), fetch=(), limit=LIMIT):
    shapes = [jax.ShapeDtypeStruct(out[0], out[1]) for out in outs]
    is_far = [len(out) > 2 for out in outs] + [False] * len(fetch)
    results = len(shapes)
    shapes += [jax.ShapeDtypeStruct(p.shape, p.array.dtype) for p in fetch]
    remote = [isinstance(p, Part) for p in operands]
    arrays = [p.array if r else p for p, r in zip(operands, remote)]
    buffers = [VMEM(p.shape, p.array.dtype) for p, r in zip(operands, remote) if r]
    buffers += [VMEM(s.shape, s.dtype) for s, r in zip(shapes, is_far) if r]
    copies = len(buffers) + len(fetch)
    sems = [pltpu.SemaphoreType.DMA((max(copies, 1),))]

    def run(*refs):
        refs = list(refs)

        def cut(count):
            taken = refs[:count]
            del refs[:count]
            return taken

        scalars, sources, origins = cut(len(smem)), cut(len(arrays)), cut(len(fetch))
        cut(len(after))
        targets, held, (sem,) = cut(len(shapes)), cut(len(buffers)), cut(1)
        sems = [sem.at[at] for at in range(copies)]
        ins, leaving, fetched = [], [], []
        for part, source, r in zip(operands, sources, remote):
            if r:
                view = source.at[part.index] if part.index else source
                ref = held.pop(0)
                copy = pltpu.make_async_copy(view, ref, sems.pop(0))
                copy.start()
                source = Arriving(copy, ref)
            ins.append(source)
        for part, origin, target in zip(fetch, origins, targets[results:]):
            view = origin.at[part.index] if part.index else origin
            copy = pltpu.make_async_copy(view, target, sems.pop(0))
            copy.start()
            fetched.append(copy)
        results_here = []
        for target, r in zip(targets[:results], is_far):
            if r:
                ref = held.pop(0)
                target = Leaving(pltpu.make_async_copy(ref, target, sems.pop(0)), ref)
                leaving.append(target)
            results_here.append(target)
        kernel(*scalars, *ins, *results_here, *refs)
        for ref in ins:
            if isinstance(ref, Arriving):
                ref[:1]
        for ref in leaving:
            ref.flush()
        for copy in fetched:
            copy.wait()
        for ref in leaving:
            ref.copy.wait()

    def space(r):
        return pl.BlockSpec(memory_space=pl.ANY if r else VMEM)

    return pl.pallas_call(
        run,
        in_specs=[pl.BlockSpec(memory_space=pltpu.SMEM)] * len(smem)
        + [space(r) for r in remote]
        + [space(True)] * len(fetch)
        + [pl.BlockSpec(memory_space=pl.ANY)] * len(after),
        out_specs=tuple(space(r) for r in is_far),
        out_shape=tuple((pltpu.HBM if r else VMEM)(s.shape, s.dtype) for s, r in zip(shapes, is_far)),
        scratch_shapes=buffers + sems + list(scratch),
        compiler_params=pltpu.CompilerParams(vmem_limit_bytes=limit),
        cost_estimate=pl.CostEstimate(flops=0, bytes_accessed=0, transcendentals=0),
    )(*smem, *arrays, *[p.array for p in fetch], *after)


def flush(*refs):
    for ref in refs:
        if isinstance(ref, Leaving):
            ref.flush()


def dot(a, b):
    return jnp.dot(a, b, preferred_element_type=F32)


def dot_nt(a, b):
    return lax.dot_general(a, b, (((1,), (1,)), ((), ())), preferred_element_type=F32)


def dot_tn(a, b):
    return lax.dot_general(a, b, (((0,), (0,)), ((), ())), preferred_element_type=F32)


def silu_and_slope(values):
    sigmoid = 0.5 * jnp.tanh(0.5 * values) + 0.5
    act = values * sigmoid
    return act, sigmoid + act * (1.0 - sigmoid)


def norm_parts(values):
    center = jnp.mean(values, axis=-1, keepdims=True)
    shifted = values - center
    inverse = lax.rsqrt(jnp.mean(shifted * shifted, axis=-1, keepdims=True) + EPS)
    return shifted * inverse, inverse


def norm_back(normed, inverse, upstream):
    return inverse * (
        upstream
        - jnp.mean(upstream, axis=-1, keepdims=True)
        - normed * jnp.mean(upstream * normed, axis=-1, keepdims=True)
    )


def halves(values):
    high = values.astype(BF16)
    low = (values - high.astype(F32)).astype(BF16)
    return jnp.concatenate([high, low], axis=0)


def node_of_edge(rows, nodes, slots):
    edge = lax.broadcasted_iota(jnp.int32, (rows, nodes), 0)
    node = lax.broadcasted_iota(jnp.int32, (rows, nodes), 1)
    return (edge // slots) == node


def pick_rows(send_ref, nodes):
    row = lax.broadcasted_iota(jnp.int32, (nodes, send_ref.shape[1]), 0)
    return (row == send_ref[...]).astype(F32).astype(BF16)


def pack_kernel(send_ref, h_ref, packed_ref):
    pick = pick_rows(send_ref, h_ref.shape[0])
    packed_ref[...] = dot_tn(pick, h_ref[...]).astype(BF16)


def prepare_kernel(
    table, chunk, nb_ref, count_ref, ocean_ref, h_ref, e_ref, we_ref, wr_ref,
    spread_ref, mask_ref, live_ref, wet_ref, pre_ref,
):
    slots, nodes = nb_ref.shape
    rows = nodes * slots
    owner = node_of_edge(rows, nodes, slots).astype(F32)
    owner16 = owner.astype(BF16)
    listed = dot_nt(owner16, nb_ref[...].astype(F32).astype(BF16))
    slot_here = lax.broadcasted_iota(jnp.int32, (rows, slots), 0) % slots
    slot_at = lax.broadcasted_iota(jnp.int32, (rows, slots), 1)
    source = jnp.sum(jnp.where(slot_here == slot_at, listed, 0.0), axis=1, keepdims=True)
    half = (table - nodes) // 2
    moved = jnp.where(source >= nodes + half, source - half, source + half)
    source = jnp.where(source >= nodes, moved, source)
    at = lax.broadcasted_iota(jnp.int32, (rows, table), 1).astype(F32)
    spread_ref[:, :table] = jnp.where(at == source, 1.0, 0.0).astype(BF16)
    spread_ref[:, table:] = owner16
    slot_of_row = lax.broadcasted_iota(jnp.int32, (rows, nodes), 0) % slots
    mask = jnp.where(slot_of_row < count_ref[...], owner, 0.0)
    mask_ref[...] = mask.astype(BF16)
    live_ref[...] = jnp.sum(mask, axis=1, keepdims=True)
    row = lax.broadcasted_iota(jnp.int32, (nodes, nodes), 0)
    column = lax.broadcasted_iota(jnp.int32, (nodes, nodes), 1)
    wet = jnp.where(row == column, ocean_ref[...].astype(F32), 0.0)
    wet_ref[...] = jnp.sum(wet, axis=1, keepdims=True)
    partial_kernel(chunk, h_ref, spread_ref, e_ref, we_ref, wr_ref, pre_ref)


def partial_kernel(chunk, h_ref, spread_ref, e_ref, we_ref, wr_ref, pre_ref):
    rows, width = e_ref.shape
    known = spread_ref.shape[1] - h_ref.shape[0]
    h = h_ref[...]
    for start in range(0, rows, chunk):
        at = pl.ds(start, chunk)
        own = dot(spread_ref[at, known:], h).astype(BF16)
        pre = dot(e_ref[at, :], we_ref[...])
        pre_ref[at, :] = pre + dot(own, wr_ref[...])


def forward_edges(chunk, pre_ref, e_ref, table, spread_ref, live_ref, ws_ref, wo_ref, put):
    rows, width = e_ref.shape
    known = table.shape[0]
    for start in range(0, rows, chunk):
        at = pl.ds(start, chunk)
        src = dot(spread_ref[at, :known], table).astype(BF16)
        pre = pre_ref[at, :] + dot(src, ws_ref[...])
        act, slope = silu_and_slope(pre)
        act = act.astype(BF16)
        normed, inverse = norm_parts(dot(act, wo_ref[...]))
        new_e = (e_ref[at, :].astype(F32) + live_ref[at, :] * normed).astype(BF16)
        put(at, act, slope, normed, inverse, new_e)


def forward_nodes(h, message, wi_ref, wo_ref):
    width = h.shape[1]
    pre = dot(h, wi_ref[:width, :]) + dot(message, wi_ref[width:, :])
    act, slope = silu_and_slope(pre)
    act = act.astype(BF16)
    normed, inverse = norm_parts(dot(act, wo_ref[...]))
    return act, slope, normed, inverse


def first_forward_kernel(
    chunk, pre_ref, e_ref, h_ref, halo_ref, spread_ref, mask_ref, live_ref, wet_ref, send_ref,
    ws_ref, weo_ref, wni_ref, wno_ref,
    act_ref, slope_ref, normed_ref, inverse_ref, new_e_ref,
    new_h_ref, message_ref, act_n_ref, slope_n_ref, normed_n_ref, inverse_n_ref, packed_ref,
):
    h = h_ref[...]
    table = jnp.concatenate([h, halo_ref[...]], axis=0)

    def put(at, act, slope, normed, inverse, new_e):
        act_ref[at, :] = act
        slope_ref[at, :] = slope.astype(BF16)
        normed_ref[at, :] = normed.astype(BF16)
        inverse_ref[at, :] = inverse
        new_e_ref[at, :] = new_e

    forward_edges(chunk, pre_ref, e_ref, table, spread_ref, live_ref, ws_ref, weo_ref, put)
    flush(act_ref, slope_ref, normed_ref, inverse_ref, new_e_ref)
    message = dot_tn(mask_ref[...], new_e_ref[...]).astype(BF16)
    act, slope, normed, inverse = forward_nodes(h, message, wni_ref, wno_ref)
    message_ref[...] = message
    act_n_ref[...] = act
    slope_n_ref[...] = slope.astype(BF16)
    normed_n_ref[...] = normed.astype(BF16)
    inverse_n_ref[...] = inverse
    flush(message_ref, act_n_ref, slope_n_ref, normed_n_ref, inverse_n_ref)
    new_h = (h.astype(F32) + wet_ref[...] * normed).astype(BF16)
    new_h_ref[...] = new_h
    packed_ref[...] = dot_tn(pick_rows(send_ref, h.shape[0]), new_h).astype(BF16)


def backward_nodes(gh, slope, normed, inverse, wet_ref, wi_ref, wo_ref, gout_ref, gpre_ref):
    gout = norm_back(normed, inverse, wet_ref[...] * gh).astype(BF16)
    gpre = (dot_nt(gout, wo_ref[...]) * slope).astype(BF16)
    gout_ref[...] = gout
    gpre_ref[...] = gpre
    ginput = dot_nt(gpre, wi_ref[...])
    width = gh.shape[1]
    return gh + ginput[:, :width], ginput[:, width:]


def backward_edges(
    chunk, known, gh, gmsg, ge_ref, spread_ref, live_ref, slope_ref, normed_ref, inverse_ref,
    we_ref, wr_ref, wo_ref, gh_out_ref, more_ref, own_ref, halo_out_ref, ge_out_ref, gedge_ref, gpe_ref, sums_ref,
):
    rows, width = ge_ref.shape
    nodes = gh.shape[0]
    gh_out_ref[...] = gh
    gmsg = halves(gmsg)
    for start in range(0, rows, chunk):
        at = pl.ds(start, chunk)
        live = live_ref[at, :]
        owner = spread_ref[at, known:]
        sent = dot(jnp.concatenate([owner, owner], axis=1), gmsg)
        ge = ge_ref[at, :].astype(F32) + live * sent
        gedge = norm_back(normed_ref[at, :].astype(F32), inverse_ref[at, :], live * ge)
        gedge = gedge.astype(BF16)
        gpe = (dot_nt(gedge, wo_ref[...]) * slope_ref[at, :].astype(F32)).astype(BF16)
        gedge_ref[at, :] = gedge
        gpe_ref[at, :] = gpe
        ge = ge + dot_nt(gpe, we_ref[...])
        ge_out_ref[at, :] = ge.astype(ge_out_ref.dtype)
    flush(gedge_ref, gpe_ref, ge_out_ref)
    gathered = dot_tn(spread_ref[...], gpe_ref[...])
    own_ref[...] = gathered[:nodes]
    halo_out_ref[...] = gathered[nodes:known].astype(BF16)
    sums_ref[...] = gathered.astype(BF16)
    both = dot_nt(halves(gathered[known:]), wr_ref[...])
    more_ref[...] = both[:nodes] + both[nodes:]


def middle_kernel(
    chunk, pre_ref, e_ref, h_ref, halo_ref, spread_ref, mask_ref, live_ref, wet_ref,
    gh_ref, ge_ref, ws_ref, weo_ref, wni_ref, wno_ref, we_ref, wr_ref,
    act_ref, message_ref, act_n_ref, gout_ref, gpre_ref,
    gh_out_ref, more_ref, own_ref, halo_out_ref, ge_out_ref, gedge_ref, gpe_ref, sums_ref,
    slope_ref, normed_ref, inverse_ref, new_e_ref,
):
    h = h_ref[...]
    table = jnp.concatenate([h, halo_ref[...]], axis=0)

    def put(at, act, slope, normed, inverse, new_e):
        act_ref[at, :] = act
        slope_ref[at, :] = slope.astype(BF16)
        normed_ref[at, :] = normed.astype(BF16)
        inverse_ref[at, :] = inverse
        new_e_ref[at, :] = new_e

    forward_edges(chunk, pre_ref, e_ref, table, spread_ref, live_ref, ws_ref, weo_ref, put)
    message = dot_tn(mask_ref[...], new_e_ref[...]).astype(BF16)
    act, slope, normed, inverse = forward_nodes(h, message, wni_ref, wno_ref)
    message_ref[...] = message
    act_n_ref[...] = act
    flush(act_ref)
    gh, gmsg = backward_nodes(
        gh_ref[...].astype(F32), slope, normed, inverse, wet_ref, wni_ref, wno_ref, gout_ref, gpre_ref
    )
    backward_edges(
        chunk, table.shape[0], gh, gmsg, ge_ref, spread_ref, live_ref, slope_ref, normed_ref,
        inverse_ref, we_ref, wr_ref, weo_ref, gh_out_ref, more_ref, own_ref, halo_out_ref, ge_out_ref,
        gedge_ref, gpe_ref, sums_ref,
    )


def return_halo(gh_ref, more_ref, own_ref, back_ref, send_ref, wei_ref):
    nodes, width = gh_ref.shape
    total = own_ref[...] + dot(pick_rows(send_ref, nodes), back_ref[...])
    both = dot_nt(halves(total), wei_ref[...])
    return gh_ref[...] + more_ref[...] + both[:nodes] + both[nodes:]


def first_backward_kernel(
    chunk, gh_ref, more_ref, own_ref, back_ref, send_ref, slope_n_ref, normed_n_ref, inverse_n_ref, wet_ref,
    ge_ref, spread_ref, live_ref, slope_ref, normed_ref, inverse_ref,
    ws_ref, wno_ref, wni_ref, weo_ref, we_ref, wr_ref,
    gout_ref, gpre_ref, gh_out_ref, more_out_ref, own_out_ref, halo_out_ref, ge_out_ref,
    gedge_ref, gpe_ref, sums_ref,
):
    gh = return_halo(gh_ref, more_ref, own_ref, back_ref, send_ref, ws_ref)
    gh, gmsg = backward_nodes(
        gh, slope_n_ref[...].astype(F32), normed_n_ref[...].astype(F32), inverse_n_ref[...],
        wet_ref, wni_ref, wno_ref, gout_ref, gpre_ref,
    )
    known = spread_ref.shape[1] - gh.shape[0]
    backward_edges(
        chunk, known, gh, gmsg, ge_ref, spread_ref, live_ref, slope_ref, normed_ref,
        inverse_ref, we_ref, wr_ref, weo_ref, gh_out_ref, more_out_ref, own_out_ref, halo_out_ref, ge_out_ref,
        gedge_ref, gpe_ref, sums_ref,
    )


def last_kernel(gh_ref, more_ref, own_ref, back_ref, send_ref, wei_ref, out_ref):
    out_ref[...] = return_halo(gh_ref, more_ref, own_ref, back_ref, send_ref, wei_ref)


def place(order, me_ref, first_ref, second_ref, keep_ref, sent_ref):
    rows = keep_ref.shape[1]
    count = keep_ref.shape[0]
    for bits in range(0, count, 2):
        spots = [order.index((bits, side)) for side in (0, 1)]
        for bit, out_ref in ((0, keep_ref), (1, sent_ref)):
            device = jnp.bitwise_xor(me_ref[0], bits + bit)
            row = 0
            for ref in (first_ref, second_ref):
                size = ref.shape[0] // count
                start = pl.multiple_of(device * size, 16)
                done = 0
                while done < size:
                    half, at = divmod(row, rows)
                    step = min(size - done, rows - at)
                    index = jnp.where(me_ref[1] == half, spots[0], spots[1])
                    piece = ref[pl.ds(pl.multiple_of(start + done, 16), step), :]
                    out_ref[index, at : at + step, :] = piece.astype(BF16)
                    row += step
                    done += step
            if row < 2 * rows:
                index = jnp.where(me_ref[1] == 1, spots[0], spots[1])
                filler = jnp.zeros((2 * rows - row, keep_ref.shape[2]), BF16)
                out_ref[index, row - rows :, :] = filler


def edge_weights_kernel(
    layout, me_ref, e_ref, h_ref, halo_ref, act_ref, gedge_ref, gpe_ref, sums_ref,
    keep_ref, sent_ref, grad_in_ref, grad_out_ref,
):
    width = e_ref.shape[1]
    h = h_ref[...]
    known = h.shape[0] + halo_ref.shape[0]
    table = jnp.concatenate([h, halo_ref[...]], axis=0)
    grad_in_ref[:width, :] = dot_tn(e_ref[...], gpe_ref[...])
    grad_in_ref[width : 2 * width, :] = dot_tn(table, sums_ref[:known, :])
    grad_in_ref[2 * width :, :] = dot_tn(h, sums_ref[known:, :])
    grad_out_ref[...] = dot_tn(act_ref[...], gedge_ref[...])
    place(layout, me_ref, grad_in_ref, grad_out_ref, keep_ref, sent_ref)


def node_weights_kernel(
    layout, me_ref, h_ref, message_ref, act_ref, gout_ref, gpre_ref,
    keep_ref, sent_ref, grad_in_ref, grad_out_ref,
):
    width = h_ref.shape[1]
    gpre = gpre_ref[...]
    grad_in_ref[:width, :] = dot_tn(h_ref[...], gpre)
    grad_in_ref[width:, :] = dot_tn(message_ref[...], gpre)
    grad_out_ref[...] = dot_tn(act_ref[...], gout_ref[...])
    place(layout, me_ref, grad_in_ref, grad_out_ref, keep_ref, sent_ref)


def trade(rows, back=False):
    count = lax.axis_size("mesh")
    if count == 2:
        return lax.ppermute(rows, "mesh", [(0, 1), (1, 0)])
    half = rows.shape[0] // 2
    up = [(i, (i + 1) % count) for i in range(count)]
    down = [(j, i) for i, j in up]
    first, second = (up, down) if back else (down, up)
    return jnp.concatenate(
        [lax.ppermute(rows[:half], "mesh", first), lax.ppermute(rows[half:], "mesh", second)], axis=0
    )


def flip(values, axis, bit):
    return lax.ppermute(values, axis, [(i, i ^ bit) for i in range(lax.axis_size(axis))])


def bits_of(axis):
    size = lax.axis_size(axis)
    return [1 << i for i in range(size.bit_length() - 1)]


def slot_order(route):
    order = [(0, 0)]
    for axis, bit in reversed(route):
        if axis == "dp":
            order = order + [(bits + bit, side) for bits, side in order]
        else:
            order = order + [(bits, 1) for bits, side in order]
    return order


class Sum:
    def __init__(self, keep):
        self.held = [(keep, 0)]
        self.slots, self.rows = keep.shape[0], keep.shape[1]

    def parts(self, start, stop):
        return [
            Part(
                array,
                (pl.ds(start, stop - start), pl.ds(row, self.rows)),
                (stop - start, self.rows, array.shape[2]),
                pin=at == 0,
            )
            for at, (array, row) in enumerate(self.held)
        ]


def add_kernel(groups, tail, *refs):
    refs = list(refs)
    count = sum(sum(group) for group in groups) + tail
    outs = refs[count:]
    if tail:
        more = refs[count - 1]
        outs[-1][outs[-1].shape[0] - 1, : more.shape[0], :] = more[...]
    for group, out in zip(groups, outs):
        row = 0
        for count in group:
            terms, refs = refs[:count], refs[count:]
            rows = terms[0].shape[1]
            total = sum(term[...].astype(F32) for term in terms)
            out[: terms[0].shape[0], row : row + rows, :] = total.astype(BF16)
            row += rows
        flush(out)


def add(wanted, after=(), tail=None):
    operands, groups, outs = [], [], []
    for sums in wanted:
        group, count = [], 0
        for one in sums:
            if one.slots > 1:
                one.slots //= 2
                span = (one.slots, 2 * one.slots)
            else:
                span = (0, 1)
            parts = one.parts(*span)
            operands += parts
            group.append(len(parts))
            count = span[1] - span[0]
        groups.append(group)
        outs.append(((count, sum(one.rows for one in sums), parts[0].shape[2]), BF16))
    if tail is not None:
        (count, size, depth), dtype = outs[-1]
        outs[-1] = ((count + 1, size, depth), dtype)
        operands.append(tail)
    return call(functools.partial(add_kernel, groups, tail is not None), operands, outs, after=after)


def take(sums, values):
    row = 0
    for one in sums:
        one.held.append((values, row))
        row += one.rows


def gather(values):
    mine = values[0]
    for bit in bits_of("mesh")[1:]:
        mine = (mine.astype(F32) + flip(mine, "mesh", bit).astype(F32)).astype(BF16)
    return mine, flip(mine, "mesh", 1)


def output_kernel(
    factor, splits, me_ref, mine0_ref, other0_ref, mine1_ref, other1_ref, *outs
):
    low = me_ref[1] == 0
    for layer, (mine, other) in enumerate(((mine0_ref, other0_ref), (mine1_ref, other1_ref))):
        row = 0
        for pair, rows in enumerate(splits):
            a = mine[row : row + rows, :].astype(F32) * factor
            b = other[row : row + rows, :].astype(F32) * factor
            both = jnp.concatenate([jnp.where(low, a, b), jnp.where(low, b, a)], axis=0)
            first, second = outs[2 * pair], outs[2 * pair + 1]
            cut, end = first.shape[1], first.shape[1] + second.shape[1]
            first[layer] = both[:cut]
            second[layer] = both[cut:end]
            row += rows


def body(
    node_feats,
    edge_feats,
    node_cot,
    edge_cot,
    w_edge_in,
    w_edge_out,
    w_node_in,
    w_node_out,
    neighbours,
    send_rows,
    edge_counts,
    ocean_mask,
):
    samples, nodes, width = node_feats.shape
    slots = neighbours.shape[1]
    rows = nodes * slots
    sent = send_rows.shape[1]
    known = nodes + sent
    chunk = rows // 2
    shards = lax.axis_size("dp")
    total_rows = samples * shards * nodes * lax.axis_size("mesh")
    factor = 1.0 / total_rows**0.5
    beyond = [("dp", bit) for bit in bits_of("dp")[2:]]
    edge_route = [("dp", 2), ("mesh", 1)] + beyond
    node_route = [("mesh", 1), ("dp", 2)] + beyond
    edge_order, node_order = slot_order(edge_route), slot_order(node_route)
    me = jnp.stack([lax.axis_index("dp"), lax.axis_index("mesh") % 2]).astype(jnp.int32)

    h0 = node_feats.reshape(nodes, width)
    e0 = edge_feats.reshape(rows, width)
    gh = node_cot.reshape(nodes, width)
    ge = edge_cot.reshape(rows, width)
    weights = (w_edge_in, w_edge_out, w_node_in, w_node_out)
    small, large, thin = (nodes, width), (rows, width), (sent, width)
    source = [rows_of(w_edge_in, layer, width, 2 * width) for layer in range(2)]
    edge = [rows_of(w_edge_in, layer, 0, width) for layer in range(2)]
    receiver = [rows_of(w_edge_in, layer, 2 * width) for layer in range(2)]
    edge_out = [rows_of(w_edge_out, layer) for layer in range(2)]
    node_in = [rows_of(w_node_in, layer) for layer in range(2)]
    node_out = [rows_of(w_node_out, layer) for layer in range(2)]

    (packed0,) = call(pack_kernel, (Part(send_rows), Part(h0)), [(thin, BF16)])
    halo0 = trade(packed0)
    spread, mask, live, wet, pre0, h0_near, e0_near, source0, edge_out0, node_in0, node_out0 = call(
        functools.partial(prepare_kernel, known, chunk),
        (Part(neighbours.T), Part(edge_counts.reshape(1, nodes)), Part(ocean_mask.reshape(1, nodes)))
        + (Part(h0), Part(e0), edge[0], receiver[0]),
        [
            ((rows, known + nodes), BF16), ((rows, nodes), BF16), ((rows, 1), F32),
            ((nodes, 1), F32), (large, F32),
        ],
        fetch=(Part(h0), Part(e0), source[0], edge_out[0], node_in[0], node_out[0]),
    )
    (
        act0, slope0, normed0, inverse0, e1,
        h1, message0, act_n0, slope_n0, normed_n0, inverse_n0, packed1,
        edge1_w, receiver1_w, source1_w,
    ) = call(
        functools.partial(first_forward_kernel, chunk),
        (pre0, e0_near, h0_near, halo0, spread, mask, live, wet, send_rows)
        + (source0, edge_out0, node_in0, node_out0),
        [far(large, BF16)] * 3 + [far((rows, 1), F32), (large, BF16), (small, BF16)]
        + [far(small, BF16)] * 4 + [far((nodes, 1), F32), (thin, BF16)],
        fetch=(edge[1], receiver[1], source[1]),
    )
    halo1 = trade(packed1)
    pre1, edge_out1, node_in1, node_out1, gh_near, ge_near = call(
        functools.partial(partial_kernel, chunk),
        (h1, spread, e1, edge1_w, receiver1_w),
        [(large, F32)],
        fetch=(edge_out[1], node_in[1], node_out[1], Part(gh), Part(ge)),
    )
    backward_outs = [(small, F32)] * 3 + [(thin, BF16)]
    backward_tail = [(large, BF16)] * 2 + [((known + nodes, width), BF16)]
    act1, message1, act_n1, gout1, gpre1, gh, more, own, halo_out, ge, gedge1, gpe1, sums1, *near_w = call(
        functools.partial(middle_kernel, chunk),
        (pre1, e1, h1, halo1, spread, mask, live, wet, gh_near, ge_near)
        + (source1_w, edge_out1, node_in1, node_out1, edge1_w, receiver1_w),
        [(large, BF16)] + [(small, BF16)] * 4 + backward_outs + [far(large, F32)] + backward_tail,
        scratch=[VMEM(large, BF16)] * 2 + [VMEM((rows, 1), F32), VMEM(large, BF16)],
        fetch=(node_out[0], node_in[0], edge_out[0], edge[0], receiver[0]),
    )
    back = trade(halo_out, back=True)

    def weight_sum(kernel, order, operands, kinds, after=(), fetch=()):
        size = sum(w.shape[1] // shards for w in kinds)
        size = -(-size // 32) * 32
        keep, send, *fetched = call(
            functools.partial(kernel, order),
            operands,
            [far((shards, size // 2, width), BF16), ((shards, size // 2, width), BF16)],
            scratch=[VMEM(w.shape[1:], F32) for w in kinds],
            smem=(me,),
            after=after,
            fetch=fetch,
        )
        one = Sum(keep)
        take([one], flip(send, "dp", 1))
        return one, fetched

    def edge_sum(e, h, halo, act, gedge, gpe, sums, **more):
        return weight_sum(
            edge_weights_kernel, edge_order,
            (e, h, halo, act, gedge, gpe, sums), (w_edge_in, w_edge_out), **more,
        )

    def node_sum(h, message, act, gout, gpre, **more):
        return weight_sum(
            node_weights_kernel, node_order,
            (h, message, act, gout, gpre), (w_node_in, w_node_out), **more,
        )

    needed = (Part(slope_n0), Part(normed_n0), Part(inverse_n0), Part(slope0), Part(normed0))
    edge1, near = edge_sum(e1, h1, halo1, act1, gedge1, gpe1, sums1)
    node1, near = node_sum(
        h1, message1, act_n1, gout1, gpre1, fetch=needed + (Part(inverse0), Part(ge))
    )
    both1 = [edge1, node1]
    (edge1_x,) = add([[edge1]])
    take([edge1], flip(edge1_x, "dp", 2))
    (node1_y,) = add([[node1]], after=(back,))
    take([node1], flip(node1_y, "mesh", 1))
    gout0, gpre0, gh, more, own, halo_out, ge, gedge0, gpe0, sums0, e0_near, act0, h0_near = call(
        functools.partial(first_backward_kernel, chunk),
        (gh, more, own, back, send_rows, near[0], near[1], near[2], wet)
        + (near[6], spread, live, near[3], near[4], near[5], source1_w, *near_w),
        [(small, BF16)] * 2 + backward_outs + [far(large, BF16)] + backward_tail,
        after=(edge1_x, node1_y),
        fetch=(Part(e0), Part(act0), Part(h0)),
    )
    edge0, _ = edge_sum(e0_near, h0_near, halo0, act0, gedge0, gpe0, sums0)
    node0, _ = node_sum(
        h0_near, Part(message0), Part(act_n0), gout0, gpre0, after=(edge1.held[-1][0], node1.held[-1][0])
    )
    both0 = [edge0, node0]
    edge1_y, edge0_x = add([[edge1], [edge0]])
    take([edge1], flip(edge1_y, "mesh", 1))
    take([edge0], flip(edge0_x, "dp", 2))
    joint = lax.axis_size("mesh") == 2 and sent <= node0.rows
    node1_x, node0_y = add(
        [[node1], [node0]], after=(edge0_x,), tail=halo_out if joint else None
    )
    take([node1], flip(node1_x, "dp", 2))
    arrived = flip(node0_y, "mesh", 1)
    take([node0], arrived)
    if joint:
        back = Part(arrived, (arrived.shape[0] - 1, pl.ds(0, sent)), thin, pin=False)
    else:
        back = trade(halo_out, back=True)
    bits = bits_of("dp")[2:]
    edge0_y, node0_x, near1 = add([[edge0], [node0], both1])
    take([node0], flip(node0_x, "dp", 2))
    take([edge0], flip(edge0_y, "mesh", 1))
    take(both1, flip(near1, "dp", bits[0]))
    (gh,) = call(
        last_kernel, (gh, more, own, back, send_rows, source[0]), [far(small, F32)],
        after=(edge0_y,),
    )
    done = (gh,)
    for at, bit in enumerate(bits):
        near0, near1 = add([both0, both1], after=done)
        take(both0, flip(near0, "dp", bit))
        if at + 1 < len(bits):
            take(both1, flip(near1, "dp", bits[at + 1]))
        done = ()
    mine1, other1 = gather(near1)
    (near0,) = add([both0])
    mine0, other0 = gather(near0)
    grads = call(
        functools.partial(output_kernel, factor, [one.rows for one in both0]),
        (mine0, other0, mine1, other1),
        [far((2, w.shape[1] // shards, width), F32) for w in weights],
        smem=(me,),
    )
    return (
        gh.reshape(samples, nodes, width),
        ge.reshape(samples, nodes, slots, width),
        *grads,
    )


def solution(mesh):
    placed = (
        P("dp", "mesh", None),
        P("dp", "mesh", None, None),
        P("dp", "mesh", None),
        P("dp", "mesh", None, None),
        P(),
        P(),
        P(),
        P(),
        P("mesh", None),
        P("mesh", None),
        P("mesh"),
        P("mesh"),
    )
    return jax.shard_map(
        body,
        mesh=mesh,
        in_specs=placed,
        out_specs=(
            P("dp", "mesh", None),
            P("dp", "mesh", None, None),
            P(None, "dp", None),
            P(None, "dp", None),
            P(None, "dp", None),
            P(None, "dp", None),
        ),
        check_vma=False,
    )
```

```python
import functools

import jax
import jax.numpy as jnp
from jax import lax
from jax.experimental import pallas as pl
from jax.experimental.pallas import tpu as pltpu
from jax.sharding import PartitionSpec as P

F32 = jnp.float32
BF16 = jnp.bfloat16
VMEM = pltpu.VMEM
EPS = 1e-05
MIB = 1024 * 1024
LIMIT = 20 * MIB


def in_hbm(array):
    return pltpu.with_memory_space_constraint(array, pltpu.HBM)


class Part:
    def __init__(self, array, index=(), shape=None, pin=True):
        self.array, self.index = (in_hbm(array) if pin else array), index
        self.shape = tuple(array.shape if shape is None else shape)


def rows_of(weight, layer, start=0, stop=None):
    stop = weight.shape[1] if stop is None else stop
    return Part(weight, (layer, pl.ds(start, stop - start)), (stop - start, weight.shape[2]))


class Arriving:
    def __init__(self, copy, ref):
        self.copy, self.ref, self.shape, self.dtype = copy, ref, ref.shape, ref.dtype

    def __getitem__(self, index):
        if self.copy is not None:
            self.copy.wait()
            self.copy = None
        return self.ref[index]


class Leaving:
    def __init__(self, copy, ref):
        self.copy, self.ref, self.shape, self.dtype = copy, ref, ref.shape, ref.dtype
        self.started = False

    def __getitem__(self, index):
        return self.ref[index]

    def __setitem__(self, index, value):
        self.ref[index] = value

    def flush(self):
        if not self.started:
            self.copy.start()
            self.started = True


def far(shape, dtype):
    return (shape, dtype, True)


def call(kernel, operands, outs, scratch=(), smem=(), after=(), fetch=(), limit=LIMIT):
    shapes = [jax.ShapeDtypeStruct(out[0], out[1]) for out in outs]
    is_far = [len(out) > 2 for out in outs] + [False] * len(fetch)
    results = len(shapes)
    shapes += [jax.ShapeDtypeStruct(p.shape, p.array.dtype) for p in fetch]
    remote = [isinstance(p, Part) for p in operands]
    arrays = [p.array if r else p for p, r in zip(operands, remote)]
    buffers = [VMEM(p.shape, p.array.dtype) for p, r in zip(operands, remote) if r]
    buffers += [VMEM(s.shape, s.dtype) for s, r in zip(shapes, is_far) if r]
    copies = len(buffers) + len(fetch)
    sems = [pltpu.SemaphoreType.DMA((max(copies, 1),))]

    def run(*refs):
        refs = list(refs)

        def cut(count):
            taken = refs[:count]
            del refs[:count]
            return taken

        scalars, sources, origins = cut(len(smem)), cut(len(arrays)), cut(len(fetch))
        cut(len(after))
        targets, held, (sem,) = cut(len(shapes)), cut(len(buffers)), cut(1)
        sems = [sem.at[at] for at in range(copies)]
        ins, leaving, fetched = [], [], []
        for part, source, r in zip(operands, sources, remote):
            if r:
                view = source.at[part.index] if part.index else source
                ref = held.pop(0)
                copy = pltpu.make_async_copy(view, ref, sems.pop(0))
                copy.start()
                source = Arriving(copy, ref)
            ins.append(source)
        for part, origin, target in zip(fetch, origins, targets[results:]):
            view = origin.at[part.index] if part.index else origin
            copy = pltpu.make_async_copy(view, target, sems.pop(0))
            copy.start()
            fetched.append(copy)
        results_here = []
        for target, r in zip(targets[:results], is_far):
            if r:
                ref = held.pop(0)
                target = Leaving(pltpu.make_async_copy(ref, target, sems.pop(0)), ref)
                leaving.append(target)
            results_here.append(target)
        kernel(*scalars, *ins, *results_here, *refs)
        for ref in ins:
            if isinstance(ref, Arriving):
                ref[:1]
        for ref in leaving:
            ref.flush()
        for copy in fetched:
            copy.wait()
        for ref in leaving:
            ref.copy.wait()

    def space(r):
        return pl.BlockSpec(memory_space=pl.ANY if r else VMEM)

    return pl.pallas_call(
        run,
        in_specs=[pl.BlockSpec(memory_space=pltpu.SMEM)] * len(smem)
        + [space(r) for r in remote]
        + [space(True)] * len(fetch)
        + [pl.BlockSpec(memory_space=pl.ANY)] * len(after),
        out_specs=tuple(space(r) for r in is_far),
        out_shape=tuple((pltpu.HBM if r else VMEM)(s.shape, s.dtype) for s, r in zip(shapes, is_far)),
        scratch_shapes=buffers + sems + list(scratch),
        compiler_params=pltpu.CompilerParams(vmem_limit_bytes=limit),
        cost_estimate=pl.CostEstimate(flops=0, bytes_accessed=0, transcendentals=0),
    )(*smem, *arrays, *[p.array for p in fetch], *after)


def flush(*refs):
    for ref in refs:
        if isinstance(ref, Leaving):
            ref.flush()


def dot(a, b):
    return jnp.dot(a, b, preferred_element_type=F32)


def dot_nt(a, b):
    return lax.dot_general(a, b, (((1,), (1,)), ((), ())), preferred_element_type=F32)


def dot_tn(a, b):
    return lax.dot_general(a, b, (((0,), (0,)), ((), ())), preferred_element_type=F32)


def silu_and_slope(values):
    sigmoid = 0.5 * jnp.tanh(0.5 * values) + 0.5
    act = values * sigmoid
    return act, sigmoid + act * (1.0 - sigmoid)


def norm_parts(values):
    center = jnp.mean(values, axis=-1, keepdims=True)
    shifted = values - center
    inverse = lax.rsqrt(jnp.mean(shifted * shifted, axis=-1, keepdims=True) + EPS)
    return shifted * inverse, inverse


def norm_back(normed, inverse, upstream):
    return inverse * (
        upstream
        - jnp.mean(upstream, axis=-1, keepdims=True)
        - normed * jnp.mean(upstream * normed, axis=-1, keepdims=True)
    )


def halves(values):
    high = values.astype(BF16)
    low = (values - high.astype(F32)).astype(BF16)
    return jnp.concatenate([high, low], axis=0)


def node_of_edge(rows, nodes, slots):
    edge = lax.broadcasted_iota(jnp.int32, (rows, nodes), 0)
    node = lax.broadcasted_iota(jnp.int32, (rows, nodes), 1)
    return (edge // slots) == node


def pick_rows(send_ref, nodes):
    row = lax.broadcasted_iota(jnp.int32, (nodes, send_ref.shape[1]), 0)
    return (row == send_ref[...]).astype(F32).astype(BF16)


def pack_kernel(send_ref, h_ref, packed_ref):
    pick = pick_rows(send_ref, h_ref.shape[0])
    packed_ref[...] = dot_tn(pick, h_ref[...]).astype(BF16)


def prepare_kernel(
    table, chunk, nb_ref, count_ref, ocean_ref, h_ref, e_ref, we_ref, wr_ref,
    spread_ref, mask_ref, live_ref, wet_ref, pre_ref,
):
    slots, nodes = nb_ref.shape
    rows = nodes * slots
    owner = node_of_edge(rows, nodes, slots).astype(F32)
    owner16 = owner.astype(BF16)
    listed = dot_nt(owner16, nb_ref[...].astype(F32).astype(BF16))
    slot_here = lax.broadcasted_iota(jnp.int32, (rows, slots), 0) % slots
    slot_at = lax.broadcasted_iota(jnp.int32, (rows, slots), 1)
    source = jnp.sum(jnp.where(slot_here == slot_at, listed, 0.0), axis=1, keepdims=True)
    half = (table - nodes) // 2
    moved = jnp.where(source >= nodes + half, source - half, source + half)
    source = jnp.where(source >= nodes, moved, source)
    at = lax.broadcasted_iota(jnp.int32, (rows, table), 1).astype(F32)
    spread_ref[:, :table] = jnp.where(at == source, 1.0, 0.0).astype(BF16)
    spread_ref[:, table:] = owner16
    slot_of_row = lax.broadcasted_iota(jnp.int32, (rows, nodes), 0) % slots
    mask = jnp.where(slot_of_row < count_ref[...], owner, 0.0)
    mask_ref[...] = mask.astype(BF16)
    live_ref[...] = jnp.sum(mask, axis=1, keepdims=True)
    row = lax.broadcasted_iota(jnp.int32, (nodes, nodes), 0)
    column = lax.broadcasted_iota(jnp.int32, (nodes, nodes), 1)
    wet = jnp.where(row == column, ocean_ref[...].astype(F32), 0.0)
    wet_ref[...] = jnp.sum(wet, axis=1, keepdims=True)
    partial_kernel(chunk, h_ref, spread_ref, e_ref, we_ref, wr_ref, pre_ref)


def partial_kernel(chunk, h_ref, spread_ref, e_ref, we_ref, wr_ref, pre_ref):
    rows, width = e_ref.shape
    known = spread_ref.shape[1] - h_ref.shape[0]
    h = h_ref[...]
    for start in range(0, rows, chunk):
        at = pl.ds(start, chunk)
        own = dot(spread_ref[at, known:], h).astype(BF16)
        pre = dot(e_ref[at, :], we_ref[...])
        pre_ref[at, :] = pre + dot(own, wr_ref[...])


def forward_edges(chunk, pre_ref, e_ref, table, spread_ref, live_ref, ws_ref, wo_ref, put):
    rows, width = e_ref.shape
    known = table.shape[0]
    for start in range(0, rows, chunk):
        at = pl.ds(start, chunk)
        src = dot(spread_ref[at, :known], table).astype(BF16)
        pre = pre_ref[at, :] + dot(src, ws_ref[...])
        act, slope = silu_and_slope(pre)
        act = act.astype(BF16)
        normed, inverse = norm_parts(dot(act, wo_ref[...]))
        new_e = (e_ref[at, :].astype(F32) + live_ref[at, :] * normed).astype(BF16)
        put(at, act, slope, normed, inverse, new_e)


def forward_nodes(h, message, wi_ref, wo_ref):
    width = h.shape[1]
    pre = dot(h, wi_ref[:width, :]) + dot(message, wi_ref[width:, :])
    act, slope = silu_and_slope(pre)
    act = act.astype(BF16)
    normed, inverse = norm_parts(dot(act, wo_ref[...]))
    return act, slope, normed, inverse


def first_forward_kernel(
    chunk, pre_ref, e_ref, h_ref, halo_ref, spread_ref, mask_ref, live_ref, wet_ref, send_ref,
    ws_ref, weo_ref, wni_ref, wno_ref,
    act_ref, slope_ref, normed_ref, inverse_ref, new_e_ref,
    new_h_ref, message_ref, act_n_ref, slope_n_ref, normed_n_ref, inverse_n_ref, packed_ref,
):
    h = h_ref[...]
    table = jnp.concatenate([h, halo_ref[...]], axis=0)

    def put(at, act, slope, normed, inverse, new_e):
        act_ref[at, :] = act
        slope_ref[at, :] = slope.astype(BF16)
        normed_ref[at, :] = normed.astype(BF16)
        inverse_ref[at, :] = inverse
        new_e_ref[at, :] = new_e

    forward_edges(chunk, pre_ref, e_ref, table, spread_ref, live_ref, ws_ref, weo_ref, put)
    flush(act_ref, slope_ref, normed_ref, inverse_ref, new_e_ref)
    message = dot_tn(mask_ref[...], new_e_ref[...]).astype(BF16)
    act, slope, normed, inverse = forward_nodes(h, message, wni_ref, wno_ref)
    message_ref[...] = message
    act_n_ref[...] = act
    slope_n_ref[...] = slope.astype(BF16)
    normed_n_ref[...] = normed.astype(BF16)
    inverse_n_ref[...] = inverse
    flush(message_ref, act_n_ref, slope_n_ref, normed_n_ref, inverse_n_ref)
    new_h = (h.astype(F32) + wet_ref[...] * normed).astype(BF16)
    new_h_ref[...] = new_h
    packed_ref[...] = dot_tn(pick_rows(send_ref, h.shape[0]), new_h).astype(BF16)


def backward_nodes(gh, slope, normed, inverse, wet_ref, wi_ref, wo_ref, gout_ref, gpre_ref):
    gout = norm_back(normed, inverse, wet_ref[...] * gh).astype(BF16)
    gpre = (dot_nt(gout, wo_ref[...]) * slope).astype(BF16)
    gout_ref[...] = gout
    gpre_ref[...] = gpre
    ginput = dot_nt(gpre, wi_ref[...])
    width = gh.shape[1]
    return gh + ginput[:, :width], ginput[:, width:]


def backward_edges(
    chunk, known, gh, gmsg, ge_ref, spread_ref, live_ref, slope_ref, normed_ref, inverse_ref,
    we_ref, wr_ref, wo_ref, gh_out_ref, more_ref, own_ref, halo_out_ref, ge_out_ref, gedge_ref, gpe_ref, sums_ref,
):
    rows, width = ge_ref.shape
    nodes = gh.shape[0]
    gh_out_ref[...] = gh
    gmsg = halves(gmsg)
    for start in range(0, rows, chunk):
        at = pl.ds(start, chunk)
        live = live_ref[at, :]
        owner = spread_ref[at, known:]
        sent = dot(jnp.concatenate([owner, owner], axis=1), gmsg)
        ge = ge_ref[at, :].astype(F32) + live * sent
        gedge = norm_back(normed_ref[at, :].astype(F32), inverse_ref[at, :], live * ge)
        gedge = gedge.astype(BF16)
        gpe = (dot_nt(gedge, wo_ref[...]) * slope_ref[at, :].astype(F32)).astype(BF16)
        gedge_ref[at, :] = gedge
        gpe_ref[at, :] = gpe
        ge = ge + dot_nt(gpe, we_ref[...])
        ge_out_ref[at, :] = ge.astype(ge_out_ref.dtype)
    flush(gedge_ref, gpe_ref, ge_out_ref)
    gathered = dot_tn(spread_ref[...], gpe_ref[...])
    own_ref[...] = gathered[:nodes]
    halo_out_ref[...] = gathered[nodes:known].astype(BF16)
    sums_ref[...] = gathered.astype(BF16)
    both = dot_nt(halves(gathered[known:]), wr_ref[...])
    more_ref[...] = both[:nodes] + both[nodes:]


def middle_kernel(
    chunk, pre_ref, e_ref, h_ref, halo_ref, spread_ref, mask_ref, live_ref, wet_ref,
    gh_ref, ge_ref, ws_ref, weo_ref, wni_ref, wno_ref, we_ref, wr_ref,
    act_ref, message_ref, act_n_ref, gout_ref, gpre_ref,
    gh_out_ref, more_ref, own_ref, halo_out_ref, ge_out_ref, gedge_ref, gpe_ref, sums_ref,
    slope_ref, normed_ref, inverse_ref, new_e_ref,
):
    h = h_ref[...]
    table = jnp.concatenate([h, halo_ref[...]], axis=0)

    def put(at, act, slope, normed, inverse, new_e):
        act_ref[at, :] = act
        slope_ref[at, :] = slope.astype(BF16)
        normed_ref[at, :] = normed.astype(BF16)
        inverse_ref[at, :] = inverse
        new_e_ref[at, :] = new_e

    forward_edges(chunk, pre_ref, e_ref, table, spread_ref, live_ref, ws_ref, weo_ref, put)
    message = dot_tn(mask_ref[...], new_e_ref[...]).astype(BF16)
    act, slope, normed, inverse = forward_nodes(h, message, wni_ref, wno_ref)
    message_ref[...] = message
    act_n_ref[...] = act
    flush(act_ref)
    gh, gmsg = backward_nodes(
        gh_ref[...].astype(F32), slope, normed, inverse, wet_ref, wni_ref, wno_ref, gout_ref, gpre_ref
    )
    backward_edges(
        chunk, table.shape[0], gh, gmsg, ge_ref, spread_ref, live_ref, slope_ref, normed_ref,
        inverse_ref, we_ref, wr_ref, weo_ref, gh_out_ref, more_ref, own_ref, halo_out_ref, ge_out_ref,
        gedge_ref, gpe_ref, sums_ref,
    )


def return_halo(gh_ref, more_ref, own_ref, back_ref, send_ref, wei_ref):
    nodes, width = gh_ref.shape
    total = own_ref[...] + dot(pick_rows(send_ref, nodes), back_ref[...])
    both = dot_nt(halves(total), wei_ref[...])
    return gh_ref[...] + more_ref[...] + both[:nodes] + both[nodes:]


def first_backward_kernel(
    chunk, gh_ref, more_ref, own_ref, back_ref, send_ref, slope_n_ref, normed_n_ref, inverse_n_ref, wet_ref,
    ge_ref, spread_ref, live_ref, slope_ref, normed_ref, inverse_ref,
    ws_ref, wno_ref, wni_ref, weo_ref, we_ref, wr_ref,
    gout_ref, gpre_ref, gh_out_ref, more_out_ref, own_out_ref, halo_out_ref, ge_out_ref,
    gedge_ref, gpe_ref, sums_ref,
):
    gh = return_halo(gh_ref, more_ref, own_ref, back_ref, send_ref, ws_ref)
    gh, gmsg = backward_nodes(
        gh, slope_n_ref[...].astype(F32), normed_n_ref[...].astype(F32), inverse_n_ref[...],
        wet_ref, wni_ref, wno_ref, gout_ref, gpre_ref,
    )
    known = spread_ref.shape[1] - gh.shape[0]
    backward_edges(
        chunk, known, gh, gmsg, ge_ref, spread_ref, live_ref, slope_ref, normed_ref,
        inverse_ref, we_ref, wr_ref, weo_ref, gh_out_ref, more_out_ref, own_out_ref, halo_out_ref, ge_out_ref,
        gedge_ref, gpe_ref, sums_ref,
    )


def last_kernel(gh_ref, more_ref, own_ref, back_ref, send_ref, wei_ref, out_ref):
    out_ref[...] = return_halo(gh_ref, more_ref, own_ref, back_ref, send_ref, wei_ref)


def place(order, me_ref, first_ref, second_ref, keep_ref, sent_ref):
    rows = keep_ref.shape[1]
    blocks = sorted({bits for bits, _ in order})
    sides = len(order) // len(blocks)
    for bits in blocks:
        spots = [order.index((bits, side)) for side in range(sides)]

        def spot(half):
            return jnp.where(me_ref[1] == half, spots[0], spots[1]) if sides == 2 else spots[0]

        for bit, out_ref in ((0, keep_ref), (1, sent_ref)):
            device = jnp.bitwise_xor(me_ref[0], bits + bit)
            row = 0
            for ref in (first_ref, second_ref):
                size = ref.shape[0] // (2 * len(blocks))
                start = pl.multiple_of(device * size, 16)
                done = 0
                while done < size:
                    half, at = divmod(row, rows)
                    step = min(size - done, rows - at)
                    piece = ref[pl.ds(pl.multiple_of(start + done, 16), step), :]
                    out_ref[spot(half), at : at + step, :] = piece.astype(BF16)
                    row += step
                    done += step
            if row < sides * rows:
                filler = jnp.zeros((sides * rows - row, keep_ref.shape[2]), BF16)
                out_ref[spot(sides - 1), row - (sides - 1) * rows :, :] = filler


def edge_weights_kernel(
    layout, me_ref, e_ref, h_ref, halo_ref, act_ref, gedge_ref, gpe_ref, sums_ref,
    keep_ref, sent_ref, grad_in_ref, grad_out_ref,
):
    width = e_ref.shape[1]
    h = h_ref[...]
    known = h.shape[0] + halo_ref.shape[0]
    table = jnp.concatenate([h, halo_ref[...]], axis=0)
    grad_in_ref[:width, :] = dot_tn(e_ref[...], gpe_ref[...])
    grad_in_ref[width : 2 * width, :] = dot_tn(table, sums_ref[:known, :])
    grad_in_ref[2 * width :, :] = dot_tn(h, sums_ref[known:, :])
    grad_out_ref[...] = dot_tn(act_ref[...], gedge_ref[...])
    place(layout, me_ref, grad_in_ref, grad_out_ref, keep_ref, sent_ref)


def node_weights_kernel(
    layout, me_ref, h_ref, message_ref, act_ref, gout_ref, gpre_ref,
    keep_ref, sent_ref, grad_in_ref, grad_out_ref,
):
    width = h_ref.shape[1]
    gpre = gpre_ref[...]
    grad_in_ref[:width, :] = dot_tn(h_ref[...], gpre)
    grad_in_ref[width:, :] = dot_tn(message_ref[...], gpre)
    grad_out_ref[...] = dot_tn(act_ref[...], gout_ref[...])
    place(layout, me_ref, grad_in_ref, grad_out_ref, keep_ref, sent_ref)


def trade(rows, back=False):
    count = lax.axis_size("mesh")
    if count == 2:
        return lax.ppermute(rows, "mesh", [(0, 1), (1, 0)])
    half = rows.shape[0] // 2
    up = [(i, (i + 1) % count) for i in range(count)]
    down = [(j, i) for i, j in up]
    first, second = (up, down) if back else (down, up)
    return jnp.concatenate(
        [lax.ppermute(rows[:half], "mesh", first), lax.ppermute(rows[half:], "mesh", second)], axis=0
    )


def flip(values, axis, bit):
    return lax.ppermute(values, axis, [(i, i ^ bit) for i in range(lax.axis_size(axis))])


def bits_of(axis):
    size = lax.axis_size(axis)
    return [1 << i for i in range(size.bit_length() - 1)]


def slot_order(route):
    order = [(0, 0)]
    for axis, bit in reversed(route):
        if axis == "dp":
            order = order + [(bits + bit, side) for bits, side in order]
        else:
            order = order + [(bits, 1) for bits, side in order]
    return order


class Sum:
    def __init__(self, keep, route):
        self.base, self.arrived, self.row = Part(keep), None, 0
        self.slots, self.rows, self.width = keep.shape
        self.route = list(route)


def add_kernel(groups, tail, *refs):
    refs = list(refs)
    flat = [group for output in groups for group in output]
    terms, refs = refs[: 2 * len(flat)], refs[2 * len(flat) :]
    if tail:
        more, refs = refs[0], refs[1:]
    outs, kept = refs[: len(groups)], refs[len(groups) :]
    if tail:
        outs[-1][outs[-1].shape[0] - 1, : more.shape[0], :] = more[...]
    for output, out in zip(groups, outs):
        at = 0
        for rows, row, slots in output:
            base, arrived, terms = terms[0], terms[1], terms[2:]
            half = slots // 2
            low, high = (0, 1) if slots == 1 else (half, slots)
            total = base[low:high].astype(F32) + arrived[low:high, row : row + rows, :].astype(F32)
            out[: high - low, at : at + rows, :] = total.astype(BF16)
            at += rows
            if half:
                left, kept = kept[0], kept[1:]
                left[...] = base[:half].astype(F32) + arrived[:half, row : row + rows, :].astype(F32)


def add(wanted, after=(), tail=None):
    operands, groups, outs, kept = [], [], [], []
    for sums in wanted:
        group = []
        for one in sums:
            operands += [one.base, one.arrived]
            group.append((one.rows, one.row, one.slots))
            half = one.slots // 2
            if half:
                kept.append((one, ((half, one.rows, one.width), F32)))
        groups.append(group)
        outs.append(((max(half, 1), sum(one.rows for one in sums), one.width), BF16))
    if tail is not None:
        (count, size, width), dtype = outs[-1]
        outs[-1] = ((count + 1, size, width), dtype)
        operands.append(tail)
    results = call(
        functools.partial(add_kernel, groups, tail is not None),
        operands,
        outs + [shape for _, shape in kept],
        after=after,
    )
    for (one, _), base in zip(kept, results[len(outs) :]):
        one.base = base
        one.slots //= 2
    return results[: len(outs)]


def advance(wanted, after=(), tail=None):
    sent = add(wanted, after, tail)
    arrived = []
    for sums, values in zip(wanted, sent):
        steps = [one.route.pop(0) for one in sums if one.route]
        if not steps:
            arrived.append(None)
            continue
        other = flip(values, *steps[0])
        row = 0
        for one in sums:
            one.arrived, one.row = other, row
            row += one.rows
        arrived.append(other)
    return sent, arrived


def across(values):
    mine = values[0]
    for bit in bits_of("mesh")[1:]:
        mine = (mine.astype(F32) + flip(mine, "mesh", bit).astype(F32)).astype(BF16)
    return mine, flip(mine, "mesh", 1)


def output_kernel(
    factor, halves_of, me_ref, mine0_ref, other0_ref, mine1_ref, other1_ref, *outs
):
    low = me_ref[1] == 0
    row0 = row1 = 0
    for pair, rows in enumerate(halves_of):
        first, second = outs[2 * pair], outs[2 * pair + 1]
        cut, end = first.shape[1], first.shape[1] + second.shape[1]
        a = mine0_ref[row0 : row0 + rows, :].astype(F32) * factor
        b = other0_ref[row0 : row0 + rows, :].astype(F32) * factor
        both = jnp.concatenate([jnp.where(low, a, b), jnp.where(low, b, a)], axis=0)
        first[0] = both[:cut]
        second[0] = both[cut:end]
        a = mine1_ref[row1 : row1 + end, :].astype(F32)
        both = (a + other1_ref[row1 : row1 + end, :].astype(F32)) * factor
        first[1] = both[:cut]
        second[1] = both[cut:end]
        row0 += rows
        row1 += end


def body(
    node_feats,
    edge_feats,
    node_cot,
    edge_cot,
    w_edge_in,
    w_edge_out,
    w_node_in,
    w_node_out,
    neighbours,
    send_rows,
    edge_counts,
    ocean_mask,
):
    samples, nodes, width = node_feats.shape
    slots = neighbours.shape[1]
    rows = nodes * slots
    sent = send_rows.shape[1]
    known = nodes + sent
    chunk = rows // 2
    shards = lax.axis_size("dp")
    total_rows = samples * shards * nodes * lax.axis_size("mesh")
    factor = 1.0 / total_rows**0.5
    beyond = [("dp", bit) for bit in bits_of("dp")[2:]]
    along = [("dp", 2)]
    edge_routes = (along + [("mesh", 1)] + beyond, along + beyond)
    node_routes = ([("mesh", 1)] + along + beyond, beyond + along)
    me = jnp.stack([lax.axis_index("dp"), lax.axis_index("mesh") % 2]).astype(jnp.int32)

    h0 = node_feats.reshape(nodes, width)
    e0 = edge_feats.reshape(rows, width)
    gh = node_cot.reshape(nodes, width)
    ge = edge_cot.reshape(rows, width)
    weights = (w_edge_in, w_edge_out, w_node_in, w_node_out)
    small, large, thin = (nodes, width), (rows, width), (sent, width)
    source = [rows_of(w_edge_in, layer, width, 2 * width) for layer in range(2)]
    edge = [rows_of(w_edge_in, layer, 0, width) for layer in range(2)]
    receiver = [rows_of(w_edge_in, layer, 2 * width) for layer in range(2)]
    edge_out = [rows_of(w_edge_out, layer) for layer in range(2)]
    node_in = [rows_of(w_node_in, layer) for layer in range(2)]
    node_out = [rows_of(w_node_out, layer) for layer in range(2)]

    (packed0,) = call(pack_kernel, (Part(send_rows), Part(h0)), [(thin, BF16)])
    halo0 = trade(packed0)
    spread, mask, live, wet, pre0, h0_near, e0_near, source0, edge_out0, node_in0, node_out0 = call(
        functools.partial(prepare_kernel, known, chunk),
        (Part(neighbours.T), Part(edge_counts.reshape(1, nodes)), Part(ocean_mask.reshape(1, nodes)))
        + (Part(h0), Part(e0), edge[0], receiver[0]),
        [
            ((rows, known + nodes), BF16), ((rows, nodes), BF16), ((rows, 1), F32),
            ((nodes, 1), F32), (large, F32),
        ],
        fetch=(Part(h0), Part(e0), source[0], edge_out[0], node_in[0], node_out[0]),
    )
    (
        act0, slope0, normed0, inverse0, e1,
        h1, message0, act_n0, slope_n0, normed_n0, inverse_n0, packed1,
        edge1_w, receiver1_w, source1_w,
    ) = call(
        functools.partial(first_forward_kernel, chunk),
        (pre0, e0_near, h0_near, halo0, spread, mask, live, wet, send_rows)
        + (source0, edge_out0, node_in0, node_out0),
        [far(large, BF16)] * 3 + [far((rows, 1), F32), (large, BF16), (small, BF16)]
        + [far(small, BF16)] * 4 + [far((nodes, 1), F32), (thin, BF16)],
        fetch=(edge[1], receiver[1], source[1]),
    )
    halo1 = trade(packed1)
    pre1, edge_out1, node_in1, node_out1, gh_near, ge_near = call(
        functools.partial(partial_kernel, chunk),
        (h1, spread, e1, edge1_w, receiver1_w),
        [(large, F32)],
        fetch=(edge_out[1], node_in[1], node_out[1], Part(gh), Part(ge)),
    )
    backward_outs = [(small, F32)] * 3 + [(thin, BF16)]
    backward_tail = [(large, BF16)] * 2 + [((known + nodes, width), BF16)]
    act1, message1, act_n1, gout1, gpre1, gh, more, own, halo_out, ge, gedge1, gpe1, sums1, *near_w = call(
        functools.partial(middle_kernel, chunk),
        (pre1, e1, h1, halo1, spread, mask, live, wet, gh_near, ge_near)
        + (source1_w, edge_out1, node_in1, node_out1, edge1_w, receiver1_w),
        [(large, BF16)] + [(small, BF16)] * 4 + backward_outs + [far(large, F32)] + backward_tail,
        scratch=[VMEM(large, BF16)] * 2 + [VMEM((rows, 1), F32), VMEM(large, BF16)],
        fetch=(node_out[0], node_in[0], edge_out[0], edge[0], receiver[0]),
    )
    back = trade(halo_out, back=True)

    def weight_sum(kernel, route, operands, kinds, **more):
        order = slot_order(route)
        size = sum(w.shape[1] // shards for w in kinds)
        rows_in = size if ("mesh", 1) not in route else -(-size // 32) * 16
        shape = (len(order), rows_in, width)
        keep, send, *fetched = call(
            functools.partial(kernel, order),
            operands,
            [far(shape, BF16), (shape, BF16)],
            scratch=[VMEM(w.shape[1:], F32) for w in kinds],
            smem=(me,),
            **more,
        )
        one = Sum(keep, route)
        one.arrived = flip(send, "dp", 1)
        return one, fetched

    def edge_sum(layer, operands, **more):
        return weight_sum(
            edge_weights_kernel, edge_routes[layer], operands, (w_edge_in, w_edge_out), **more
        )

    def node_sum(layer, operands, **more):
        return weight_sum(
            node_weights_kernel, node_routes[layer], operands, (w_node_in, w_node_out), **more
        )

    needed = (Part(slope_n0), Part(normed_n0), Part(inverse_n0), Part(slope0), Part(normed0))
    edge1, _ = edge_sum(1, (e1, h1, halo1, act1, gedge1, gpe1, sums1))
    node1, near = node_sum(
        1, (h1, message1, act_n1, gout1, gpre1), fetch=needed + (Part(inverse0), Part(ge))
    )
    first, arrived = advance([[edge1], [node1]])
    gout0, gpre0, gh, more, own, halo_out, ge, gedge0, gpe0, sums0, e0_near, act0, h0_near = call(
        functools.partial(first_backward_kernel, chunk),
        (gh, more, own, back, send_rows, near[0], near[1], near[2], wet)
        + (near[6], spread, live, near[3], near[4], near[5], source1_w, *near_w),
        [(small, BF16)] * 2 + backward_outs + [far(large, BF16)] + backward_tail,
        after=tuple(first),
        fetch=(Part(e0), Part(act0), Part(h0)),
    )
    edge0, _ = edge_sum(0, (e0_near, h0_near, halo0, act0, gedge0, gpe0, sums0))
    node0, _ = node_sum(
        0, (h0_near, Part(message0), Part(act_n0), gout0, gpre0), after=tuple(arrived)
    )
    joint = lax.axis_size("mesh") == 2 and sent <= node0.rows
    wanted = [[edge0], [edge1], [node1], [node0]]
    _, arrived = advance(wanted, tail=halo_out if joint else None)
    if joint:
        back = Part(arrived[-1], (arrived[-1].shape[0] - 1, pl.ds(0, sent)), thin, pin=False)
    else:
        back = trade(halo_out, back=True)
    out, _ = advance(wanted)
    (gh,) = call(
        last_kernel, (gh, more, own, back, send_rows, source[0]), [far(small, F32)], after=(out[0],)
    )
    done = (gh,)
    while edge1.route:
        advance([[edge0, node0], [edge1], [node1]], after=done)
        done = ()
    (_, value1), _ = advance([[edge0, node0], [edge1, node1]], after=done)
    mine1, other1 = across(value1)
    while edge0.route:
        advance([[edge0, node0]])
    ((value0,), _) = advance([[edge0, node0]])
    mine0, other0 = across(value0)
    grads = call(
        functools.partial(output_kernel, factor, (edge0.rows, node0.rows)),
        (mine0, other0, mine1, other1),
        [far((2, w.shape[1] // shards, width), F32) for w in weights],
        smem=(me,),
    )
    return (
        gh.reshape(samples, nodes, width),
        ge.reshape(samples, nodes, slots, width),
        *grads,
    )


def solution(mesh):
    placed = (
        P("dp", "mesh", None),
        P("dp", "mesh", None, None),
        P("dp", "mesh", None),
        P("dp", "mesh", None, None),
        P(),
        P(),
        P(),
        P(),
        P("mesh", None),
        P("mesh", None),
        P("mesh"),
        P("mesh"),
    )
    return jax.shard_map(
        body,
        mesh=mesh,
        in_specs=placed,
        out_specs=(
            P("dp", "mesh", None),
            P("dp", "mesh", None, None),
            P(None, "dp", None),
            P(None, "dp", None),
            P(None, "dp", None),
            P(None, "dp", None),
        ),
        check_vma=False,
    )
```

```python
import functools

import jax
import jax.numpy as jnp
from jax import lax
from jax.experimental import pallas as pl
from jax.experimental.pallas import tpu as pltpu
from jax.sharding import PartitionSpec as P

F32 = jnp.float32
BF16 = jnp.bfloat16
VMEM = pltpu.VMEM
EPS = 1e-05
MIB = 1024 * 1024
LIMIT = 20 * MIB


def in_hbm(array):
    return pltpu.with_memory_space_constraint(array, pltpu.HBM)


class Part:
    def __init__(self, array, index=(), shape=None, pin=True):
        self.array, self.index = (in_hbm(array) if pin else array), index
        self.shape = tuple(array.shape if shape is None else shape)


def rows_of(weight, layer, start=0, stop=None):
    stop = weight.shape[1] if stop is None else stop
    return Part(weight, (layer, pl.ds(start, stop - start)), (stop - start, weight.shape[2]))


class Arriving:
    def __init__(self, copy, ref):
        self.copy, self.ref, self.shape, self.dtype = copy, ref, ref.shape, ref.dtype

    def __getitem__(self, index):
        if self.copy is not None:
            self.copy.wait()
            self.copy = None
        return self.ref[index]


class Leaving:
    def __init__(self, copy, ref):
        self.copy, self.ref, self.shape, self.dtype = copy, ref, ref.shape, ref.dtype
        self.started = False

    def __getitem__(self, index):
        return self.ref[index]

    def __setitem__(self, index, value):
        self.ref[index] = value

    def flush(self):
        if not self.started:
            self.copy.start()
            self.started = True


def far(shape, dtype):
    return (shape, dtype, True)


def call(kernel, operands, outs, scratch=(), smem=(), after=(), fetch=(), limit=LIMIT):
    shapes = [jax.ShapeDtypeStruct(out[0], out[1]) for out in outs]
    is_far = [len(out) > 2 for out in outs] + [False] * len(fetch)
    results = len(shapes)
    shapes += [jax.ShapeDtypeStruct(p.shape, p.array.dtype) for p in fetch]
    remote = [isinstance(p, Part) for p in operands]
    arrays = [p.array if r else p for p, r in zip(operands, remote)]
    buffers = [VMEM(p.shape, p.array.dtype) for p, r in zip(operands, remote) if r]
    buffers += [VMEM(s.shape, s.dtype) for s, r in zip(shapes, is_far) if r]
    copies = len(buffers) + len(fetch)
    sems = [pltpu.SemaphoreType.DMA((max(copies, 1),))]

    def run(*refs):
        refs = list(refs)

        def cut(count):
            taken = refs[:count]
            del refs[:count]
            return taken

        scalars, sources, origins = cut(len(smem)), cut(len(arrays)), cut(len(fetch))
        cut(len(after))
        targets, held, (sem,) = cut(len(shapes)), cut(len(buffers)), cut(1)
        sems = [sem.at[at] for at in range(copies)]
        ins, leaving, fetched = [], [], []
        for part, source, r in zip(operands, sources, remote):
            if r:
                view = source.at[part.index] if part.index else source
                ref = held.pop(0)
                copy = pltpu.make_async_copy(view, ref, sems.pop(0))
                copy.start()
                source = Arriving(copy, ref)
            ins.append(source)
        for part, origin, target in zip(fetch, origins, targets[results:]):
            view = origin.at[part.index] if part.index else origin
            copy = pltpu.make_async_copy(view, target, sems.pop(0))
            copy.start()
            fetched.append(copy)
        results_here = []
        for target, r in zip(targets[:results], is_far):
            if r:
                ref = held.pop(0)
                target = Leaving(pltpu.make_async_copy(ref, target, sems.pop(0)), ref)
                leaving.append(target)
            results_here.append(target)
        kernel(*scalars, *ins, *results_here, *refs)
        for ref in ins:
            if isinstance(ref, Arriving):
                ref[:1]
        for ref in leaving:
            ref.flush()
        for copy in fetched:
            copy.wait()
        for ref in leaving:
            ref.copy.wait()

    def space(r):
        return pl.BlockSpec(memory_space=pl.ANY if r else VMEM)

    return pl.pallas_call(
        run,
        in_specs=[pl.BlockSpec(memory_space=pltpu.SMEM)] * len(smem)
        + [space(r) for r in remote]
        + [space(True)] * len(fetch)
        + [pl.BlockSpec(memory_space=pl.ANY)] * len(after),
        out_specs=tuple(space(r) for r in is_far),
        out_shape=tuple((pltpu.HBM if r else VMEM)(s.shape, s.dtype) for s, r in zip(shapes, is_far)),
        scratch_shapes=buffers + sems + list(scratch),
        compiler_params=pltpu.CompilerParams(vmem_limit_bytes=limit),
        cost_estimate=pl.CostEstimate(flops=0, bytes_accessed=0, transcendentals=0),
    )(*smem, *arrays, *[p.array for p in fetch], *after)


def flush(*refs):
    for ref in refs:
        if isinstance(ref, Leaving):
            ref.flush()


def dot(a, b):
    return jnp.dot(a, b, preferred_element_type=F32)


def dot_nt(a, b):
    return lax.dot_general(a, b, (((1,), (1,)), ((), ())), preferred_element_type=F32)


def dot_tn(a, b):
    return lax.dot_general(a, b, (((0,), (0,)), ((), ())), preferred_element_type=F32)


def silu_and_slope(values):
    sigmoid = 0.5 * jnp.tanh(0.5 * values) + 0.5
    act = values * sigmoid
    return act, sigmoid + act * (1.0 - sigmoid)


def norm_parts(values):
    center = jnp.mean(values, axis=-1, keepdims=True)
    shifted = values - center
    inverse = lax.rsqrt(jnp.mean(shifted * shifted, axis=-1, keepdims=True) + EPS)
    return shifted * inverse, inverse


def norm_back(normed, inverse, upstream):
    return inverse * (
        upstream
        - jnp.mean(upstream, axis=-1, keepdims=True)
        - normed * jnp.mean(upstream * normed, axis=-1, keepdims=True)
    )


def halves(values):
    high = values.astype(BF16)
    low = (values - high.astype(F32)).astype(BF16)
    return jnp.concatenate([high, low], axis=0)


def node_of_edge(rows, nodes, slots):
    edge = lax.broadcasted_iota(jnp.int32, (rows, nodes), 0)
    node = lax.broadcasted_iota(jnp.int32, (rows, nodes), 1)
    return (edge // slots) == node


def pick_rows(send_ref, nodes):
    row = lax.broadcasted_iota(jnp.int32, (nodes, send_ref.shape[1]), 0)
    return (row == send_ref[...]).astype(F32).astype(BF16)


def pack_kernel(send_ref, h_ref, packed_ref):
    pick = pick_rows(send_ref, h_ref.shape[0])
    packed_ref[...] = dot_tn(pick, h_ref[...]).astype(BF16)


def prepare_kernel(
    table, chunk, nb_ref, count_ref, ocean_ref, h_ref, e_ref, we_ref, wr_ref,
    spread_ref, mask_ref, live_ref, wet_ref, pre_ref,
):
    slots, nodes = nb_ref.shape
    rows = nodes * slots
    owner = node_of_edge(rows, nodes, slots).astype(F32)
    owner16 = owner.astype(BF16)
    listed = dot_nt(owner16, nb_ref[...].astype(F32).astype(BF16))
    slot_here = lax.broadcasted_iota(jnp.int32, (rows, slots), 0) % slots
    slot_at = lax.broadcasted_iota(jnp.int32, (rows, slots), 1)
    source = jnp.sum(jnp.where(slot_here == slot_at, listed, 0.0), axis=1, keepdims=True)
    half = (table - nodes) // 2
    moved = jnp.where(source >= nodes + half, source - half, source + half)
    source = jnp.where(source >= nodes, moved, source)
    at = lax.broadcasted_iota(jnp.int32, (rows, table), 1).astype(F32)
    spread_ref[:, :table] = jnp.where(at == source, 1.0, 0.0).astype(BF16)
    spread_ref[:, table:] = owner16
    slot_of_row = lax.broadcasted_iota(jnp.int32, (rows, nodes), 0) % slots
    mask = jnp.where(slot_of_row < count_ref[...], owner, 0.0)
    mask_ref[...] = mask.astype(BF16)
    live_ref[...] = jnp.sum(mask, axis=1, keepdims=True)
    row = lax.broadcasted_iota(jnp.int32, (nodes, nodes), 0)
    column = lax.broadcasted_iota(jnp.int32, (nodes, nodes), 1)
    wet = jnp.where(row == column, ocean_ref[...].astype(F32), 0.0)
    wet_ref[...] = jnp.sum(wet, axis=1, keepdims=True)
    partial_kernel(chunk, h_ref, spread_ref, e_ref, we_ref, wr_ref, pre_ref)


def partial_kernel(chunk, h_ref, spread_ref, e_ref, we_ref, wr_ref, pre_ref):
    rows, width = e_ref.shape
    known = spread_ref.shape[1] - h_ref.shape[0]
    h = h_ref[...]
    for start in range(0, rows, chunk):
        at = pl.ds(start, chunk)
        own = dot(spread_ref[at, known:], h).astype(BF16)
        pre = dot(e_ref[at, :], we_ref[...])
        pre_ref[at, :] = pre + dot(own, wr_ref[...])


def forward_edges(chunk, pre_ref, e_ref, table, spread_ref, live_ref, ws_ref, wo_ref, put):
    rows, width = e_ref.shape
    known = table.shape[0]
    for start in range(0, rows, chunk):
        at = pl.ds(start, chunk)
        src = dot(spread_ref[at, :known], table).astype(BF16)
        pre = pre_ref[at, :] + dot(src, ws_ref[...])
        act, slope = silu_and_slope(pre)
        act = act.astype(BF16)
        normed, inverse = norm_parts(dot(act, wo_ref[...]))
        new_e = (e_ref[at, :].astype(F32) + live_ref[at, :] * normed).astype(BF16)
        put(at, act, slope, normed, inverse, new_e)


def forward_nodes(h, message, wi_ref, wo_ref):
    width = h.shape[1]
    pre = dot(h, wi_ref[:width, :]) + dot(message, wi_ref[width:, :])
    act, slope = silu_and_slope(pre)
    act = act.astype(BF16)
    normed, inverse = norm_parts(dot(act, wo_ref[...]))
    return act, slope, normed, inverse


def first_forward_kernel(
    chunk, pre_ref, e_ref, h_ref, halo_ref, spread_ref, mask_ref, live_ref, wet_ref, send_ref,
    ws_ref, weo_ref, wni_ref, wno_ref,
    act_ref, slope_ref, normed_ref, inverse_ref, new_e_ref,
    new_h_ref, message_ref, act_n_ref, slope_n_ref, normed_n_ref, inverse_n_ref, packed_ref,
):
    h = h_ref[...]
    table = jnp.concatenate([h, halo_ref[...]], axis=0)

    def put(at, act, slope, normed, inverse, new_e):
        act_ref[at, :] = act
        slope_ref[at, :] = slope.astype(BF16)
        normed_ref[at, :] = normed.astype(BF16)
        inverse_ref[at, :] = inverse
        new_e_ref[at, :] = new_e

    forward_edges(chunk, pre_ref, e_ref, table, spread_ref, live_ref, ws_ref, weo_ref, put)
    flush(act_ref, slope_ref, normed_ref, inverse_ref, new_e_ref)
    message = dot_tn(mask_ref[...], new_e_ref[...]).astype(BF16)
    act, slope, normed, inverse = forward_nodes(h, message, wni_ref, wno_ref)
    message_ref[...] = message
    act_n_ref[...] = act
    slope_n_ref[...] = slope.astype(BF16)
    normed_n_ref[...] = normed.astype(BF16)
    inverse_n_ref[...] = inverse
    flush(message_ref, act_n_ref, slope_n_ref, normed_n_ref, inverse_n_ref)
    new_h = (h.astype(F32) + wet_ref[...] * normed).astype(BF16)
    new_h_ref[...] = new_h
    packed_ref[...] = dot_tn(pick_rows(send_ref, h.shape[0]), new_h).astype(BF16)


def backward_nodes(gh, slope, normed, inverse, wet_ref, wi_ref, wo_ref, gout_ref, gpre_ref):
    gout = norm_back(normed, inverse, wet_ref[...] * gh).astype(BF16)
    gpre = (dot_nt(gout, wo_ref[...]) * slope).astype(BF16)
    gout_ref[...] = gout
    gpre_ref[...] = gpre
    ginput = dot_nt(gpre, wi_ref[...])
    width = gh.shape[1]
    return gh + ginput[:, :width], ginput[:, width:]


def backward_edges(
    chunk, known, gh, gmsg, ge_ref, spread_ref, live_ref, slope_ref, normed_ref, inverse_ref,
    we_ref, wr_ref, wo_ref, gh_out_ref, more_ref, own_ref, halo_out_ref, ge_out_ref, gedge_ref, gpe_ref, sums_ref,
):
    rows, width = ge_ref.shape
    nodes = gh.shape[0]
    gh_out_ref[...] = gh
    gmsg = halves(gmsg)
    for start in range(0, rows, chunk):
        at = pl.ds(start, chunk)
        live = live_ref[at, :]
        owner = spread_ref[at, known:]
        sent = dot(jnp.concatenate([owner, owner], axis=1), gmsg)
        ge = ge_ref[at, :].astype(F32) + live * sent
        gedge = norm_back(normed_ref[at, :].astype(F32), inverse_ref[at, :], live * ge)
        gedge = gedge.astype(BF16)
        gpe = (dot_nt(gedge, wo_ref[...]) * slope_ref[at, :].astype(F32)).astype(BF16)
        gedge_ref[at, :] = gedge
        gpe_ref[at, :] = gpe
        ge = ge + dot_nt(gpe, we_ref[...])
        ge_out_ref[at, :] = ge.astype(ge_out_ref.dtype)
    flush(gedge_ref, gpe_ref, ge_out_ref)
    gathered = dot_tn(spread_ref[...], gpe_ref[...])
    own_ref[...] = gathered[:nodes]
    halo_out_ref[...] = gathered[nodes:known].astype(BF16)
    sums_ref[...] = gathered.astype(BF16)
    both = dot_nt(halves(gathered[known:]), wr_ref[...])
    more_ref[...] = both[:nodes] + both[nodes:]


def middle_kernel(
    chunk, pre_ref, e_ref, h_ref, halo_ref, spread_ref, mask_ref, live_ref, wet_ref,
    gh_ref, ge_ref, ws_ref, weo_ref, wni_ref, wno_ref, we_ref, wr_ref,
    act_ref, message_ref, act_n_ref, gout_ref, gpre_ref,
    gh_out_ref, more_ref, own_ref, halo_out_ref, ge_out_ref, gedge_ref, gpe_ref, sums_ref,
    slope_ref, normed_ref, inverse_ref, new_e_ref,
):
    h = h_ref[...]
    table = jnp.concatenate([h, halo_ref[...]], axis=0)

    def put(at, act, slope, normed, inverse, new_e):
        act_ref[at, :] = act
        slope_ref[at, :] = slope.astype(BF16)
        normed_ref[at, :] = normed.astype(BF16)
        inverse_ref[at, :] = inverse
        new_e_ref[at, :] = new_e

    forward_edges(chunk, pre_ref, e_ref, table, spread_ref, live_ref, ws_ref, weo_ref, put)
    message = dot_tn(mask_ref[...], new_e_ref[...]).astype(BF16)
    act, slope, normed, inverse = forward_nodes(h, message, wni_ref, wno_ref)
    message_ref[...] = message
    act_n_ref[...] = act
    flush(act_ref)
    gh, gmsg = backward_nodes(
        gh_ref[...].astype(F32), slope, normed, inverse, wet_ref, wni_ref, wno_ref, gout_ref, gpre_ref
    )
    backward_edges(
        chunk, table.shape[0], gh, gmsg, ge_ref, spread_ref, live_ref, slope_ref, normed_ref,
        inverse_ref, we_ref, wr_ref, weo_ref, gh_out_ref, more_ref, own_ref, halo_out_ref, ge_out_ref,
        gedge_ref, gpe_ref, sums_ref,
    )


def return_halo(gh_ref, more_ref, own_ref, back_ref, send_ref, wei_ref):
    nodes, width = gh_ref.shape
    total = own_ref[...] + dot(pick_rows(send_ref, nodes), back_ref[...])
    both = dot_nt(halves(total), wei_ref[...])
    return gh_ref[...] + more_ref[...] + both[:nodes] + both[nodes:]


def first_backward_kernel(
    chunk, gh_ref, more_ref, own_ref, back_ref, send_ref, slope_n_ref, normed_n_ref, inverse_n_ref, wet_ref,
    ge_ref, spread_ref, live_ref, slope_ref, normed_ref, inverse_ref,
    ws_ref, wno_ref, wni_ref, weo_ref, we_ref, wr_ref,
    gout_ref, gpre_ref, gh_out_ref, more_out_ref, own_out_ref, halo_out_ref, ge_out_ref,
    gedge_ref, gpe_ref, sums_ref,
):
    gh = return_halo(gh_ref, more_ref, own_ref, back_ref, send_ref, ws_ref)
    gh, gmsg = backward_nodes(
        gh, slope_n_ref[...].astype(F32), normed_n_ref[...].astype(F32), inverse_n_ref[...],
        wet_ref, wni_ref, wno_ref, gout_ref, gpre_ref,
    )
    known = spread_ref.shape[1] - gh.shape[0]
    backward_edges(
        chunk, known, gh, gmsg, ge_ref, spread_ref, live_ref, slope_ref, normed_ref,
        inverse_ref, we_ref, wr_ref, weo_ref, gh_out_ref, more_out_ref, own_out_ref, halo_out_ref, ge_out_ref,
        gedge_ref, gpe_ref, sums_ref,
    )


def last_kernel(gh_ref, more_ref, own_ref, back_ref, send_ref, wei_ref, out_ref):
    out_ref[...] = return_halo(gh_ref, more_ref, own_ref, back_ref, send_ref, wei_ref)


def place(order, me_ref, first_ref, second_ref, keep_ref, sent_ref):
    rows = keep_ref.shape[1]
    blocks = sorted({bits for bits, _ in order})
    sides = len(order) // len(blocks)
    for bits in blocks:
        spots = [order.index((bits, side)) for side in range(sides)]

        def spot(half):
            return jnp.where(me_ref[1] == half, spots[0], spots[1]) if sides == 2 else spots[0]

        for bit, out_ref in ((0, keep_ref), (1, sent_ref)):
            device = jnp.bitwise_xor(me_ref[0], bits + bit)
            row = 0
            for ref in (first_ref, second_ref):
                size = ref.shape[0] // (2 * len(blocks))
                start = pl.multiple_of(device * size, 16)
                done = 0
                while done < size:
                    half, at = divmod(row, rows)
                    step = min(size - done, rows - at)
                    piece = ref[pl.ds(pl.multiple_of(start + done, 16), step), :]
                    out_ref[spot(half), at : at + step, :] = piece.astype(BF16)
                    row += step
                    done += step
            if row < sides * rows:
                filler = jnp.zeros((sides * rows - row, keep_ref.shape[2]), BF16)
                out_ref[spot(sides - 1), row - (sides - 1) * rows :, :] = filler


def edge_weights_kernel(
    layout, me_ref, e_ref, h_ref, halo_ref, act_ref, gedge_ref, gpe_ref, sums_ref,
    keep_ref, sent_ref, grad_in_ref, grad_out_ref,
):
    width = e_ref.shape[1]
    h = h_ref[...]
    known = h.shape[0] + halo_ref.shape[0]
    table = jnp.concatenate([h, halo_ref[...]], axis=0)
    grad_in_ref[:width, :] = dot_tn(e_ref[...], gpe_ref[...])
    grad_in_ref[width : 2 * width, :] = dot_tn(table, sums_ref[:known, :])
    grad_in_ref[2 * width :, :] = dot_tn(h, sums_ref[known:, :])
    grad_out_ref[...] = dot_tn(act_ref[...], gedge_ref[...])
    place(layout, me_ref, grad_in_ref, grad_out_ref, keep_ref, sent_ref)


def node_weights_kernel(
    layout, me_ref, h_ref, message_ref, act_ref, gout_ref, gpre_ref,
    keep_ref, sent_ref, grad_in_ref, grad_out_ref,
):
    width = h_ref.shape[1]
    gpre = gpre_ref[...]
    grad_in_ref[:width, :] = dot_tn(h_ref[...], gpre)
    grad_in_ref[width:, :] = dot_tn(message_ref[...], gpre)
    grad_out_ref[...] = dot_tn(act_ref[...], gout_ref[...])
    place(layout, me_ref, grad_in_ref, grad_out_ref, keep_ref, sent_ref)


def trade(rows, back=False):
    count = lax.axis_size("mesh")
    if count == 2:
        return lax.ppermute(rows, "mesh", [(0, 1), (1, 0)])
    half = rows.shape[0] // 2
    up = [(i, (i + 1) % count) for i in range(count)]
    down = [(j, i) for i, j in up]
    first, second = (up, down) if back else (down, up)
    return jnp.concatenate(
        [lax.ppermute(rows[:half], "mesh", first), lax.ppermute(rows[half:], "mesh", second)], axis=0
    )


def flip(values, axis, bit):
    return lax.ppermute(values, axis, [(i, i ^ bit) for i in range(lax.axis_size(axis))])


def bits_of(axis):
    size = lax.axis_size(axis)
    return [1 << i for i in range(size.bit_length() - 1)]


def slot_order(route):
    order = [(0, 0)]
    for axis, bit in reversed(route):
        if axis == "dp":
            order = order + [(bits + bit, side) for bits, side in order]
        else:
            order = order + [(bits, 1) for bits, side in order]
    return order


class Sum:
    def __init__(self, keep, route):
        self.base, self.arrived, self.row = keep, None, 0
        self.slots, self.rows, self.width = keep.shape
        self.route = list(route)


def add_kernel(groups, tail, *refs):
    refs = list(refs)
    flat = [group for output in groups for group in output]
    terms, refs = refs[: 2 * len(flat)], refs[2 * len(flat) :]
    if tail:
        more, refs = refs[0], refs[1:]
    outs, kept = refs[: len(groups)], refs[len(groups) :]
    if tail:
        outs[-1][outs[-1].shape[0] - 1, : more.shape[0], :] = more[...]
    for output, out in zip(groups, outs):
        at = 0
        for rows, row, slots in output:
            base, arrived, terms = terms[0], terms[1], terms[2:]
            half = slots // 2
            low, high = (0, 1) if slots == 1 else (half, slots)
            total = base[low:high].astype(F32) + arrived[low:high, row : row + rows, :].astype(F32)
            out[: high - low, at : at + rows, :] = total.astype(BF16)
            at += rows
            if half:
                left, kept = kept[0], kept[1:]
                left[...] = base[:half].astype(F32) + arrived[:half, row : row + rows, :].astype(F32)


def add(wanted, after=(), tail=None):
    operands, groups, outs, kept = [], [], [], []
    for sums in wanted:
        group = []
        for one in sums:
            operands += [one.base, one.arrived]
            group.append((one.rows, one.row, one.slots))
            half = one.slots // 2
            if half:
                kept.append((one, ((half, one.rows, one.width), F32)))
        groups.append(group)
        outs.append(((max(half, 1), sum(one.rows for one in sums), one.width), BF16))
    if tail is not None:
        (count, size, width), dtype = outs[-1]
        outs[-1] = ((count + 1, size, width), dtype)
        operands.append(tail)
    results = call(
        functools.partial(add_kernel, groups, tail is not None),
        operands,
        outs + [shape for _, shape in kept],
        after=after,
    )
    for (one, _), base in zip(kept, results[len(outs) :]):
        one.base = base
        one.slots //= 2
    return results[: len(outs)]


def advance(wanted, after=(), tail=None):
    sent = add(wanted, after, tail)
    arrived = []
    for sums, values in zip(wanted, sent):
        steps = [one.route.pop(0) for one in sums if one.route]
        if not steps:
            arrived.append(None)
            continue
        other = flip(values, *steps[0])
        row = 0
        for one in sums:
            one.arrived, one.row = other, row
            row += one.rows
        arrived.append(other)
    return sent, arrived


def across(values):
    mine = values[0]
    for bit in bits_of("mesh")[1:]:
        mine = (mine.astype(F32) + flip(mine, "mesh", bit).astype(F32)).astype(BF16)
    return mine, flip(mine, "mesh", 1)


def output_kernel(
    factor, halves_of, me_ref, mine0_ref, other0_ref, mine1_ref, other1_ref, *outs
):
    low = me_ref[1] == 0
    row0 = row1 = 0
    for pair, rows in enumerate(halves_of):
        first, second = outs[2 * pair], outs[2 * pair + 1]
        cut, end = first.shape[1], first.shape[1] + second.shape[1]
        a = mine0_ref[row0 : row0 + rows, :].astype(F32) * factor
        b = other0_ref[row0 : row0 + rows, :].astype(F32) * factor
        both = jnp.concatenate([jnp.where(low, a, b), jnp.where(low, b, a)], axis=0)
        first[0] = both[:cut]
        second[0] = both[cut:end]
        a = mine1_ref[row1 : row1 + end, :].astype(F32)
        both = (a + other1_ref[row1 : row1 + end, :].astype(F32)) * factor
        first[1] = both[:cut]
        second[1] = both[cut:end]
        row0 += rows
        row1 += end


def body(
    node_feats,
    edge_feats,
    node_cot,
    edge_cot,
    w_edge_in,
    w_edge_out,
    w_node_in,
    w_node_out,
    neighbours,
    send_rows,
    edge_counts,
    ocean_mask,
):
    samples, nodes, width = node_feats.shape
    slots = neighbours.shape[1]
    rows = nodes * slots
    sent = send_rows.shape[1]
    known = nodes + sent
    chunk = rows
    shards = lax.axis_size("dp")
    total_rows = samples * shards * nodes * lax.axis_size("mesh")
    factor = 1.0 / total_rows**0.5
    beyond = [("dp", bit) for bit in bits_of("dp")[2:]]
    along = [("dp", 2)]
    edge_routes = (along + [("mesh", 1)] + beyond, along + beyond)
    node_routes = ([("mesh", 1)] + along + beyond, beyond + along)
    me = jnp.stack([lax.axis_index("dp"), lax.axis_index("mesh") % 2]).astype(jnp.int32)

    h0 = node_feats.reshape(nodes, width)
    e0 = edge_feats.reshape(rows, width)
    gh = node_cot.reshape(nodes, width)
    ge = edge_cot.reshape(rows, width)
    weights = (w_edge_in, w_edge_out, w_node_in, w_node_out)
    small, large, thin = (nodes, width), (rows, width), (sent, width)
    source = [rows_of(w_edge_in, layer, width, 2 * width) for layer in range(2)]
    edge = [rows_of(w_edge_in, layer, 0, width) for layer in range(2)]
    receiver = [rows_of(w_edge_in, layer, 2 * width) for layer in range(2)]
    edge_out = [rows_of(w_edge_out, layer) for layer in range(2)]
    node_in = [rows_of(w_node_in, layer) for layer in range(2)]
    node_out = [rows_of(w_node_out, layer) for layer in range(2)]

    (packed0,) = call(pack_kernel, (Part(send_rows), Part(h0)), [(thin, BF16)])
    halo0 = trade(packed0)
    spread, mask, live, wet, pre0, h0_near, e0_near, source0, edge_out0, node_in0, node_out0 = call(
        functools.partial(prepare_kernel, known, chunk),
        (Part(neighbours.T), Part(edge_counts.reshape(1, nodes)), Part(ocean_mask.reshape(1, nodes)))
        + (Part(h0), Part(e0), edge[0], receiver[0]),
        [
            ((rows, known + nodes), BF16), ((rows, nodes), BF16), ((rows, 1), F32),
            ((nodes, 1), F32), (large, F32),
        ],
        fetch=(Part(h0), Part(e0), source[0], edge_out[0], node_in[0], node_out[0]),
    )
    (
        act0, slope0, normed0, inverse0, e1,
        h1, message0, act_n0, slope_n0, normed_n0, inverse_n0, packed1,
        edge1_w, receiver1_w, source1_w,
    ) = call(
        functools.partial(first_forward_kernel, chunk),
        (pre0, e0_near, h0_near, halo0, spread, mask, live, wet, send_rows)
        + (source0, edge_out0, node_in0, node_out0),
        [(large, BF16)] * 3 + [((rows, 1), F32), (large, BF16), (small, BF16)]
        + [(small, BF16)] * 4 + [((nodes, 1), F32), (thin, BF16)],
        fetch=(edge[1], receiver[1], source[1]),
    )
    halo1 = trade(packed1)
    pre1, edge_out1, node_in1, node_out1, gh_near, ge_near = call(
        functools.partial(partial_kernel, chunk),
        (h1, spread, e1, edge1_w, receiver1_w),
        [(large, F32)],
        fetch=(edge_out[1], node_in[1], node_out[1], Part(gh), Part(ge)),
    )
    backward_outs = [(small, F32)] * 3 + [(thin, BF16)]
    backward_tail = [(large, BF16)] * 2 + [((known + nodes, width), BF16)]
    act1, message1, act_n1, gout1, gpre1, gh, more, own, halo_out, ge, gedge1, gpe1, sums1, *near_w = call(
        functools.partial(middle_kernel, chunk),
        (pre1, e1, h1, halo1, spread, mask, live, wet, gh_near, ge_near)
        + (source1_w, edge_out1, node_in1, node_out1, edge1_w, receiver1_w),
        [(large, BF16)] + [(small, BF16)] * 4 + backward_outs + [(large, F32)] + backward_tail,
        scratch=[VMEM(large, BF16)] * 2 + [VMEM((rows, 1), F32), VMEM(large, BF16)],
        fetch=(node_out[0], node_in[0], edge_out[0], edge[0], receiver[0]),
    )
    back = trade(halo_out, back=True)

    def weight_sum(kernel, route, operands, kinds, **more):
        order = slot_order(route)
        size = sum(w.shape[1] // shards for w in kinds)
        rows_in = size if ("mesh", 1) not in route else -(-size // 32) * 16
        shape = (len(order), rows_in, width)
        keep, send, *fetched = call(
            functools.partial(kernel, order),
            operands,
            [(shape, BF16)] * 2,
            scratch=[VMEM(w.shape[1:], F32) for w in kinds],
            smem=(me,),
            **more,
        )
        one = Sum(keep, route)
        one.arrived = flip(send, "dp", 1)
        return one, fetched

    def edge_sum(layer, operands, **more):
        return weight_sum(
            edge_weights_kernel, edge_routes[layer], operands, (w_edge_in, w_edge_out), **more
        )

    def node_sum(layer, operands, **more):
        return weight_sum(
            node_weights_kernel, node_routes[layer], operands, (w_node_in, w_node_out), **more
        )

    edge1, _ = edge_sum(1, (e1, h1, halo1, act1, gedge1, gpe1, sums1))
    node1, _ = node_sum(1, (h1, message1, act_n1, gout1, gpre1))
    _, arrived = advance([[edge1]])
    first, arrived_n = advance([[node1]])
    arrived += arrived_n
    gout0, gpre0, gh, more, own, halo_out, ge, gedge0, gpe0, sums0, e0_near, h0_near = call(
        functools.partial(first_backward_kernel, chunk),
        (gh, more, own, back, send_rows, slope_n0, normed_n0, inverse_n0, wet)
        + (ge, spread, live, slope0, normed0, inverse0, source1_w, *near_w),
        [(small, BF16)] * 2 + backward_outs + [far(large, BF16)] + backward_tail,
        after=tuple(first),
        fetch=(Part(e0), Part(h0)),
    )
    edge0, _ = edge_sum(0, (e0_near, h0_near, halo0, act0, gedge0, gpe0, sums0))
    node0, _ = node_sum(
        0, (h0_near, message0, act_n0, gout0, gpre0), after=tuple(arrived)
    )
    joint = lax.axis_size("mesh") == 2 and sent <= node0.rows
    wanted = [[edge0], [edge1], [node1], [node0]]
    _, arrived = advance(wanted, tail=halo_out if joint else None)
    if joint:
        back = Part(arrived[-1], (arrived[-1].shape[0] - 1, pl.ds(0, sent)), thin, pin=False)
    else:
        back = trade(halo_out, back=True)
    out, _ = advance(wanted)
    (gh,) = call(
        last_kernel, (gh, more, own, back, send_rows, source[0]), [far(small, F32)], after=(out[0],)
    )
    done = (in_hbm(gh),)
    while edge1.route:
        advance([[edge0, node0], [edge1], [node1]], after=done)
        done = ()
    (_, value1), _ = advance([[edge0, node0], [edge1, node1]], after=done)
    mine1, other1 = across(value1)
    while edge0.route:
        advance([[edge0, node0]])
    ((value0,), _) = advance([[edge0, node0]], after=(other1,))
    mine0, other0 = across(value0)
    grads = call(
        functools.partial(output_kernel, factor, (edge0.rows, node0.rows)),
        (mine0, other0, mine1, other1),
        [far((2, w.shape[1] // shards, width), F32) for w in weights],
        smem=(me,),
    )
    return (
        gh.reshape(samples, nodes, width),
        ge.reshape(samples, nodes, slots, width),
        *grads,
    )


def solution(mesh):
    placed = (
        P("dp", "mesh", None),
        P("dp", "mesh", None, None),
        P("dp", "mesh", None),
        P("dp", "mesh", None, None),
        P(),
        P(),
        P(),
        P(),
        P("mesh", None),
        P("mesh", None),
        P("mesh"),
        P("mesh"),
    )
    return jax.shard_map(
        body,
        mesh=mesh,
        in_specs=placed,
        out_specs=(
            P("dp", "mesh", None),
            P("dp", "mesh", None, None),
            P(None, "dp", None),
            P(None, "dp", None),
            P(None, "dp", None),
            P(None, "dp", None),
        ),
        check_vma=False,
    )
```

```python
import functools

import jax
import jax.numpy as jnp
from jax import lax
from jax.experimental import pallas as pl
from jax.experimental.pallas import tpu as pltpu
from jax.sharding import PartitionSpec as P

F32 = jnp.float32
BF16 = jnp.bfloat16
VMEM = pltpu.VMEM
EPS = 1e-05
MIB = 1024 * 1024
LIMIT = 20 * MIB


def in_hbm(array):
    return pltpu.with_memory_space_constraint(array, pltpu.HBM)


class Part:
    def __init__(self, array, index=(), shape=None, pin=True):
        self.array, self.index = (in_hbm(array) if pin else array), index
        self.shape = tuple(array.shape if shape is None else shape)


def rows_of(weight, layer, start=0, stop=None):
    stop = weight.shape[1] if stop is None else stop
    return Part(weight, (layer, pl.ds(start, stop - start)), (stop - start, weight.shape[2]))


class Arriving:
    def __init__(self, copy, ref):
        self.copy, self.ref, self.shape, self.dtype = copy, ref, ref.shape, ref.dtype

    def __getitem__(self, index):
        if self.copy is not None:
            self.copy.wait()
            self.copy = None
        return self.ref[index]


class Leaving:
    def __init__(self, copy, ref):
        self.copy, self.ref, self.shape, self.dtype = copy, ref, ref.shape, ref.dtype
        self.started = False

    def __getitem__(self, index):
        return self.ref[index]

    def __setitem__(self, index, value):
        self.ref[index] = value

    def flush(self):
        if not self.started:
            self.copy.start()
            self.started = True


def far(shape, dtype):
    return (shape, dtype, True)


def call(kernel, operands, outs, scratch=(), smem=(), after=(), fetch=(), limit=LIMIT):
    shapes = [jax.ShapeDtypeStruct(out[0], out[1]) for out in outs]
    is_far = [len(out) > 2 for out in outs] + [False] * len(fetch)
    results = len(shapes)
    shapes += [jax.ShapeDtypeStruct(p.shape, p.array.dtype) for p in fetch]
    remote = [isinstance(p, Part) for p in operands]
    arrays = [p.array if r else p for p, r in zip(operands, remote)]
    buffers = [VMEM(p.shape, p.array.dtype) for p, r in zip(operands, remote) if r]
    buffers += [VMEM(s.shape, s.dtype) for s, r in zip(shapes, is_far) if r]
    copies = len(buffers) + len(fetch)
    sems = [pltpu.SemaphoreType.DMA((max(copies, 1),))]

    def run(*refs):
        refs = list(refs)

        def cut(count):
            taken = refs[:count]
            del refs[:count]
            return taken

        scalars, sources, origins = cut(len(smem)), cut(len(arrays)), cut(len(fetch))
        cut(len(after))
        targets, held, (sem,) = cut(len(shapes)), cut(len(buffers)), cut(1)
        sems = [sem.at[at] for at in range(copies)]
        ins, leaving, fetched = [], [], []
        for part, source, r in zip(operands, sources, remote):
            if r:
                view = source.at[part.index] if part.index else source
                ref = held.pop(0)
                copy = pltpu.make_async_copy(view, ref, sems.pop(0))
                copy.start()
                source = Arriving(copy, ref)
            ins.append(source)
        for part, origin, target in zip(fetch, origins, targets[results:]):
            view = origin.at[part.index] if part.index else origin
            copy = pltpu.make_async_copy(view, target, sems.pop(0))
            copy.start()
            fetched.append(copy)
        results_here = []
        for target, r in zip(targets[:results], is_far):
            if r:
                ref = held.pop(0)
                target = Leaving(pltpu.make_async_copy(ref, target, sems.pop(0)), ref)
                leaving.append(target)
            results_here.append(target)
        kernel(*scalars, *ins, *results_here, *refs)
        for ref in ins:
            if isinstance(ref, Arriving):
                ref[:1]
        for ref in leaving:
            ref.flush()
        for copy in fetched:
            copy.wait()
        for ref in leaving:
            ref.copy.wait()

    def space(r):
        return pl.BlockSpec(memory_space=pl.ANY if r else VMEM)

    return pl.pallas_call(
        run,
        in_specs=[pl.BlockSpec(memory_space=pltpu.SMEM)] * len(smem)
        + [space(r) for r in remote]
        + [space(True)] * len(fetch)
        + [pl.BlockSpec(memory_space=pl.ANY)] * len(after),
        out_specs=tuple(space(r) for r in is_far),
        out_shape=tuple((pltpu.HBM if r else VMEM)(s.shape, s.dtype) for s, r in zip(shapes, is_far)),
        scratch_shapes=buffers + sems + list(scratch),
        compiler_params=pltpu.CompilerParams(vmem_limit_bytes=limit),
        cost_estimate=pl.CostEstimate(flops=0, bytes_accessed=0, transcendentals=0),
    )(*smem, *arrays, *[p.array for p in fetch], *after)


def flush(*refs):
    for ref in refs:
        if isinstance(ref, Leaving):
            ref.flush()


def dot(a, b):
    return jnp.dot(a, b, preferred_element_type=F32)


def dot_nt(a, b):
    return lax.dot_general(a, b, (((1,), (1,)), ((), ())), preferred_element_type=F32)


def dot_tn(a, b):
    return lax.dot_general(a, b, (((0,), (0,)), ((), ())), preferred_element_type=F32)


def silu_and_slope(values):
    sigmoid = 0.5 * jnp.tanh(0.5 * values) + 0.5
    act = values * sigmoid
    return act, sigmoid + act * (1.0 - sigmoid)


def norm_parts(values):
    center = jnp.mean(values, axis=-1, keepdims=True)
    shifted = values - center
    inverse = lax.rsqrt(jnp.mean(shifted * shifted, axis=-1, keepdims=True) + EPS)
    return shifted * inverse, inverse


def norm_back(normed, inverse, upstream):
    return inverse * (
        upstream
        - jnp.mean(upstream, axis=-1, keepdims=True)
        - normed * jnp.mean(upstream * normed, axis=-1, keepdims=True)
    )


def halves(values):
    high = values.astype(BF16)
    low = (values - high.astype(F32)).astype(BF16)
    return jnp.concatenate([high, low], axis=0)


def node_of_edge(rows, nodes, slots):
    edge = lax.broadcasted_iota(jnp.int32, (rows, nodes), 0)
    node = lax.broadcasted_iota(jnp.int32, (rows, nodes), 1)
    return (edge // slots) == node


def pick_rows(send_ref, nodes):
    row = lax.broadcasted_iota(jnp.int32, (nodes, send_ref.shape[1]), 0)
    return (row == send_ref[...]).astype(F32).astype(BF16)


def pack_kernel(send_ref, h_ref, packed_ref):
    pick = pick_rows(send_ref, h_ref.shape[0])
    packed_ref[...] = dot_tn(pick, h_ref[...]).astype(BF16)


def prepare_kernel(
    table, chunk, nb_ref, count_ref, ocean_ref, h_ref, e_ref, we_ref, wr_ref,
    spread_ref, mask_ref, live_ref, wet_ref, pre_ref,
):
    slots, nodes = nb_ref.shape
    rows = nodes * slots
    owner = node_of_edge(rows, nodes, slots).astype(F32)
    owner16 = owner.astype(BF16)
    listed = dot_nt(owner16, nb_ref[...].astype(F32).astype(BF16))
    slot_here = lax.broadcasted_iota(jnp.int32, (rows, slots), 0) % slots
    slot_at = lax.broadcasted_iota(jnp.int32, (rows, slots), 1)
    source = jnp.sum(jnp.where(slot_here == slot_at, listed, 0.0), axis=1, keepdims=True)
    half = (table - nodes) // 2
    moved = jnp.where(source >= nodes + half, source - half, source + half)
    source = jnp.where(source >= nodes, moved, source)
    at = lax.broadcasted_iota(jnp.int32, (rows, table), 1).astype(F32)
    spread_ref[:, :table] = jnp.where(at == source, 1.0, 0.0).astype(BF16)
    spread_ref[:, table:] = owner16
    slot_of_row = lax.broadcasted_iota(jnp.int32, (rows, nodes), 0) % slots
    mask = jnp.where(slot_of_row < count_ref[...], owner, 0.0)
    mask_ref[...] = mask.astype(BF16)
    live_ref[...] = jnp.sum(mask, axis=1, keepdims=True)
    row = lax.broadcasted_iota(jnp.int32, (nodes, nodes), 0)
    column = lax.broadcasted_iota(jnp.int32, (nodes, nodes), 1)
    wet = jnp.where(row == column, ocean_ref[...].astype(F32), 0.0)
    wet_ref[...] = jnp.sum(wet, axis=1, keepdims=True)
    partial_kernel(chunk, h_ref, spread_ref, e_ref, we_ref, wr_ref, pre_ref)


def partial_kernel(chunk, h_ref, spread_ref, e_ref, we_ref, wr_ref, pre_ref):
    rows, width = e_ref.shape
    known = spread_ref.shape[1] - h_ref.shape[0]
    h = h_ref[...]
    for start in range(0, rows, chunk):
        at = pl.ds(start, chunk)
        own = dot(spread_ref[at, known:], h).astype(BF16)
        pre = dot(e_ref[at, :], we_ref[...])
        pre_ref[at, :] = pre + dot(own, wr_ref[...])


def forward_edges(chunk, pre_ref, e_ref, table, spread_ref, live_ref, ws_ref, wo_ref, put):
    rows, width = e_ref.shape
    known = table.shape[0]
    for start in range(0, rows, chunk):
        at = pl.ds(start, chunk)
        src = dot(spread_ref[at, :known], table).astype(BF16)
        pre = pre_ref[at, :] + dot(src, ws_ref[...])
        act, slope = silu_and_slope(pre)
        act = act.astype(BF16)
        normed, inverse = norm_parts(dot(act, wo_ref[...]))
        new_e = (e_ref[at, :].astype(F32) + live_ref[at, :] * normed).astype(BF16)
        put(at, act, slope, normed, inverse, new_e)


def forward_nodes(h, message, wi_ref, wo_ref):
    width = h.shape[1]
    pre = dot(h, wi_ref[:width, :]) + dot(message, wi_ref[width:, :])
    act, slope = silu_and_slope(pre)
    act = act.astype(BF16)
    normed, inverse = norm_parts(dot(act, wo_ref[...]))
    return act, slope, normed, inverse


def first_forward_kernel(
    chunk, pre_ref, e_ref, h_ref, halo_ref, spread_ref, mask_ref, live_ref, wet_ref, send_ref,
    ws_ref, weo_ref, wni_ref, wno_ref,
    act_ref, slope_ref, normed_ref, inverse_ref, new_e_ref,
    new_h_ref, message_ref, act_n_ref, slope_n_ref, normed_n_ref, inverse_n_ref, packed_ref,
):
    h = h_ref[...]
    table = jnp.concatenate([h, halo_ref[...]], axis=0)

    def put(at, act, slope, normed, inverse, new_e):
        act_ref[at, :] = act
        slope_ref[at, :] = slope.astype(BF16)
        normed_ref[at, :] = normed.astype(BF16)
        inverse_ref[at, :] = inverse
        new_e_ref[at, :] = new_e

    forward_edges(chunk, pre_ref, e_ref, table, spread_ref, live_ref, ws_ref, weo_ref, put)
    flush(act_ref, slope_ref, normed_ref, inverse_ref, new_e_ref)
    message = dot_tn(mask_ref[...], new_e_ref[...]).astype(BF16)
    act, slope, normed, inverse = forward_nodes(h, message, wni_ref, wno_ref)
    message_ref[...] = message
    act_n_ref[...] = act
    slope_n_ref[...] = slope.astype(BF16)
    normed_n_ref[...] = normed.astype(BF16)
    inverse_n_ref[...] = inverse
    flush(message_ref, act_n_ref, slope_n_ref, normed_n_ref, inverse_n_ref)
    new_h = (h.astype(F32) + wet_ref[...] * normed).astype(BF16)
    new_h_ref[...] = new_h
    packed_ref[...] = dot_tn(pick_rows(send_ref, h.shape[0]), new_h).astype(BF16)


def backward_nodes(gh, slope, normed, inverse, wet_ref, wi_ref, wo_ref, gout_ref, gpre_ref):
    gout = norm_back(normed, inverse, wet_ref[...] * gh).astype(BF16)
    gpre = (dot_nt(gout, wo_ref[...]) * slope).astype(BF16)
    gout_ref[...] = gout
    gpre_ref[...] = gpre
    ginput = dot_nt(gpre, wi_ref[...])
    width = gh.shape[1]
    return gh + ginput[:, :width], ginput[:, width:]


def backward_edges(
    chunk, known, gh, gmsg, ge_ref, spread_ref, live_ref, slope_ref, normed_ref, inverse_ref,
    we_ref, wr_ref, wo_ref, gh_out_ref, more_ref, own_ref, halo_out_ref, ge_out_ref, gedge_ref, gpe_ref, sums_ref,
):
    rows, width = ge_ref.shape
    nodes = gh.shape[0]
    gh_out_ref[...] = gh
    gmsg = halves(gmsg)
    for start in range(0, rows, chunk):
        at = pl.ds(start, chunk)
        live = live_ref[at, :]
        owner = spread_ref[at, known:]
        sent = dot(jnp.concatenate([owner, owner], axis=1), gmsg)
        ge = ge_ref[at, :].astype(F32) + live * sent
        gedge = norm_back(normed_ref[at, :].astype(F32), inverse_ref[at, :], live * ge)
        gedge = gedge.astype(BF16)
        gpe = (dot_nt(gedge, wo_ref[...]) * slope_ref[at, :].astype(F32)).astype(BF16)
        gedge_ref[at, :] = gedge
        gpe_ref[at, :] = gpe
        ge = ge + dot_nt(gpe, we_ref[...])
        ge_out_ref[at, :] = ge.astype(ge_out_ref.dtype)
    flush(gedge_ref, gpe_ref, ge_out_ref)
    gathered = dot_tn(spread_ref[...], gpe_ref[...])
    own_ref[...] = gathered[:nodes]
    halo_out_ref[...] = gathered[nodes:known].astype(BF16)
    sums_ref[...] = gathered.astype(BF16)
    both = dot_nt(halves(gathered[known:]), wr_ref[...])
    more_ref[...] = both[:nodes] + both[nodes:]


def middle_kernel(
    chunk, pre_ref, e_ref, h_ref, halo_ref, spread_ref, mask_ref, live_ref, wet_ref,
    gh_ref, ge_ref, ws_ref, weo_ref, wni_ref, wno_ref, we_ref, wr_ref,
    act_ref, message_ref, act_n_ref, gout_ref, gpre_ref,
    gh_out_ref, more_ref, own_ref, halo_out_ref, ge_out_ref, gedge_ref, gpe_ref, sums_ref,
    slope_ref, normed_ref, inverse_ref, new_e_ref,
):
    h = h_ref[...]
    table = jnp.concatenate([h, halo_ref[...]], axis=0)

    def put(at, act, slope, normed, inverse, new_e):
        act_ref[at, :] = act
        slope_ref[at, :] = slope.astype(BF16)
        normed_ref[at, :] = normed.astype(BF16)
        inverse_ref[at, :] = inverse
        new_e_ref[at, :] = new_e

    forward_edges(chunk, pre_ref, e_ref, table, spread_ref, live_ref, ws_ref, weo_ref, put)
    message = dot_tn(mask_ref[...], new_e_ref[...]).astype(BF16)
    act, slope, normed, inverse = forward_nodes(h, message, wni_ref, wno_ref)
    message_ref[...] = message
    act_n_ref[...] = act
    flush(act_ref)
    gh, gmsg = backward_nodes(
        gh_ref[...].astype(F32), slope, normed, inverse, wet_ref, wni_ref, wno_ref, gout_ref, gpre_ref
    )
    backward_edges(
        chunk, table.shape[0], gh, gmsg, ge_ref, spread_ref, live_ref, slope_ref, normed_ref,
        inverse_ref, we_ref, wr_ref, weo_ref, gh_out_ref, more_ref, own_ref, halo_out_ref, ge_out_ref,
        gedge_ref, gpe_ref, sums_ref,
    )


def return_halo(gh_ref, more_ref, own_ref, back_ref, send_ref, wei_ref):
    nodes, width = gh_ref.shape
    sent = send_ref.shape[1]
    first = 0 if back_ref.shape[0] == sent else nodes
    total = own_ref[...] + dot(pick_rows(send_ref, nodes), back_ref[first : first + sent, :])
    both = dot_nt(halves(total), wei_ref[...])
    return gh_ref[...] + more_ref[...] + both[:nodes] + both[nodes:]


def first_backward_kernel(
    chunk, gh_ref, more_ref, own_ref, back_ref, send_ref, slope_n_ref, normed_n_ref, inverse_n_ref, wet_ref,
    ge_ref, spread_ref, live_ref, slope_ref, normed_ref, inverse_ref,
    ws_ref, wno_ref, wni_ref, weo_ref, we_ref, wr_ref,
    gout_ref, gpre_ref, gh_out_ref, more_out_ref, own_out_ref, halo_out_ref, ge_out_ref,
    gedge_ref, gpe_ref, sums_ref,
):
    gh = return_halo(gh_ref, more_ref, own_ref, back_ref, send_ref, ws_ref)
    gh, gmsg = backward_nodes(
        gh, slope_n_ref[...].astype(F32), normed_n_ref[...].astype(F32), inverse_n_ref[...],
        wet_ref, wni_ref, wno_ref, gout_ref, gpre_ref,
    )
    known = spread_ref.shape[1] - gh.shape[0]
    backward_edges(
        chunk, known, gh, gmsg, ge_ref, spread_ref, live_ref, slope_ref, normed_ref,
        inverse_ref, we_ref, wr_ref, weo_ref, gh_out_ref, more_out_ref, own_out_ref, halo_out_ref, ge_out_ref,
        gedge_ref, gpe_ref, sums_ref,
    )


def last_kernel(gh_ref, more_ref, own_ref, back_ref, send_ref, wei_ref, out_ref):
    out_ref[...] = return_halo(gh_ref, more_ref, own_ref, back_ref, send_ref, wei_ref)


def place(order, me_ref, first_ref, second_ref, keep_ref, sent_ref):
    rows = keep_ref.shape[1]
    blocks = sorted({bits for bits, _ in order})
    sides = len(order) // len(blocks)
    for bits in blocks:
        spots = [order.index((bits, side)) for side in range(sides)]

        def spot(half):
            return jnp.where(me_ref[1] == half, spots[0], spots[1]) if sides == 2 else spots[0]

        for bit, out_ref in ((0, keep_ref), (1, sent_ref)):
            device = jnp.bitwise_xor(me_ref[0], bits + bit)
            row = 0
            for ref in (first_ref, second_ref):
                size = ref.shape[0] // (2 * len(blocks))
                start = pl.multiple_of(device * size, 16)
                done = 0
                while done < size:
                    half, at = divmod(row, rows)
                    step = min(size - done, rows - at)
                    piece = ref[pl.ds(pl.multiple_of(start + done, 16), step), :]
                    out_ref[spot(half), at : at + step, :] = piece.astype(BF16)
                    row += step
                    done += step
            if row < sides * rows:
                filler = jnp.zeros((sides * rows - row, keep_ref.shape[2]), BF16)
                out_ref[spot(sides - 1), row - (sides - 1) * rows :, :] = filler


def edge_weights_kernel(
    layout, me_ref, e_ref, h_ref, halo_ref, act_ref, gedge_ref, gpe_ref, sums_ref,
    keep_ref, sent_ref, grad_in_ref, grad_out_ref,
):
    width = e_ref.shape[1]
    h = h_ref[...]
    known = h.shape[0] + halo_ref.shape[0]
    table = jnp.concatenate([h, halo_ref[...]], axis=0)
    grad_in_ref[:width, :] = dot_tn(e_ref[...], gpe_ref[...])
    grad_in_ref[width : 2 * width, :] = dot_tn(table, sums_ref[:known, :])
    grad_in_ref[2 * width :, :] = dot_tn(h, sums_ref[known:, :])
    grad_out_ref[...] = dot_tn(act_ref[...], gedge_ref[...])
    place(layout, me_ref, grad_in_ref, grad_out_ref, keep_ref, sent_ref)


def node_weights_kernel(
    layout, me_ref, h_ref, message_ref, act_ref, gout_ref, gpre_ref,
    keep_ref, sent_ref, grad_in_ref, grad_out_ref,
):
    width = h_ref.shape[1]
    gpre = gpre_ref[...]
    grad_in_ref[:width, :] = dot_tn(h_ref[...], gpre)
    grad_in_ref[width:, :] = dot_tn(message_ref[...], gpre)
    grad_out_ref[...] = dot_tn(act_ref[...], gout_ref[...])
    place(layout, me_ref, grad_in_ref, grad_out_ref, keep_ref, sent_ref)


def trade(rows, back=False):
    count = lax.axis_size("mesh")
    if count == 2:
        return lax.ppermute(rows, "mesh", [(0, 1), (1, 0)])
    half = rows.shape[0] // 2
    up = [(i, (i + 1) % count) for i in range(count)]
    down = [(j, i) for i, j in up]
    first, second = (up, down) if back else (down, up)
    return jnp.concatenate(
        [lax.ppermute(rows[:half], "mesh", first), lax.ppermute(rows[half:], "mesh", second)], axis=0
    )


def flip(values, axis, bit):
    return lax.ppermute(values, axis, [(i, i ^ bit) for i in range(lax.axis_size(axis))])


def bits_of(axis):
    size = lax.axis_size(axis)
    return [1 << i for i in range(size.bit_length() - 1)]


def slot_order(route):
    order = [(0, 0)]
    for axis, bit in reversed(route):
        if axis == "dp":
            order = order + [(bits + bit, side) for bits, side in order]
        else:
            order = order + [(bits, 1) for bits, side in order]
    return order


class Sum:
    def __init__(self, keep, route):
        self.base, self.arrived, self.row = keep, None, 0
        self.slots, self.rows, self.width = keep.shape
        self.route = list(route)


def add_kernel(groups, tail, *refs):
    refs = list(refs)
    flat = [group for output in groups for group in output]
    terms, refs = refs[: 2 * len(flat)], refs[2 * len(flat) :]
    if tail:
        more, refs = refs[0], refs[1:]
    outs, kept = refs[: len(groups)], refs[len(groups) :]
    if tail:
        outs[-1][outs[-1].shape[0] - 1, : more.shape[0], :] = more[...]
    for output, out in zip(groups, outs):
        at = 0
        for rows, row, slots in output:
            base, arrived, terms = terms[0], terms[1], terms[2:]
            half = slots // 2
            low, high = (0, 1) if slots == 1 else (half, slots)
            total = base[low:high].astype(F32) + arrived[low:high, row : row + rows, :].astype(F32)
            out[: high - low, at : at + rows, :] = total.astype(BF16)
            at += rows
            if half:
                left, kept = kept[0], kept[1:]
                left[...] = base[:half].astype(F32) + arrived[:half, row : row + rows, :].astype(F32)


def add(wanted, after=(), tail=None):
    operands, groups, outs, kept = [], [], [], []
    for sums in wanted:
        group = []
        for one in sums:
            operands += [one.base, one.arrived]
            group.append((one.rows, one.row, one.slots))
            half = one.slots // 2
            if half:
                kept.append((one, ((half, one.rows, one.width), F32)))
        groups.append(group)
        outs.append(((max(half, 1), sum(one.rows for one in sums), one.width), BF16))
    if tail is not None:
        (count, size, width), dtype = outs[-1]
        outs[-1] = ((count + 1, size, width), dtype)
        operands.append(tail)
    results = call(
        functools.partial(add_kernel, groups, tail is not None),
        operands,
        outs + [shape for _, shape in kept],
        after=after,
    )
    for (one, _), base in zip(kept, results[len(outs) :]):
        one.base = base
        one.slots //= 2
    return results[: len(outs)]


def advance(wanted, after=(), tail=None):
    sent = add(wanted, after, tail)
    arrived = []
    for sums, values in zip(wanted, sent):
        steps = [one.route.pop(0) for one in sums if one.route]
        if not steps:
            arrived.append(None)
            continue
        other = flip(values, *steps[0])
        row = 0
        for one in sums:
            one.arrived, one.row = other, row
            row += one.rows
        arrived.append(other)
    return sent, arrived


def across(values):
    mine = values[0]
    for bit in bits_of("mesh")[1:]:
        mine = (mine.astype(F32) + flip(mine, "mesh", bit).astype(F32)).astype(BF16)
    return mine, flip(mine, "mesh", 1)


def output_kernel(
    factor, halves_of, me_ref, mine0_ref, other0_ref, mine1_ref, other1_ref, *outs
):
    low = me_ref[1] == 0
    row0 = row1 = 0
    for pair, rows in enumerate(halves_of):
        first, second = outs[2 * pair], outs[2 * pair + 1]
        cut, end = first.shape[1], first.shape[1] + second.shape[1]
        a = mine0_ref[row0 : row0 + rows, :].astype(F32) * factor
        b = other0_ref[row0 : row0 + rows, :].astype(F32) * factor
        both = jnp.concatenate([jnp.where(low, a, b), jnp.where(low, b, a)], axis=0)
        first[0] = both[:cut]
        second[0] = both[cut:end]
        a = mine1_ref[row1 : row1 + end, :].astype(F32)
        both = (a + other1_ref[row1 : row1 + end, :].astype(F32)) * factor
        first[1] = both[:cut]
        second[1] = both[cut:end]
        row0 += rows
        row1 += end


def body(
    node_feats,
    edge_feats,
    node_cot,
    edge_cot,
    w_edge_in,
    w_edge_out,
    w_node_in,
    w_node_out,
    neighbours,
    send_rows,
    edge_counts,
    ocean_mask,
):
    samples, nodes, width = node_feats.shape
    slots = neighbours.shape[1]
    rows = nodes * slots
    sent = send_rows.shape[1]
    known = nodes + sent
    chunk = rows
    shards = lax.axis_size("dp")
    total_rows = samples * shards * nodes * lax.axis_size("mesh")
    factor = 1.0 / total_rows**0.5
    beyond = [("dp", bit) for bit in bits_of("dp")[2:]]
    along = [("dp", 2)]
    edge_routes = (along + [("mesh", 1)] + beyond, along + beyond)
    node_routes = ([("mesh", 1)] + along + beyond, beyond + along)
    me = jnp.stack([lax.axis_index("dp"), lax.axis_index("mesh") % 2]).astype(jnp.int32)

    h0 = node_feats.reshape(nodes, width)
    e0 = edge_feats.reshape(rows, width)
    gh = node_cot.reshape(nodes, width)
    ge = edge_cot.reshape(rows, width)
    weights = (w_edge_in, w_edge_out, w_node_in, w_node_out)
    small, large, thin = (nodes, width), (rows, width), (sent, width)
    source = [rows_of(w_edge_in, layer, width, 2 * width) for layer in range(2)]
    edge = [rows_of(w_edge_in, layer, 0, width) for layer in range(2)]
    receiver = [rows_of(w_edge_in, layer, 2 * width) for layer in range(2)]
    edge_out = [rows_of(w_edge_out, layer) for layer in range(2)]
    node_in = [rows_of(w_node_in, layer) for layer in range(2)]
    node_out = [rows_of(w_node_out, layer) for layer in range(2)]

    (packed0,) = call(pack_kernel, (Part(send_rows), Part(h0)), [(thin, BF16)])
    halo0 = trade(packed0)
    spread, mask, live, wet, pre0, h0_near, e0_near, source0, edge_out0, node_in0, node_out0 = call(
        functools.partial(prepare_kernel, known, chunk),
        (Part(neighbours.T), Part(edge_counts.reshape(1, nodes)), Part(ocean_mask.reshape(1, nodes)))
        + (Part(h0), Part(e0), edge[0], receiver[0]),
        [
            ((rows, known + nodes), BF16), ((rows, nodes), BF16), ((rows, 1), F32),
            ((nodes, 1), F32), (large, F32),
        ],
        fetch=(Part(h0), Part(e0), source[0], edge_out[0], node_in[0], node_out[0]),
    )
    (
        act0, slope0, normed0, inverse0, e1,
        h1, message0, act_n0, slope_n0, normed_n0, inverse_n0, packed1,
        edge1_w, receiver1_w, source1_w,
    ) = call(
        functools.partial(first_forward_kernel, chunk),
        (pre0, e0_near, h0_near, halo0, spread, mask, live, wet, send_rows)
        + (source0, edge_out0, node_in0, node_out0),
        [(large, BF16)] * 3 + [((rows, 1), F32), (large, BF16), (small, BF16)]
        + [(small, BF16)] * 4 + [((nodes, 1), F32), (thin, BF16)],
        fetch=(edge[1], receiver[1], source[1]),
    )
    halo1 = trade(packed1)
    pre1, edge_out1, node_in1, node_out1, gh_near, ge_near = call(
        functools.partial(partial_kernel, chunk),
        (h1, spread, e1, edge1_w, receiver1_w),
        [(large, F32)],
        fetch=(edge_out[1], node_in[1], node_out[1], Part(gh), Part(ge)),
    )
    backward_outs = [(small, F32)] * 3 + [(thin, BF16)]
    backward_tail = [(large, BF16)] * 2 + [((known + nodes, width), BF16)]
    act1, message1, act_n1, gout1, gpre1, gh, more, own, halo_out, ge, gedge1, gpe1, sums1, *near_w = call(
        functools.partial(middle_kernel, chunk),
        (pre1, e1, h1, halo1, spread, mask, live, wet, gh_near, ge_near)
        + (source1_w, edge_out1, node_in1, node_out1, edge1_w, receiver1_w),
        [(large, BF16)] + [(small, BF16)] * 4 + backward_outs + [(large, F32)] + backward_tail,
        scratch=[VMEM(large, BF16)] * 2 + [VMEM((rows, 1), F32), VMEM(large, BF16)],
        fetch=(node_out[0], node_in[0], edge_out[0], edge[0], receiver[0]),
    )
    back = trade(halo_out if lax.axis_size("mesh") > 2 else sums1, back=True)

    def weight_sum(kernel, route, operands, kinds, **more):
        order = slot_order(route)
        size = sum(w.shape[1] // shards for w in kinds)
        rows_in = size if ("mesh", 1) not in route else -(-size // 32) * 16
        shape = (len(order), rows_in, width)
        keep, send, *fetched = call(
            functools.partial(kernel, order),
            operands,
            [(shape, BF16)] * 2,
            scratch=[VMEM(w.shape[1:], F32) for w in kinds],
            smem=(me,),
            **more,
        )
        one = Sum(keep, route)
        one.arrived = flip(send, "dp", 1)
        return one, fetched

    def edge_sum(layer, operands, **more):
        return weight_sum(
            edge_weights_kernel, edge_routes[layer], operands, (w_edge_in, w_edge_out), **more
        )

    def node_sum(layer, operands, **more):
        return weight_sum(
            node_weights_kernel, node_routes[layer], operands, (w_node_in, w_node_out), **more
        )

    edge1, _ = edge_sum(1, (e1, h1, halo1, act1, gedge1, gpe1, sums1))
    node1, _ = node_sum(1, (h1, message1, act_n1, gout1, gpre1))
    _, arrived = advance([[edge1]])
    first, arrived_n = advance([[node1]])
    arrived += arrived_n
    gout0, gpre0, gh, more, own, halo_out, ge, gedge0, gpe0, sums0, e0_near, h0_near = call(
        functools.partial(first_backward_kernel, chunk),
        (gh, more, own, back, send_rows, slope_n0, normed_n0, inverse_n0, wet)
        + (ge, spread, live, slope0, normed0, inverse0, source1_w, *near_w),
        [(small, BF16)] * 2 + backward_outs + [far(large, BF16)] + backward_tail,
        after=tuple(first),
        fetch=(Part(e0), Part(h0)),
    )
    edge0, _ = edge_sum(0, (e0_near, h0_near, halo0, act0, gedge0, gpe0, sums0))
    node0, _ = node_sum(
        0, (h0_near, message0, act_n0, gout0, gpre0), after=tuple(arrived)
    )
    joint = lax.axis_size("mesh") == 2 and sent <= node0.rows
    wanted = [[edge0], [edge1], [node1], [node0]]
    out, _ = advance([[edge0], [edge1]])
    _, arrived = advance([[node1], [node0]], after=(out[0],), tail=halo_out if joint else None)
    if joint:
        back = Part(arrived[-1], (arrived[-1].shape[0] - 1, pl.ds(0, sent)), thin, pin=False)
    else:
        back = trade(halo_out, back=True)
    out, _ = advance(wanted)
    (gh,) = call(
        last_kernel, (gh, more, own, back, send_rows, source[0]), [far(small, F32)], after=(out[0],)
    )
    done = (in_hbm(gh),)
    while edge1.route:
        advance([[edge0, node0], [edge1], [node1]], after=done)
        done = ()
    (_, value1), _ = advance([[edge0, node0], [edge1, node1]], after=done)
    mine1, other1 = across(value1)
    while edge0.route:
        advance([[edge0, node0]])
    ((value0,), _) = advance([[edge0, node0]], after=(other1,))
    mine0, other0 = across(value0)
    grads = call(
        functools.partial(output_kernel, factor, (edge0.rows, node0.rows)),
        (mine0, other0, mine1, other1),
        [far((2, w.shape[1] // shards, width), F32) for w in weights],
        smem=(me,),
    )
    return (
        gh.reshape(samples, nodes, width),
        ge.reshape(samples, nodes, slots, width),
        *grads,
    )


def solution(mesh):
    placed = (
        P("dp", "mesh", None),
        P("dp", "mesh", None, None),
        P("dp", "mesh", None),
        P("dp", "mesh", None, None),
        P(),
        P(),
        P(),
        P(),
        P("mesh", None),
        P("mesh", None),
        P("mesh"),
        P("mesh"),
    )
    return jax.shard_map(
        body,
        mesh=mesh,
        in_specs=placed,
        out_specs=(
            P("dp", "mesh", None),
            P("dp", "mesh", None, None),
            P(None, "dp", None),
            P(None, "dp", None),
            P(None, "dp", None),
            P(None, "dp", None),
        ),
        check_vma=False,
    )
```

```python
import functools

import jax
import jax.numpy as jnp
from jax import lax
from jax.experimental import pallas as pl
from jax.experimental.pallas import tpu as pltpu
from jax.sharding import PartitionSpec as P

F32 = jnp.float32
BF16 = jnp.bfloat16
VMEM = pltpu.VMEM
EPS = 1e-05
MIB = 1024 * 1024
LIMIT = 20 * MIB


def in_hbm(array):
    return pltpu.with_memory_space_constraint(array, pltpu.HBM)


class Part:
    def __init__(self, array, index=(), shape=None, pin=True):
        self.array, self.index = (in_hbm(array) if pin else array), index
        self.shape = tuple(array.shape if shape is None else shape)


def rows_of(weight, layer, start=0, stop=None):
    stop = weight.shape[1] if stop is None else stop
    return Part(weight, (layer, pl.ds(start, stop - start)), (stop - start, weight.shape[2]))


class Arriving:
    def __init__(self, copy, ref):
        self.copy, self.ref, self.shape, self.dtype = copy, ref, ref.shape, ref.dtype

    def __getitem__(self, index):
        if self.copy is not None:
            self.copy.wait()
            self.copy = None
        return self.ref[index]


class Leaving:
    def __init__(self, copy, ref):
        self.copy, self.ref, self.shape, self.dtype = copy, ref, ref.shape, ref.dtype
        self.started = False

    def __getitem__(self, index):
        return self.ref[index]

    def __setitem__(self, index, value):
        self.ref[index] = value

    def flush(self):
        if not self.started:
            self.copy.start()
            self.started = True


def far(shape, dtype):
    return (shape, dtype, True)


def call(kernel, operands, outs, scratch=(), smem=(), after=(), fetch=(), limit=LIMIT):
    shapes = [jax.ShapeDtypeStruct(out[0], out[1]) for out in outs]
    is_far = [len(out) > 2 for out in outs] + [False] * len(fetch)
    results = len(shapes)
    shapes += [jax.ShapeDtypeStruct(p.shape, p.array.dtype) for p in fetch]
    remote = [isinstance(p, Part) for p in operands]
    arrays = [p.array if r else p for p, r in zip(operands, remote)]
    buffers = [VMEM(p.shape, p.array.dtype) for p, r in zip(operands, remote) if r]
    buffers += [VMEM(s.shape, s.dtype) for s, r in zip(shapes, is_far) if r]
    copies = len(buffers) + len(fetch)
    sems = [pltpu.SemaphoreType.DMA((max(copies, 1),))]

    def run(*refs):
        refs = list(refs)

        def cut(count):
            taken = refs[:count]
            del refs[:count]
            return taken

        scalars, sources, origins = cut(len(smem)), cut(len(arrays)), cut(len(fetch))
        cut(len(after))
        targets, held, (sem,) = cut(len(shapes)), cut(len(buffers)), cut(1)
        sems = [sem.at[at] for at in range(copies)]
        ins, leaving, fetched = [], [], []
        for part, source, r in zip(operands, sources, remote):
            if r:
                view = source.at[part.index] if part.index else source
                ref = held.pop(0)
                copy = pltpu.make_async_copy(view, ref, sems.pop(0))
                copy.start()
                source = Arriving(copy, ref)
            ins.append(source)
        for part, origin, target in zip(fetch, origins, targets[results:]):
            view = origin.at[part.index] if part.index else origin
            copy = pltpu.make_async_copy(view, target, sems.pop(0))
            copy.start()
            fetched.append(copy)
        results_here = []
        for target, r in zip(targets[:results], is_far):
            if r:
                ref = held.pop(0)
                target = Leaving(pltpu.make_async_copy(ref, target, sems.pop(0)), ref)
                leaving.append(target)
            results_here.append(target)
        kernel(*scalars, *ins, *results_here, *refs)
        for ref in ins:
            if isinstance(ref, Arriving):
                ref[:1]
        for ref in leaving:
            ref.flush()
        for copy in fetched:
            copy.wait()
        for ref in leaving:
            ref.copy.wait()

    def space(r):
        return pl.BlockSpec(memory_space=pl.ANY if r else VMEM)

    return pl.pallas_call(
        run,
        in_specs=[pl.BlockSpec(memory_space=pltpu.SMEM)] * len(smem)
        + [space(r) for r in remote]
        + [space(True)] * len(fetch)
        + [pl.BlockSpec(memory_space=pl.ANY)] * len(after),
        out_specs=tuple(space(r) for r in is_far),
        out_shape=tuple((pltpu.HBM if r else VMEM)(s.shape, s.dtype) for s, r in zip(shapes, is_far)),
        scratch_shapes=buffers + sems + list(scratch),
        compiler_params=pltpu.CompilerParams(vmem_limit_bytes=limit),
        cost_estimate=pl.CostEstimate(flops=100000000, bytes_accessed=0, transcendentals=0),
    )(*smem, *arrays, *[p.array for p in fetch], *after)


def flush(*refs):
    for ref in refs:
        if isinstance(ref, Leaving):
            ref.flush()


def dot(a, b):
    return jnp.dot(a, b, preferred_element_type=F32)


def dot_nt(a, b):
    return lax.dot_general(a, b, (((1,), (1,)), ((), ())), preferred_element_type=F32)


def dot_tn(a, b):
    return lax.dot_general(a, b, (((0,), (0,)), ((), ())), preferred_element_type=F32)


def silu_and_slope(values):
    sigmoid = 0.5 * jnp.tanh(0.5 * values) + 0.5
    act = values * sigmoid
    return act, sigmoid + act * (1.0 - sigmoid)


def norm_parts(values):
    center = jnp.mean(values, axis=-1, keepdims=True)
    shifted = values - center
    inverse = lax.rsqrt(jnp.mean(shifted * shifted, axis=-1, keepdims=True) + EPS)
    return shifted * inverse, inverse


def norm_back(normed, inverse, upstream):
    return inverse * (
        upstream
        - jnp.mean(upstream, axis=-1, keepdims=True)
        - normed * jnp.mean(upstream * normed, axis=-1, keepdims=True)
    )


def halves(values):
    high = values.astype(BF16)
    low = (values - high.astype(F32)).astype(BF16)
    return jnp.concatenate([high, low], axis=0)


def node_of_edge(rows, nodes, slots):
    edge = lax.broadcasted_iota(jnp.int32, (rows, nodes), 0)
    node = lax.broadcasted_iota(jnp.int32, (rows, nodes), 1)
    return (edge // slots) == node


def pick_rows(send_ref, nodes):
    row = lax.broadcasted_iota(jnp.int32, (nodes, send_ref.shape[1]), 0)
    return (row == send_ref[...]).astype(F32).astype(BF16)


def pack_kernel(send_ref, h_ref, packed_ref):
    pick = pick_rows(send_ref, h_ref.shape[0])
    packed_ref[...] = dot_tn(pick, h_ref[...]).astype(BF16)


def prepare_kernel(
    table, chunk, nb_ref, count_ref, ocean_ref, h_ref, e_ref, we_ref, wr_ref,
    spread_ref, mask_ref, live_ref, wet_ref, pre_ref,
):
    slots, nodes = nb_ref.shape
    rows = nodes * slots
    owner = node_of_edge(rows, nodes, slots).astype(F32)
    owner16 = owner.astype(BF16)
    listed = dot_nt(owner16, nb_ref[...].astype(F32).astype(BF16))
    slot_here = lax.broadcasted_iota(jnp.int32, (rows, slots), 0) % slots
    slot_at = lax.broadcasted_iota(jnp.int32, (rows, slots), 1)
    source = jnp.sum(jnp.where(slot_here == slot_at, listed, 0.0), axis=1, keepdims=True)
    half = (table - nodes) // 2
    moved = jnp.where(source >= nodes + half, source - half, source + half)
    source = jnp.where(source >= nodes, moved, source)
    at = lax.broadcasted_iota(jnp.int32, (rows, table), 1).astype(F32)
    spread_ref[:, :table] = jnp.where(at == source, 1.0, 0.0).astype(BF16)
    spread_ref[:, table:] = owner16
    slot_of_row = lax.broadcasted_iota(jnp.int32, (rows, nodes), 0) % slots
    mask = jnp.where(slot_of_row < count_ref[...], owner, 0.0)
    mask_ref[...] = mask.astype(BF16)
    live_ref[...] = jnp.sum(mask, axis=1, keepdims=True)
    row = lax.broadcasted_iota(jnp.int32, (nodes, nodes), 0)
    column = lax.broadcasted_iota(jnp.int32, (nodes, nodes), 1)
    wet = jnp.where(row == column, ocean_ref[...].astype(F32), 0.0)
    wet_ref[...] = jnp.sum(wet, axis=1, keepdims=True)
    partial_kernel(chunk, h_ref, spread_ref, e_ref, we_ref, wr_ref, pre_ref)


def partial_kernel(chunk, h_ref, spread_ref, e_ref, we_ref, wr_ref, pre_ref):
    rows, width = e_ref.shape
    known = spread_ref.shape[1] - h_ref.shape[0]
    h = h_ref[...]
    for start in range(0, rows, chunk):
        at = pl.ds(start, chunk)
        own = dot(spread_ref[at, known:], h).astype(BF16)
        pre = dot(e_ref[at, :], we_ref[...])
        pre_ref[at, :] = pre + dot(own, wr_ref[...])


def forward_edges(chunk, pre_ref, e_ref, table, spread_ref, live_ref, ws_ref, wo_ref, put):
    rows, width = e_ref.shape
    known = table.shape[0]
    for start in range(0, rows, chunk):
        at = pl.ds(start, chunk)
        src = dot(spread_ref[at, :known], table).astype(BF16)
        pre = pre_ref[at, :] + dot(src, ws_ref[...])
        act, slope = silu_and_slope(pre)
        act = act.astype(BF16)
        normed, inverse = norm_parts(dot(act, wo_ref[...]))
        new_e = (e_ref[at, :].astype(F32) + live_ref[at, :] * normed).astype(BF16)
        put(at, act, slope, normed, inverse, new_e)


def forward_nodes(h, message, wi_ref, wo_ref):
    width = h.shape[1]
    pre = dot(h, wi_ref[:width, :]) + dot(message, wi_ref[width:, :])
    act, slope = silu_and_slope(pre)
    act = act.astype(BF16)
    normed, inverse = norm_parts(dot(act, wo_ref[...]))
    return act, slope, normed, inverse


def first_forward_kernel(
    chunk, pre_ref, e_ref, h_ref, halo_ref, spread_ref, mask_ref, live_ref, wet_ref, send_ref,
    ws_ref, weo_ref, wni_ref, wno_ref,
    act_ref, slope_ref, normed_ref, inverse_ref, new_e_ref,
    new_h_ref, message_ref, act_n_ref, slope_n_ref, normed_n_ref, inverse_n_ref, packed_ref,
):
    h = h_ref[...]
    table = jnp.concatenate([h, halo_ref[...]], axis=0)

    def put(at, act, slope, normed, inverse, new_e):
        act_ref[at, :] = act
        slope_ref[at, :] = slope.astype(BF16)
        normed_ref[at, :] = normed.astype(BF16)
        inverse_ref[at, :] = inverse
        new_e_ref[at, :] = new_e

    forward_edges(chunk, pre_ref, e_ref, table, spread_ref, live_ref, ws_ref, weo_ref, put)
    flush(act_ref, slope_ref, normed_ref, inverse_ref, new_e_ref)
    message = dot_tn(mask_ref[...], new_e_ref[...]).astype(BF16)
    act, slope, normed, inverse = forward_nodes(h, message, wni_ref, wno_ref)
    message_ref[...] = message
    act_n_ref[...] = act
    slope_n_ref[...] = slope.astype(BF16)
    normed_n_ref[...] = normed.astype(BF16)
    inverse_n_ref[...] = inverse
    flush(message_ref, act_n_ref, slope_n_ref, normed_n_ref, inverse_n_ref)
    new_h = (h.astype(F32) + wet_ref[...] * normed).astype(BF16)
    new_h_ref[...] = new_h
    packed_ref[...] = dot_tn(pick_rows(send_ref, h.shape[0]), new_h).astype(BF16)


def backward_nodes(gh, slope, normed, inverse, wet_ref, wi_ref, wo_ref, gout_ref, gpre_ref):
    gout = norm_back(normed, inverse, wet_ref[...] * gh).astype(BF16)
    gpre = (dot_nt(gout, wo_ref[...]) * slope).astype(BF16)
    gout_ref[...] = gout
    gpre_ref[...] = gpre
    ginput = dot_nt(gpre, wi_ref[...])
    width = gh.shape[1]
    return gh + ginput[:, :width], ginput[:, width:]


def backward_edges(
    chunk, known, gh, gmsg, ge_ref, spread_ref, live_ref, slope_ref, normed_ref, inverse_ref,
    we_ref, wr_ref, wo_ref, gh_out_ref, more_ref, own_ref, halo_out_ref, ge_out_ref, gedge_ref, gpe_ref, sums_ref,
):
    rows, width = ge_ref.shape
    nodes = gh.shape[0]
    gh_out_ref[...] = gh
    gmsg = halves(gmsg)
    for start in range(0, rows, chunk):
        at = pl.ds(start, chunk)
        live = live_ref[at, :]
        owner = spread_ref[at, known:]
        sent = dot(jnp.concatenate([owner, owner], axis=1), gmsg)
        ge = ge_ref[at, :].astype(F32) + live * sent
        gedge = norm_back(normed_ref[at, :].astype(F32), inverse_ref[at, :], live * ge)
        gedge = gedge.astype(BF16)
        gpe = (dot_nt(gedge, wo_ref[...]) * slope_ref[at, :].astype(F32)).astype(BF16)
        gedge_ref[at, :] = gedge
        gpe_ref[at, :] = gpe
        ge = ge + dot_nt(gpe, we_ref[...])
        ge_out_ref[at, :] = ge.astype(ge_out_ref.dtype)
    flush(gedge_ref, gpe_ref, ge_out_ref)
    gathered = dot_tn(spread_ref[...], gpe_ref[...])
    own_ref[...] = gathered[:nodes]
    halo_out_ref[...] = gathered[nodes:known].astype(BF16)
    sums_ref[...] = gathered.astype(BF16)
    both = dot_nt(halves(gathered[known:]), wr_ref[...])
    more_ref[...] = both[:nodes] + both[nodes:]


def middle_kernel(
    chunk, pre_ref, e_ref, h_ref, halo_ref, spread_ref, mask_ref, live_ref, wet_ref,
    gh_ref, ge_ref, ws_ref, weo_ref, wni_ref, wno_ref, we_ref, wr_ref,
    act_ref, message_ref, act_n_ref, gout_ref, gpre_ref,
    gh_out_ref, more_ref, own_ref, halo_out_ref, ge_out_ref, gedge_ref, gpe_ref, sums_ref,
    slope_ref, normed_ref, inverse_ref, new_e_ref,
):
    h = h_ref[...]
    table = jnp.concatenate([h, halo_ref[...]], axis=0)

    def put(at, act, slope, normed, inverse, new_e):
        act_ref[at, :] = act
        slope_ref[at, :] = slope.astype(BF16)
        normed_ref[at, :] = normed.astype(BF16)
        inverse_ref[at, :] = inverse
        new_e_ref[at, :] = new_e

    forward_edges(chunk, pre_ref, e_ref, table, spread_ref, live_ref, ws_ref, weo_ref, put)
    message = dot_tn(mask_ref[...], new_e_ref[...]).astype(BF16)
    act, slope, normed, inverse = forward_nodes(h, message, wni_ref, wno_ref)
    message_ref[...] = message
    act_n_ref[...] = act
    flush(act_ref)
    gh, gmsg = backward_nodes(
        gh_ref[...].astype(F32), slope, normed, inverse, wet_ref, wni_ref, wno_ref, gout_ref, gpre_ref
    )
    backward_edges(
        chunk, table.shape[0], gh, gmsg, ge_ref, spread_ref, live_ref, slope_ref, normed_ref,
        inverse_ref, we_ref, wr_ref, weo_ref, gh_out_ref, more_ref, own_ref, halo_out_ref, ge_out_ref,
        gedge_ref, gpe_ref, sums_ref,
    )


def return_halo(gh_ref, more_ref, own_ref, back_ref, send_ref, wei_ref):
    nodes, width = gh_ref.shape
    sent = send_ref.shape[1]
    first = 0 if back_ref.shape[0] == sent else nodes
    total = own_ref[...] + dot(pick_rows(send_ref, nodes), back_ref[first : first + sent, :])
    both = dot_nt(halves(total), wei_ref[...])
    return gh_ref[...] + more_ref[...] + both[:nodes] + both[nodes:]


def first_backward_kernel(
    chunk, gh_ref, more_ref, own_ref, back_ref, send_ref, slope_n_ref, normed_n_ref, inverse_n_ref, wet_ref,
    ge_ref, spread_ref, live_ref, slope_ref, normed_ref, inverse_ref,
    ws_ref, wno_ref, wni_ref, weo_ref, we_ref, wr_ref,
    gout_ref, gpre_ref, gh_out_ref, more_out_ref, own_out_ref, halo_out_ref, ge_out_ref,
    gedge_ref, gpe_ref, sums_ref,
):
    gh = return_halo(gh_ref, more_ref, own_ref, back_ref, send_ref, ws_ref)
    gh, gmsg = backward_nodes(
        gh, slope_n_ref[...].astype(F32), normed_n_ref[...].astype(F32), inverse_n_ref[...],
        wet_ref, wni_ref, wno_ref, gout_ref, gpre_ref,
    )
    known = spread_ref.shape[1] - gh.shape[0]
    backward_edges(
        chunk, known, gh, gmsg, ge_ref, spread_ref, live_ref, slope_ref, normed_ref,
        inverse_ref, we_ref, wr_ref, weo_ref, gh_out_ref, more_out_ref, own_out_ref, halo_out_ref, ge_out_ref,
        gedge_ref, gpe_ref, sums_ref,
    )


def last_kernel(gh_ref, more_ref, own_ref, back_ref, send_ref, wei_ref, out_ref):
    out_ref[...] = return_halo(gh_ref, more_ref, own_ref, back_ref, send_ref, wei_ref)


def place(order, me_ref, first_ref, second_ref, keep_ref, sent_ref):
    rows = keep_ref.shape[1]
    blocks = sorted({bits for bits, _ in order})
    sides = len(order) // len(blocks)
    for bits in blocks:
        spots = [order.index((bits, side)) for side in range(sides)]

        def spot(half):
            return jnp.where(me_ref[1] == half, spots[0], spots[1]) if sides == 2 else spots[0]

        for bit, out_ref in ((0, keep_ref), (1, sent_ref)):
            device = jnp.bitwise_xor(me_ref[0], bits + bit)
            row = 0
            for ref in (first_ref, second_ref):
                size = ref.shape[0] // (2 * len(blocks))
                start = pl.multiple_of(device * size, 16)
                done = 0
                while done < size:
                    half, at = divmod(row, rows)
                    step = min(size - done, rows - at)
                    piece = ref[pl.ds(pl.multiple_of(start + done, 16), step), :]
                    out_ref[spot(half), at : at + step, :] = piece.astype(BF16)
                    row += step
                    done += step
            if row < sides * rows:
                filler = jnp.zeros((sides * rows - row, keep_ref.shape[2]), BF16)
                out_ref[spot(sides - 1), row - (sides - 1) * rows :, :] = filler


def edge_weights_kernel(
    layout, me_ref, e_ref, h_ref, halo_ref, act_ref, gedge_ref, gpe_ref, sums_ref,
    keep_ref, sent_ref, grad_in_ref, grad_out_ref,
):
    width = e_ref.shape[1]
    h = h_ref[...]
    known = h.shape[0] + halo_ref.shape[0]
    table = jnp.concatenate([h, halo_ref[...]], axis=0)
    grad_in_ref[:width, :] = dot_tn(e_ref[...], gpe_ref[...])
    grad_in_ref[width : 2 * width, :] = dot_tn(table, sums_ref[:known, :])
    grad_in_ref[2 * width :, :] = dot_tn(h, sums_ref[known:, :])
    grad_out_ref[...] = dot_tn(act_ref[...], gedge_ref[...])
    place(layout, me_ref, grad_in_ref, grad_out_ref, keep_ref, sent_ref)


def node_weights_kernel(
    layout, me_ref, h_ref, message_ref, act_ref, gout_ref, gpre_ref,
    keep_ref, sent_ref, grad_in_ref, grad_out_ref,
):
    width = h_ref.shape[1]
    gpre = gpre_ref[...]
    grad_in_ref[:width, :] = dot_tn(h_ref[...], gpre)
    grad_in_ref[width:, :] = dot_tn(message_ref[...], gpre)
    grad_out_ref[...] = dot_tn(act_ref[...], gout_ref[...])
    place(layout, me_ref, grad_in_ref, grad_out_ref, keep_ref, sent_ref)


def trade(rows, back=False):
    count = lax.axis_size("mesh")
    if count == 2:
        return lax.ppermute(rows, "mesh", [(0, 1), (1, 0)])
    half = rows.shape[0] // 2
    up = [(i, (i + 1) % count) for i in range(count)]
    down = [(j, i) for i, j in up]
    first, second = (up, down) if back else (down, up)
    return jnp.concatenate(
        [lax.ppermute(rows[:half], "mesh", first), lax.ppermute(rows[half:], "mesh", second)], axis=0
    )


def flip(values, axis, bit):
    return lax.ppermute(values, axis, [(i, i ^ bit) for i in range(lax.axis_size(axis))])


def bits_of(axis):
    size = lax.axis_size(axis)
    return [1 << i for i in range(size.bit_length() - 1)]


def slot_order(route):
    order = [(0, 0)]
    for axis, bit in reversed(route):
        if axis == "dp":
            order = order + [(bits + bit, side) for bits, side in order]
        else:
            order = order + [(bits, 1) for bits, side in order]
    return order


class Sum:
    def __init__(self, keep, route):
        self.base, self.arrived, self.row = keep, None, 0
        self.slots, self.rows, self.width = keep.shape
        self.route = list(route)


def add_kernel(groups, tail, *refs):
    refs = list(refs)
    flat = [group for output in groups for group in output]
    terms, refs = refs[: 2 * len(flat)], refs[2 * len(flat) :]
    if tail:
        more, refs = refs[0], refs[1:]
    outs, kept = refs[: len(groups)], refs[len(groups) :]
    if tail:
        outs[-1][outs[-1].shape[0] - 1, : more.shape[0], :] = more[...]
    for output, out in zip(groups, outs):
        at = 0
        for rows, row, slots in output:
            base, arrived, terms = terms[0], terms[1], terms[2:]
            half = slots // 2
            low, high = (0, 1) if slots == 1 else (half, slots)
            total = base[low:high].astype(F32) + arrived[low:high, row : row + rows, :].astype(F32)
            out[: high - low, at : at + rows, :] = total.astype(BF16)
            at += rows
            if half:
                left, kept = kept[0], kept[1:]
                left[...] = base[:half].astype(F32) + arrived[:half, row : row + rows, :].astype(F32)


def add(wanted, after=(), tail=None):
    operands, groups, outs, kept = [], [], [], []
    for sums in wanted:
        group = []
        for one in sums:
            operands += [one.base, one.arrived]
            group.append((one.rows, one.row, one.slots))
            half = one.slots // 2
            if half:
                kept.append((one, ((half, one.rows, one.width), F32)))
        groups.append(group)
        outs.append(((max(half, 1), sum(one.rows for one in sums), one.width), BF16))
    if tail is not None:
        (count, size, width), dtype = outs[-1]
        outs[-1] = ((count + 1, size, width), dtype)
        operands.append(tail)
    results = call(
        functools.partial(add_kernel, groups, tail is not None),
        operands,
        outs + [shape for _, shape in kept],
        after=after,
    )
    for (one, _), base in zip(kept, results[len(outs) :]):
        one.base = base
        one.slots //= 2
    return results[: len(outs)]


def advance(wanted, after=(), tail=None):
    sent = add(wanted, after, tail)
    arrived = []
    for sums, values in zip(wanted, sent):
        steps = [one.route.pop(0) for one in sums if one.route]
        if not steps:
            arrived.append(None)
            continue
        other = flip(values, *steps[0])
        row = 0
        for one in sums:
            one.arrived, one.row = other, row
            row += one.rows
        arrived.append(other)
    return sent, arrived


def across(values):
    mine = values[0]
    for bit in bits_of("mesh")[1:]:
        mine = (mine.astype(F32) + flip(mine, "mesh", bit).astype(F32)).astype(BF16)
    return mine, flip(mine, "mesh", 1)


def output_kernel(
    factor, halves_of, me_ref, mine0_ref, other0_ref, mine1_ref, other1_ref, *outs
):
    low = me_ref[1] == 0
    row0 = row1 = 0
    for pair, rows in enumerate(halves_of):
        first, second = outs[2 * pair], outs[2 * pair + 1]
        cut, end = first.shape[1], first.shape[1] + second.shape[1]
        a = mine0_ref[row0 : row0 + rows, :].astype(F32) * factor
        b = other0_ref[row0 : row0 + rows, :].astype(F32) * factor
        both = jnp.concatenate([jnp.where(low, a, b), jnp.where(low, b, a)], axis=0)
        first[0] = both[:cut]
        second[0] = both[cut:end]
        a = mine1_ref[row1 : row1 + end, :].astype(F32)
        both = (a + other1_ref[row1 : row1 + end, :].astype(F32)) * factor
        first[1] = both[:cut]
        second[1] = both[cut:end]
        flush(first, second)
        row0 += rows
        row1 += end


def body(
    node_feats,
    edge_feats,
    node_cot,
    edge_cot,
    w_edge_in,
    w_edge_out,
    w_node_in,
    w_node_out,
    neighbours,
    send_rows,
    edge_counts,
    ocean_mask,
):
    samples, nodes, width = node_feats.shape
    slots = neighbours.shape[1]
    rows = nodes * slots
    sent = send_rows.shape[1]
    known = nodes + sent
    chunk = rows
    shards = lax.axis_size("dp")
    total_rows = samples * shards * nodes * lax.axis_size("mesh")
    factor = 1.0 / total_rows**0.5
    beyond = [("dp", bit) for bit in bits_of("dp")[2:]]
    along = [("dp", 2)]
    edge_routes = (along + [("mesh", 1)] + beyond, along + beyond)
    node_routes = ([("mesh", 1)] + along + beyond, beyond + along)
    me = jnp.stack([lax.axis_index("dp"), lax.axis_index("mesh") % 2]).astype(jnp.int32)

    h0 = node_feats.reshape(nodes, width)
    e0 = edge_feats.reshape(rows, width)
    gh = node_cot.reshape(nodes, width)
    ge = edge_cot.reshape(rows, width)
    weights = (w_edge_in, w_edge_out, w_node_in, w_node_out)
    small, large, thin = (nodes, width), (rows, width), (sent, width)
    source = [rows_of(w_edge_in, layer, width, 2 * width) for layer in range(2)]
    edge = [rows_of(w_edge_in, layer, 0, width) for layer in range(2)]
    receiver = [rows_of(w_edge_in, layer, 2 * width) for layer in range(2)]
    edge_out = [rows_of(w_edge_out, layer) for layer in range(2)]
    node_in = [rows_of(w_node_in, layer) for layer in range(2)]
    node_out = [rows_of(w_node_out, layer) for layer in range(2)]

    (packed0,) = call(pack_kernel, (Part(send_rows), Part(h0)), [(thin, BF16)])
    halo0 = trade(packed0)
    spread, mask, live, wet, pre0, h0_near, e0_near, source0, edge_out0, node_in0, node_out0 = call(
        functools.partial(prepare_kernel, known, chunk),
        (Part(neighbours.T), Part(edge_counts.reshape(1, nodes)), Part(ocean_mask.reshape(1, nodes)))
        + (Part(h0), Part(e0), edge[0], receiver[0]),
        [
            ((rows, known + nodes), BF16), ((rows, nodes), BF16), ((rows, 1), F32),
            ((nodes, 1), F32), (large, F32),
        ],
        fetch=(Part(h0), Part(e0), source[0], edge_out[0], node_in[0], node_out[0]),
    )
    (
        act0, slope0, normed0, inverse0, e1,
        h1, message0, act_n0, slope_n0, normed_n0, inverse_n0, packed1,
        edge1_w, receiver1_w, source1_w,
    ) = call(
        functools.partial(first_forward_kernel, chunk),
        (pre0, e0_near, h0_near, halo0, spread, mask, live, wet, send_rows)
        + (source0, edge_out0, node_in0, node_out0),
        [(large, BF16)] * 3 + [((rows, 1), F32), (large, BF16), (small, BF16)]
        + [(small, BF16)] * 4 + [((nodes, 1), F32), (thin, BF16)],
        fetch=(edge[1], receiver[1], source[1]),
    )
    halo1 = trade(packed1)
    pre1, edge_out1, node_in1, node_out1, gh_near, ge_near = call(
        functools.partial(partial_kernel, chunk),
        (h1, spread, e1, edge1_w, receiver1_w),
        [(large, F32)],
        fetch=(edge_out[1], node_in[1], node_out[1], Part(gh), Part(ge)),
    )
    backward_outs = [(small, F32)] * 3 + [(thin, BF16)]
    backward_tail = [(large, BF16)] * 2 + [((known + nodes, width), BF16)]
    act1, message1, act_n1, gout1, gpre1, gh, more, own, halo_out, ge, gedge1, gpe1, sums1, *near_w = call(
        functools.partial(middle_kernel, chunk),
        (pre1, e1, h1, halo1, spread, mask, live, wet, gh_near, ge_near)
        + (source1_w, edge_out1, node_in1, node_out1, edge1_w, receiver1_w),
        [(large, BF16)] + [(small, BF16)] * 4 + backward_outs + [(large, F32)] + backward_tail,
        scratch=[VMEM(large, BF16)] * 2 + [VMEM((rows, 1), F32), VMEM(large, BF16)],
        fetch=(node_out[0], node_in[0], edge_out[0], edge[0], receiver[0]),
    )
    back = trade(halo_out if lax.axis_size("mesh") > 2 else sums1, back=True)

    def weight_sum(kernel, route, operands, kinds, **more):
        order = slot_order(route)
        size = sum(w.shape[1] // shards for w in kinds)
        rows_in = size if ("mesh", 1) not in route else -(-size // 32) * 16
        shape = (len(order), rows_in, width)
        keep, send, *fetched = call(
            functools.partial(kernel, order),
            operands,
            [(shape, BF16)] * 2,
            scratch=[VMEM(w.shape[1:], F32) for w in kinds],
            smem=(me,),
            **more,
        )
        one = Sum(keep, route)
        one.arrived = flip(send, "dp", 1)
        return one, fetched

    def edge_sum(layer, operands, **more):
        return weight_sum(
            edge_weights_kernel, edge_routes[layer], operands, (w_edge_in, w_edge_out), **more
        )

    def node_sum(layer, operands, **more):
        return weight_sum(
            node_weights_kernel, node_routes[layer], operands, (w_node_in, w_node_out), **more
        )

    edge1, _ = edge_sum(1, (e1, h1, halo1, act1, gedge1, gpe1, sums1))
    node1, _ = node_sum(1, (h1, message1, act_n1, gout1, gpre1))
    _, arrived = advance([[edge1]])
    first, arrived_n = advance([[node1]])
    arrived += arrived_n
    gout0, gpre0, gh, more, own, halo_out, ge, gedge0, gpe0, sums0, e0_near, h0_near = call(
        functools.partial(first_backward_kernel, chunk),
        (gh, more, own, back, send_rows, slope_n0, normed_n0, inverse_n0, wet)
        + (ge, spread, live, slope0, normed0, inverse0, source1_w, *near_w),
        [(small, BF16)] * 2 + backward_outs + [far(large, BF16)] + backward_tail,
        after=tuple(first),
        fetch=(Part(e0), Part(h0)),
    )
    edge0, _ = edge_sum(0, (e0_near, h0_near, halo0, act0, gedge0, gpe0, sums0))
    node0, _ = node_sum(
        0, (h0_near, message0, act_n0, gout0, gpre0), after=tuple(arrived)
    )
    joint = lax.axis_size("mesh") == 2 and sent <= node0.rows
    wanted = [[edge0], [edge1], [node1], [node0]]
    out, _ = advance([[edge0], [edge1]])
    _, arrived = advance([[node1], [node0]], after=(out[0],), tail=halo_out if joint else None)
    if joint:
        back = Part(arrived[-1], (arrived[-1].shape[0] - 1, pl.ds(0, sent)), thin, pin=False)
    else:
        back = trade(halo_out, back=True)
    out, _ = advance(wanted)
    (gh,) = call(
        last_kernel, (gh, more, own, back, send_rows, source[0]), [far(small, F32)], after=(out[0],)
    )
    done = (in_hbm(gh),)
    while edge1.route:
        advance([[edge0, node0], [edge1], [node1]], after=done)
        done = ()
    (_, value1), _ = advance([[edge0, node0], [edge1, node1]], after=done)
    mine1, other1 = across(value1)
    while edge0.route:
        advance([[edge0, node0]])
    ((value0,), _) = advance([[edge0, node0]], after=(other1,))
    mine0, other0 = across(value0)
    grads = call(
        functools.partial(output_kernel, factor, (edge0.rows, node0.rows)),
        (mine0, other0, mine1, other1),
        [far((2, w.shape[1] // shards, width), F32) for w in weights],
        smem=(me,),
    )
    return (
        gh.reshape(samples, nodes, width),
        ge.reshape(samples, nodes, slots, width),
        *grads,
    )


def solution(mesh):
    placed = (
        P("dp", "mesh", None),
        P("dp", "mesh", None, None),
        P("dp", "mesh", None),
        P("dp", "mesh", None, None),
        P(),
        P(),
        P(),
        P(),
        P("mesh", None),
        P("mesh", None),
        P("mesh"),
        P("mesh"),
    )
    return jax.shard_map(
        body,
        mesh=mesh,
        in_specs=placed,
        out_specs=(
            P("dp", "mesh", None),
            P("dp", "mesh", None, None),
            P(None, "dp", None),
            P(None, "dp", None),
            P(None, "dp", None),
            P(None, "dp", None),
        ),
        check_vma=False,
    )
```
